32 devices in a mesh: grp: 2 (over x), fa: 16 (over z, y, core).
Axes of the slice: x: 2, y: 2, z: 4, core: 2. Of those that a mesh axis runs over, the one named last changes fastest.
Arguments:
- hidden_f: bfloat16 [4096, 1024], P(('grp', 'fa')), parts along dimension 0, may hold values from -6 to 6
- hidden_t: bfloat16 [4096, 1024], P(('grp', 'fa')), parts along dimension 0, may hold values from -6 to 6
- hidden_b: bfloat16 [4096, 256], P(('grp', 'fa')), parts along dimension 0, may hold values from -6 to 6
- w_f: bfloat16 [1024, 256], replicated, may hold values from -0.1875 to 0.1875
- w_t: bfloat16 [1024, 256], replicated, may hold values from -0.1875 to 0.1875
- w_b: bfloat16 [256, 256], replicated, may hold values from -0.375 to 0.375
- latents: bfloat16 [1024, 256], P('grp'), parts along dimension 0, may hold values from -5 to 5
- latent_ids: int32 [4096], P(('grp', 'fa')), parts along dimension 0, may hold values from 0 to 511
- positives: int32 [4096], P(('grp', 'fa')), parts along dimension 0, may hold values from 0 to 2047, each once
Outputs:
- grad_wf: float32 [2048, 256], P('grp'), parts along dimension 0
- grad_wb: float32 [512, 256], P('grp'), parts along dimension 0
- loss: float32 [2], P('grp'), parts along dimension 0
The draws below stay inside these ranges and needn't reach their ends.
There are 2 independent parts, one for each index of `grp`. The reference program is written for one: setup_inputs(seed, part) draws one part's arguments, and reference() takes and returns one part's arrays. A program takes and returns all parts, laid end to end along the dimension named above; an argument that names none is the same for every part. Nothing has to cross between parts.
Inputs may be any that keep to these rules, and one draw needn't show every extreme that they name: `positives`: each row index of 0 to 2047 appears exactly once.
All inputs are finite; a program needn't handle non-finite values.
Results may differ from the reference program's by a relative error of at most 0.0039.
Values may be sent and summed in bfloat16 or wider, within the bound.
No kernel may reach another device: no remote copies, remote signals or barrier semaphores. Data moves between devices by JAX's collectives and lax.ppermute only.
A program may use at most 128 MiB of HBM per device.

```python
import math
import jax
import jax.numpy as jnp
from jax import lax

DIM = 256
H = 1024
HB = 256
LAT = 512
TOKENS = 2048


def with_ends(array, stream_key, least, high):
    index_at = [jax.random.randint(jax.random.fold_in(stream_key, axis), (), 0, length) for axis, length in enumerate(array.shape)]
    widest = array.shape.index(max(array.shape))
    neighbour = index_at[:widest] + [(index_at[widest] + 1) % array.shape[widest]] + index_at[widest + 1:]
    return array.at[tuple(index_at)].set(least).at[tuple(neighbour)].set(high)


def block_scale(own_key, extent, pieces, low, top_value):
    loudness = 1.0
    for dim, blocks in pieces:
        heights = jax.random.uniform(jax.random.fold_in(jax.random.fold_in(own_key, 6), dim), (blocks,), jnp.float32, low / len(pieces), top_value / len(pieces))
        loudness = loudness * jnp.repeat(jnp.exp(heights), extent[dim] // blocks).reshape((-1,) + (1,) * (len(extent) - 1 - dim))
    return loudness


def scatter_about(rng, shape, deviation, limit, cuts=(), held_as=jnp.bfloat16):
    factor_of = block_scale(rng, shape, cuts, -0.22, 0.18) if cuts else 1.0
    values = jax.random.normal(rng, shape, jnp.float32) * deviation * factor_of
    return jnp.minimum(jnp.maximum(values, -limit), limit).astype(held_as)


def setup_inputs(seed: int = 0, part: int = 0) -> dict:
    seeds = jax.random.split(jax.random.key(seed), 10)
    own_keys = jax.random.split(jax.random.fold_in(seeds[9], part), 10)
    return {
        "hidden_f": scatter_about(own_keys[0], (TOKENS, H), 1.0, 6.0, ((0, 16),)),
        "hidden_t": scatter_about(own_keys[1], (TOKENS, H), 1.0, 6.0, ((0, 16),)),
        "hidden_b": scatter_about(own_keys[2], (TOKENS, HB), 1.0, 6.0, ((0, 16),)),
        "w_f": scatter_about(seeds[3], (H, DIM), H ** -0.5, 0.1875),
        "w_t": scatter_about(seeds[4], (H, DIM), H ** -0.5, 0.1875),
        "w_b": scatter_about(seeds[5], (HB, DIM), HB ** -0.5, 0.375),
        "latents": scatter_about(own_keys[6], (LAT, DIM), 1.0, 5.0),
        "latent_ids": with_ends(jax.random.randint(own_keys[7], (TOKENS,), 0, LAT), jax.random.fold_in(own_keys[7], 1), 0, LAT - 1).astype(jnp.int32),
        "positives": jax.random.permutation(own_keys[8], TOKENS).astype(jnp.int32),
    }


GAMMA = 0.98
LAMBDA = 1.0
EPS = 1e-06

def reference(hidden_f, hidden_t, hidden_b, w_f, w_t, w_b, latents, latent_ids, positives):
    onehot = (latent_ids[:, None] == jnp.arange(LAT, dtype=jnp.int32)[None, :]).astype(latents.dtype)
    zrows = jnp.dot(onehot, latents, preferred_element_type=jnp.float32)
    feat = (jnp.dot(hidden_f, w_f, preferred_element_type=jnp.float32) + zrows).astype(jnp.bfloat16)
    feat_t = (jnp.dot(hidden_t, w_t, preferred_element_type=jnp.float32) + zrows).astype(jnp.bfloat16)
    raw = jnp.dot(hidden_b, w_b, preferred_element_type=jnp.float32)
    scale_r = lax.rsqrt(lax.optimization_barrier(jnp.mean(raw * raw, axis=-1, keepdims=True)) + EPS)
    back = (raw * scale_r).astype(jnp.bfloat16)
    pairs = float(TOKENS * (TOKENS - 1))
    block = math.gcd(TOKENS, 512)
    columns = jnp.arange(TOKENS, dtype=jnp.int32)

    def step(carry, index):
        start = (index * block).astype(jnp.int32)
        rows_f = lax.dynamic_slice_in_dim(feat, start, block, 0)
        rows_t = lax.dynamic_slice_in_dim(feat_t, start, block, 0)
        rows_b = lax.dynamic_slice_in_dim(back, start, block, 0)
        rows_p = lax.dynamic_slice_in_dim(positives, start, block, 0)
        score = jnp.dot(rows_f, back.T, preferred_element_type=jnp.float32)
        score_t = jnp.dot(rows_t, back.T, preferred_element_type=jnp.float32)
        match = rows_p[:, None] == columns[None, :]
        offdiag = jnp.where(match, 0.0, score - GAMMA * score_t)
        weights = (offdiag / pairs - jnp.where(match, 1.0 / TOKENS, 0.0)).astype(jnp.bfloat16)
        cov = jnp.dot(rows_b, back.T, preferred_element_type=jnp.float32)
        same = (start + jnp.arange(block, dtype=jnp.int32))[:, None] == columns[None, :]
        cov_off = jnp.where(same, 0.0, cov)
        cov_w = (cov_off * (2.0 * LAMBDA / pairs)).astype(jnp.bfloat16)
        part = jnp.sum(offdiag * offdiag) / (2.0 * pairs) - jnp.sum(jnp.where(match, score, 0.0)) / TOKENS
        part = part + LAMBDA * (jnp.sum(cov_off * cov_off) / (2.0 * pairs) - jnp.sum(jnp.where(same, cov, 0.0)) / TOKENS)
        grad_rows = jnp.dot(weights, back, preferred_element_type=jnp.float32)
        ortho_rows = jnp.dot(cov_w, back, preferred_element_type=jnp.float32)
        carry = carry + jnp.dot(weights.T, rows_f, preferred_element_type=jnp.float32)
        return (carry, (grad_rows, ortho_rows, part))
    init = jnp.zeros((TOKENS, DIM), jnp.float32)
    cross, (grad_f, ortho, parts) = lax.scan(step, init, jnp.arange(TOKENS // block, dtype=jnp.int32))
    grad_f = grad_f.reshape(TOKENS, DIM)
    ortho = ortho.reshape(TOKENS, DIM)
    grad_b = cross + ortho - 2.0 * LAMBDA / TOKENS * back.astype(jnp.float32)
    grad_u = scale_r * grad_b - scale_r ** 3 / DIM * lax.optimization_barrier(jnp.sum(grad_b * raw, axis=-1, keepdims=True)) * raw
    grad_wf = jnp.dot(hidden_f.T, grad_f.astype(jnp.bfloat16), preferred_element_type=jnp.float32) * math.sqrt(H)
    grad_wb = jnp.dot(hidden_b.T, grad_u.astype(jnp.bfloat16), preferred_element_type=jnp.float32) * math.sqrt(HB)
    loss = (jnp.sum(parts) / DIM).reshape(1)
    return (grad_wf, grad_wb, loss)
```

```python
import functools
import math

import jax
import jax.numpy as jnp
from jax import lax
from jax.experimental import pallas as pl
from jax.experimental.pallas import tpu as pltpu
from jax.sharding import PartitionSpec as P

GAMMA = 0.98
LAMBDA = 1.0
EPS = 1e-06
BF = jnp.bfloat16
F32 = jnp.float32


def dot(left, right):
    return jnp.dot(left, right, preferred_element_type=F32)


def dot_t(left, right):
    return lax.dot_general(left, right, (((0,), (0,)), ((), ())), preferred_element_type=F32)


def halves(array):
    high = array.astype(BF)
    return high, (array - high.astype(F32)).astype(BF)


def swap(array, mask, size):
    return lax.ppermute(array, "fa", [(i, i ^ mask) for i in range(size)])


def masks_of(size):
    return [1 << k for k in range(size.bit_length() - 1)]


def reverse_bits(value, bits):
    out = value * 0
    for k in range(bits):
        out = out + (((value >> k) & 1) << (bits - 1 - k))
    return out


def gather_swapped(array, size):
    for mask in reversed(masks_of(size)):
        array = jnp.concatenate([array, swap(array, mask, size)], axis=0)
    return array


def assemble_kernel(place_ref, blocks_ref, wf_ref, wb_ref, *, count, wf_rows, wb_rows, factor_f, factor_b):
    place = place_ref[0]
    for e in range(count):
        at = place ^ e
        wf_ref[pl.ds(pl.multiple_of(at * wf_rows, wf_rows), wf_rows), :] = (
            blocks_ref[e, :wf_rows, :].astype(F32) * factor_f
        )
        wb_ref[pl.ds(pl.multiple_of(at * wb_rows, wb_rows), wb_rows), :] = (
            blocks_ref[e, wf_rows:, :].astype(F32) * factor_b
        )


def body(hidden_f, hidden_t, hidden_b, w_f, w_t, w_b, latents, latent_ids, positives):
    rows = hidden_f.shape[0]
    width = w_f.shape[1]
    size = lax.axis_size("fa")
    bits = size.bit_length() - 1
    me = lax.axis_index("fa")
    total = size * rows
    pairs = float(total * (total - 1))
    every_hb = gather_swapped(hidden_b, size)

    onehot = (latent_ids[:, None] == jnp.arange(latents.shape[0], dtype=jnp.int32)[None, :]).astype(BF)
    zrows = dot(onehot, latents)
    feat = (dot(hidden_f, w_f) + zrows).astype(BF)
    feat_t = (dot(hidden_t, w_t) + zrows).astype(BF)
    diff = feat.astype(F32) - GAMMA * feat_t.astype(F32)
    diff_hi, diff_lo = halves(diff)
    kmat = dot_t(diff_hi, feat) + dot_t(diff_lo, feat)

    blocks = me ^ reverse_bits(jnp.arange(size, dtype=jnp.int32), bits)
    col_ids = (blocks[:, None] * rows + jnp.arange(rows, dtype=jnp.int32)[None, :]).reshape(-1)
    pick = (positives[:, None] == col_ids[None, :]).astype(BF)

    def embed(hidden):
        raw = dot(hidden, w_b)
        scale = lax.rsqrt(jnp.mean(raw * raw, axis=-1, keepdims=True) + EPS)
        return raw, scale, (raw * scale).astype(BF)

    def through(grad, raw, scale):
        return (
            scale * grad - scale**3 / width * jnp.sum(grad * raw, axis=-1, keepdims=True) * raw
        ).astype(BF)

    raw, scale, back = embed(every_hb)
    smat = dot_t(back, back)
    s_hi, s_lo = halves(smat)
    own_hb = dot(pick, every_hb).astype(BF)
    own_raw, own_scale, own_back = embed(own_hb)
    ob = own_back.astype(F32)
    ds = dot(diff_hi, s_hi) + dot(diff_lo, s_hi) + dot(diff_hi, s_lo)
    db = jnp.sum(diff * ob, axis=-1, keepdims=True)
    coef = db / pairs + 1.0 / total
    grad_f = (ds / pairs - coef * ob).astype(BF)
    local_wf = dot_t(hidden_f, grad_f)
    norm = jnp.sum(ob * ob, axis=-1, keepdims=True)
    f32feat = feat.astype(F32)
    part = (
        (jnp.sum(diff * ds) - jnp.sum(db * db)) / (2.0 * pairs)
        - jnp.sum(f32feat * ob) / total
        + LAMBDA
        * ((jnp.sum(smat * smat) / size - jnp.sum(norm * norm)) / (2.0 * pairs) - jnp.sum(norm) / total)
    )
    amat = (kmat + (2.0 * LAMBDA / size) * smat) / pairs
    a_hi, a_lo = halves(amat)
    grad_all = through(dot(back, a_hi) + dot(back, a_lo), raw, scale)
    grad_own = through(
        -coef * f32feat - (2.0 * LAMBDA / pairs * norm + 2.0 * LAMBDA / total) * ob, own_raw, own_scale
    )
    local_wb = dot_t(every_hb, grad_all) + dot_t(own_hb, grad_own)

    wf_rows = local_wf.shape[0] // 16
    wb_rows = local_wb.shape[0] // 16
    each = wf_rows + wb_rows
    current = jnp.concatenate(
        [local_wf.reshape(16, wf_rows, width), local_wb.reshape(16, wb_rows, width)], axis=1
    )
    note = jnp.full((1, 8, width), part, F32)
    split = min(4, bits)
    for k, mask in enumerate(masks_of(size)):
        if k < split:
            count = current.shape[0] // 2
            mine = (me >> k) & 1
            keep = lax.dynamic_slice_in_dim(current, mine * count, count, 0)
            send = lax.dynamic_slice_in_dim(current, (1 - mine) * count, count, 0)
        else:
            count = current.shape[0]
            keep = send = current
        sent = jnp.concatenate([send.reshape(1, count * each, width), note], axis=1)
        got = swap(sent, mask, size)
        current = keep + got[:, : count * each].reshape(count, each, width)
        note = note + got[:, count * each :]
    result = current.astype(BF)
    for mask in reversed(masks_of(size)[:split]):
        result = jnp.concatenate([result, swap(result, mask, size)], axis=0)
    place = reverse_bits(me & ((1 << split) - 1), split).astype(jnp.int32).reshape(1)
    count = result.shape[0]
    grad_wf, grad_wb = pl.pallas_call(
        functools.partial(
            assemble_kernel,
            count=count,
            wf_rows=wf_rows * (16 // count),
            wb_rows=wb_rows * (16 // count),
            factor_f=math.sqrt(hidden_f.shape[1]),
            factor_b=math.sqrt(hidden_b.shape[1]),
        ),
        in_specs=[
            pl.BlockSpec(memory_space=pltpu.SMEM),
            pl.BlockSpec(memory_space=pltpu.VMEM),
        ],
        out_specs=[pl.BlockSpec(memory_space=pltpu.VMEM)] * 2,
        out_shape=[
            jax.ShapeDtypeStruct(local_wf.shape, F32),
            jax.ShapeDtypeStruct(local_wb.shape, F32),
        ],
        compiler_params=pltpu.CompilerParams(vmem_limit_bytes=16 * 2**20),
    )(place, result)
    return (grad_wf, grad_wb, (note[0, 0, :1] / width))


def solution(mesh):
    placed = (
        P(("grp", "fa"), None),
        P(("grp", "fa"), None),
        P(("grp", "fa"), None),
        P(),
        P(),
        P(),
        P("grp", None),
        P(("grp", "fa")),
        P(("grp", "fa")),
    )
    return jax.shard_map(
        body,
        mesh=mesh,
        in_specs=placed,
        out_specs=(P("grp", None), P("grp", None), P("grp")),
        check_vma=False,
    )
```

```python
import functools
import math

import jax
import jax.numpy as jnp
from jax import lax
from jax.experimental import pallas as pl
from jax.experimental.pallas import tpu as pltpu
from jax.sharding import PartitionSpec as P

GAMMA = 0.98
LAMBDA = 1.0
EPS = 1e-06
BF = jnp.bfloat16
F32 = jnp.float32
GROUP = (0, 2, 1, 3)
PAD = 16


def dot(left, right):
    return jnp.dot(left, right, preferred_element_type=F32)


def dot_t(left, right):
    return lax.dot_general(left, right, (((0,), (0,)), ((), ())), preferred_element_type=F32)


def halves(array):
    high = array.astype(BF)
    return high, (array - high.astype(F32)).astype(BF)


def swap(array, mask, size):
    return lax.ppermute(array, "fa", [(i, i ^ mask) for i in range(size)])


def reverse_bits(value, bits):
    out = value * 0
    for k in range(bits):
        out = out + (((value >> k) & 1) << (bits - 1 - k))
    return out


def columns_of(row, rows):
    return jnp.transpose(jnp.broadcast_to(row, (rows, rows)))


def feature_kernel(
    quarter_ref, hf_ref, ht_ref, wf_ref, wt_ref, lat_ref, ids_ref, pos_ref, far_ref, near_ref, own_ref
):
    rows = hf_ref.shape[0]
    width = wf_ref.shape[1]
    cut = hf_ref.shape[1] // 4
    ids = columns_of(ids_ref[...].astype(F32), rows)
    lanes = lax.broadcasted_iota(jnp.int32, (rows, rows), 1).astype(F32)
    zrows = jnp.zeros((rows, width), F32)
    tiles = [
        jnp.where(ids == lanes + float(t * rows), 1.0, 0.0).astype(BF)
        for t in range(lat_ref.shape[0] // rows)
    ]
    zrows = dot(jnp.concatenate(tiles, axis=1), lat_ref[...])
    feat = (dot(hf_ref[...], wf_ref[...]) + zrows).astype(BF)
    feat_t = (dot(ht_ref[...], wt_ref[...]) + zrows).astype(BF)
    pos = pos_ref[...]
    line = lax.broadcasted_iota(jnp.int32, (PAD, rows), 0)
    high = jnp.broadcast_to(lax.shift_right_logical(pos, 7).astype(F32), (PAD, rows))
    low = jnp.broadcast_to((pos & 127).astype(F32), (PAD, rows))
    coded = jnp.where(line == 0, high, jnp.where(line == 1, low, 0.0)).astype(BF)
    for ref, start in ((far_ref, rows), (near_ref, 0)):
        ref[start : start + rows, :] = feat
        ref[start + rows : start + 2 * rows, :] = feat_t
        ref[start + 2 * rows : start + 2 * rows + PAD, :] = jnp.zeros((PAD, width), BF)
        ref[start + 2 * rows : start + 2 * rows + PAD, :rows] = coded

    def piece(slot):
        return hf_ref[:, pl.ds(pl.multiple_of(quarter_ref[slot] * cut, cut), cut)]

    end = 2 * rows + PAD
    own_ref[...] = piece(0)
    far_ref[:rows, :] = piece(1)
    near_ref[end : end + rows, :] = piece(2)
    far_ref[rows + end : 2 * rows + end, :] = piece(3)


def pair_kernel(
    base_ref,
    place_ref,
    hb0_ref,
    hb2_ref,
    hb1_ref,
    hb3_ref,
    own_ref,
    ff0_ref,
    ff2_ref,
    ff1_ref,
    ff3_ref,
    wb_ref,
    keep_ref,
    send_ref,
    raw_ref,
    back_ref,
    smat_ref,
    pick_ref,
    wfq_ref,
    wbq_ref,
    *,
    rows,
    total,
    chunk,
):
    width = wb_ref.shape[1]
    pairs = float(total * (total - 1))
    groups = total // (4 * rows)
    hb_refs = (hb0_ref, hb2_ref, hb1_ref, hb3_ref)
    each = hb0_ref.shape[0]
    steps = each // chunk
    tiles = chunk // rows
    wb = wb_ref[...]
    end = 2 * rows + PAD
    parts = ((ff0_ref, 0), (ff2_ref, rows), (ff1_ref, 0), (ff3_ref, rows))
    wanted = []
    for ref, start in parts:
        code = ref[start + 2 * rows : start + end, :rows].astype(F32)
        wanted.append(columns_of(code[0:1] * 128.0 + code[1:2], rows))
    lanes = lax.broadcasted_iota(jnp.int32, (rows, rows), 1)

    def embed(hidden):
        raw = dot(hidden, wb)
        scale = lax.rsqrt(jnp.mean(raw * raw, axis=-1, keepdims=True) + EPS)
        return raw, scale, (raw * scale).astype(BF)

    def through(grad, raw, scale):
        along = jnp.sum(grad * raw, axis=-1, keepdims=True)
        return (scale * grad - scale * scale * scale * (1.0 / width) * along * raw).astype(BF)

    def over_rows(step):
        for number, ref in enumerate(hb_refs):
            if steps == 1:
                step(number, ref, 0)
            else:
                lax.fori_loop(0, steps, lambda i, c: (step(number, ref, i), c)[1], 0)

    def at(number, index):
        return pl.ds(pl.multiple_of(number * each + index * chunk, chunk), chunk)

    smat_ref[...] = jnp.zeros_like(smat_ref)
    pick_ref[...] = jnp.zeros_like(pick_ref)
    wbq_ref[...] = jnp.zeros_like(wbq_ref)

    def first(number, ref, index):
        hidden = ref[pl.ds(pl.multiple_of(index * chunk, chunk), chunk), :]
        raw, _, back = embed(hidden)
        raw_ref[at(number, index), :] = raw
        back_ref[at(number, index), :] = back
        smat_ref[...] += dot_t(back, back)
        ids = [
            (lanes + base_ref[(number * steps + index) * tiles + t]).astype(F32) for t in range(tiles)
        ]
        mask = jnp.concatenate(
            [
                jnp.concatenate([jnp.where(want == i, 1.0, 0.0).astype(BF) for i in ids], axis=1)
                for want in wanted
            ],
            axis=0,
        )
        pick_ref[...] += dot(mask, hidden)

    over_rows(first)
    smat = smat_ref[...]
    s_hi, s_lo = halves(smat)
    kmat = jnp.zeros((width, width), F32)
    wfq = jnp.zeros((own_ref.shape[1], width), F32)
    sums = jnp.sum(smat * smat) / groups / (2.0 * pairs)
    cuts = (own_ref, (ff2_ref, 0), (ff1_ref, end), (ff3_ref, rows + end))
    for g, (ref, start) in enumerate(parts):
        feat = ref[start : start + rows, :]
        f32feat = feat.astype(F32)
        diff = f32feat - GAMMA * ref[start + rows : start + 2 * rows, :].astype(F32)
        d_hi, d_lo = halves(diff)
        hidden = pick_ref[g * rows : (g + 1) * rows, :].astype(BF)
        raw, scale, back = embed(hidden)
        ob = back.astype(F32)
        ds = dot(d_hi, s_hi) + dot(d_lo, s_hi) + dot(d_hi, s_lo)
        db = jnp.sum(diff * ob, axis=-1, keepdims=True)
        coef = db * (1.0 / pairs) + 1.0 / total
        norm = jnp.sum(ob * ob, axis=-1, keepdims=True)
        grad_f = (ds * (1.0 / pairs) - coef * ob).astype(BF)
        piece = cuts[g][...] if g == 0 else cuts[g][0][cuts[g][1] : cuts[g][1] + rows, :]
        wfq = wfq + dot_t(piece, grad_f)
        kmat = kmat + dot_t(d_hi, feat) + dot_t(d_lo, feat)
        sums = sums + (
            (jnp.sum(diff * ds) - jnp.sum(db * db) - LAMBDA * jnp.sum(norm * norm)) / (2.0 * pairs)
            - (jnp.sum(f32feat * ob) + LAMBDA * jnp.sum(norm)) / total
        )
        grad_own = through(
            -coef * f32feat - (norm * (2.0 * LAMBDA / pairs) + 2.0 * LAMBDA / total) * ob, raw, scale
        )
        wbq_ref[...] += dot_t(hidden, grad_own)
    wfq_ref[...] = wfq
    a_hi, a_lo = halves((kmat + (2.0 * LAMBDA / groups) * smat) * (1.0 / pairs))

    def second(number, ref, index):
        raw = raw_ref[at(number, index), :]
        back = back_ref[at(number, index), :]
        scale = lax.rsqrt(jnp.mean(raw * raw, axis=-1, keepdims=True) + EPS)
        grad = through(dot(back, a_hi) + dot(back, a_lo), raw, scale)
        hidden = ref[pl.ds(pl.multiple_of(index * chunk, chunk), chunk), :]
        wbq_ref[...] += dot_t(hidden, grad)

    over_rows(second)
    quarter, mine = place_ref[0], place_ref[1]
    wf_rows = wfq_ref.shape[0] // 4
    wb_rows = wbq_ref.shape[0] // 16
    size = wf_rows + wb_rows
    for ref, half in ((keep_ref, mine), (send_ref, 1 - mine)):
        for t in range(2):
            ref[t * size : t * size + wf_rows, :] = wfq_ref[
                pl.ds(pl.multiple_of((half * 2 + t) * wf_rows, wf_rows), wf_rows), :
            ]
            ref[t * size + wf_rows : (t + 1) * size, :] = wbq_ref[
                pl.ds(pl.multiple_of((quarter * 4 + half * 2 + t) * wb_rows, wb_rows), wb_rows), :
            ]
        ref[2 * size : 2 * size + 8, :] = jnp.full((8, width), sums, F32)


def assemble_kernel(place_ref, near_ref, far_ref, wf_ref, wb_ref, *, wf_rows, wb_rows, factor_f, factor_b):
    place = place_ref[0]
    for offset, ref in ((0, near_ref), (8, far_ref)):
        for e in range(8):
            to = place ^ (offset + e)
            wf_ref[pl.ds(pl.multiple_of(to * wf_rows, wf_rows), wf_rows), :] = (
                ref[e, :wf_rows, :].astype(F32) * factor_f
            )
            wb_ref[pl.ds(pl.multiple_of(to * wb_rows, wb_rows), wb_rows), :] = (
                ref[e, wf_rows:, :].astype(F32) * factor_b
            )


SMEM = pl.BlockSpec(memory_space=pltpu.SMEM)
VMEM = pl.BlockSpec(memory_space=pltpu.VMEM)


def body(hidden_f, hidden_t, hidden_b, w_f, w_t, w_b, latents, latent_ids, positives):
    rows, high = hidden_f.shape
    wide = hidden_b.shape[1]
    width = w_f.shape[1]
    size = lax.axis_size("fa")
    bits = size.bit_length() - 1
    outer = [1 << k for k in range(2, bits)]
    me = lax.axis_index("fa")
    total = size * rows
    cut = high // 4
    assert bits >= 4 and size == 1 << bits and cut == width

    hb0 = hidden_b
    for mask in reversed(outer):
        hb0 = jnp.concatenate([hb0, swap(hb0, mask, size)], axis=0)
    quarters = jnp.stack([reverse_bits((me ^ m) & 3, 2) for m in GROUP]).astype(jnp.int32)
    far, near, own = pl.pallas_call(
        feature_kernel,
        in_specs=[SMEM] + [VMEM] * 7,
        out_specs=[VMEM] * 3,
        out_shape=[
            jax.ShapeDtypeStruct((4 * rows + PAD, width), BF),
            jax.ShapeDtypeStruct((3 * rows + PAD, width), BF),
            jax.ShapeDtypeStruct((rows, width), BF),
        ],
        compiler_params=pltpu.CompilerParams(vmem_limit_bytes=24 * 2**20),
        cost_estimate=pl.CostEstimate(
            flops=4 * rows * high * width, bytes_accessed=4 * high * (rows + width), transcendentals=0
        ),
    )(
        quarters,
        hidden_f,
        hidden_t,
        w_f,
        w_t,
        latents,
        latent_ids.reshape(1, rows),
        positives.reshape(1, rows),
    )
    ff2 = swap(far, 2, size)
    ff1 = swap(near, 1, size)
    hb2 = swap(hb0, 2, size)
    hb1 = swap(hb0, 1, size)
    ff3 = swap(ff2, 1, size)
    hb3 = swap(hb2, 1, size)

    inner = reverse_bits(jnp.arange(size // 4, dtype=jnp.int32), bits - 2) << 2
    bases = jnp.concatenate([(me ^ m ^ inner) * rows for m in GROUP]).astype(jnp.int32)
    places = jnp.stack([quarters[0], ((me >> 2) & 1).astype(jnp.int32)])
    each = cut // 4 + wide // 16
    chunk = min(4 * rows, (size // 4) * rows)
    keep, send = pl.pallas_call(
        functools.partial(pair_kernel, rows=rows, total=total, chunk=chunk),
        in_specs=[SMEM] * 2 + [VMEM] * 10,
        out_specs=[VMEM] * 2,
        out_shape=[jax.ShapeDtypeStruct((2 * each + 8, width), F32)] * 2,
        scratch_shapes=[
            pltpu.VMEM((total, width), F32),
            pltpu.VMEM((total, width), BF),
            pltpu.VMEM((width, width), F32),
            pltpu.VMEM((4 * rows, wide), F32),
            pltpu.VMEM((cut, width), F32),
            pltpu.VMEM((wide, width), F32),
        ],
        compiler_params=pltpu.CompilerParams(vmem_limit_bytes=52 * 2**20),
    )(bases, places, hb0, hb2, hb1, hb3, own, near, ff2, ff1, ff3, w_b)

    current = keep + swap(send, outer[0], size)
    mine = (me >> 3) & 1
    note = current[2 * each :]
    keep = jnp.concatenate([lax.dynamic_slice_in_dim(current, mine * each, each, 0), note])
    send = jnp.concatenate([lax.dynamic_slice_in_dim(current, (1 - mine) * each, each, 0), note])
    current = keep + swap(send, outer[1], size)
    for mask in outer[2:]:
        current = current + swap(current, mask, size)
    result = current[:each].astype(BF).reshape(1, each, width)
    for mask in (8, 4, 2):
        result = jnp.concatenate([result, swap(result, mask, size)], axis=0)
    other = swap(result, 1, size)
    place = reverse_bits(me & 15, 4).astype(jnp.int32).reshape(1)
    grad_wf, grad_wb = pl.pallas_call(
        functools.partial(
            assemble_kernel,
            wf_rows=cut // 4,
            wb_rows=wide // 16,
            factor_f=math.sqrt(high),
            factor_b=math.sqrt(wide),
        ),
        in_specs=[SMEM, VMEM, VMEM],
        out_specs=[VMEM] * 2,
        out_shape=[
            jax.ShapeDtypeStruct((high, width), F32),
            jax.ShapeDtypeStruct((wide, width), F32),
        ],
        compiler_params=pltpu.CompilerParams(vmem_limit_bytes=16 * 2**20),
    )(place, result, other)
    return (grad_wf, grad_wb, current[each, :1] / width)


def solution(mesh):
    placed = (
        P(("grp", "fa"), None),
        P(("grp", "fa"), None),
        P(("grp", "fa"), None),
        P(),
        P(),
        P(),
        P("grp", None),
        P(("grp", "fa")),
        P(("grp", "fa")),
    )
    return jax.shard_map(
        body,
        mesh=mesh,
        in_specs=placed,
        out_specs=(P("grp", None), P("grp", None), P("grp")),
        check_vma=False,
    )
```

```python
import functools
import math

import jax
import jax.numpy as jnp
from jax import lax
from jax.experimental import pallas as pl
from jax.experimental.pallas import tpu as pltpu
from jax.sharding import PartitionSpec as P

GAMMA = 0.98
LAMBDA = 1.0
EPS = 1e-06
BF = jnp.bfloat16
F32 = jnp.float32
GROUP = (0, 2, 1, 3)
CUT_AT = (0, 0, 0, 1)
HEAD_AT = (0, 2, 1, 2)
PAD = 16
LINE = ((12, 3), (8, 1), (4, 2))


def dot(left, right):
    return jnp.dot(left, right, preferred_element_type=F32)


def dot_t(left, right):
    return lax.dot_general(left, right, (((0,), (0,)), ((), ())), preferred_element_type=F32)


def halves(array):
    high = array.astype(BF)
    return high, (array - high.astype(F32)).astype(BF)


def swap(array, mask, size):
    return lax.ppermute(array, "fa", [(i, i ^ mask) for i in range(size)])


def reverse_bits(value, bits):
    out = value * 0
    for k in range(bits):
        out = out + (((value >> k) & 1) << (bits - 1 - k))
    return out


def columns_of(row, rows):
    return jnp.transpose(jnp.broadcast_to(row, (rows, rows)))


def feature_kernel(
    hf_hbm, ht_hbm, wf_hbm, wt_hbm, lat_hbm, ids_hbm, pos_hbm, out_ref, hf, ht, wf, wt, lat, ids, pos, sems
):
    rows = hf.shape[0]
    width = wf.shape[1]
    moves = [
        pltpu.make_async_copy(source, target, sems.at[k])
        for k, (source, target) in enumerate(
            (
                (ids_hbm, ids),
                (pos_hbm, pos),
                (lat_hbm, lat),
                (hf_hbm, hf),
                (wf_hbm, wf),
                (ht_hbm, ht),
                (wt_hbm, wt),
            )
        )
    ]
    for move in moves:
        move.start()
    for move in moves[:3]:
        move.wait()
    who = columns_of(ids[...].astype(F32), rows)
    lanes = lax.broadcasted_iota(jnp.int32, (rows, rows), 1).astype(F32)
    tiles = [
        jnp.where(who == lanes + float(t * rows), 1.0, 0.0).astype(BF) for t in range(lat.shape[0] // rows)
    ]
    zrows = dot(jnp.concatenate(tiles, axis=1), lat[...])
    place = pos[...]
    line = lax.broadcasted_iota(jnp.int32, (PAD, rows), 0)
    high = jnp.broadcast_to(lax.shift_right_logical(place, 7).astype(F32), (PAD, rows))
    low = jnp.broadcast_to((place & 127).astype(F32), (PAD, rows))
    out_ref[2 * rows :, :] = jnp.zeros((PAD, width), BF)
    out_ref[2 * rows :, :rows] = jnp.where(line == 0, high, jnp.where(line == 1, low, 0.0)).astype(BF)
    moves[3].wait()
    moves[4].wait()
    out_ref[:rows, :] = (dot(hf[...], wf[...]) + zrows).astype(BF)
    moves[5].wait()
    moves[6].wait()
    out_ref[rows : 2 * rows, :] = (dot(ht[...], wt[...]) + zrows).astype(BF)


def pair_kernel(*refs, rows, total):
    base_ref, place_ref = refs[:2]
    head_ref, cut_ref, mails = refs[2], refs[3], refs[4:7]
    tails, feats, wb_ref = refs[7:11], refs[11:15], refs[15]
    keep_ref, sends = refs[16], refs[17:20]
    raw_ref, back_ref, smat_ref, pick_ref, wfq_ref, wbq_ref = refs[20:]
    heads, cuts = (head_ref,) + mails, (cut_ref,) + mails
    width = wb_ref.shape[1]
    pairs = float(total * (total - 1))
    groups = total // (4 * rows)
    span = total // 16
    wb = wb_ref[...]
    wanted = []
    for ref in feats:
        code = ref[2 * rows :, :rows].astype(F32)
        wanted.append(columns_of(code[0:1] * 128.0 + code[1:2], rows))
    lanes = lax.broadcasted_iota(jnp.int32, (rows, rows), 1)

    def embed(hidden):
        raw = dot(hidden, wb)
        scale = lax.rsqrt(jnp.mean(raw * raw, axis=-1, keepdims=True) + EPS)
        return raw, scale, (raw * scale).astype(BF)

    def through(grad, raw, scale):
        along = jnp.sum(grad * raw, axis=-1, keepdims=True)
        return (scale * grad - scale * scale * scale * (1.0 / width) * along * raw).astype(BF)

    def over_rows(step):
        for g in range(4):
            for ref, start, skip, chunk in (
                (heads[g], HEAD_AT[g] * rows, 0, rows),
                (tails[g], 0, span, 3 * rows),
            ):
                first = g * 4 * span + skip
                if span == rows:
                    step(ref, start, first, chunk)
                else:
                    lax.fori_loop(
                        0,
                        span // rows,
                        lambda i, c: (step(ref, start + i * chunk, first + i * chunk, chunk), c)[1],
                        0,
                    )

    def at(start, chunk):
        return pl.ds(pl.multiple_of(start, rows), chunk)

    smat_ref[...] = jnp.zeros_like(smat_ref)
    pick_ref[...] = jnp.zeros_like(pick_ref)
    wbq_ref[...] = jnp.zeros_like(wbq_ref)

    def first(ref, start, number, chunk):
        hidden = ref[at(start, chunk), :]
        raw, _, back = embed(hidden)
        raw_ref[at(number, chunk), :] = raw
        back_ref[at(number, chunk), :] = back
        smat_ref[...] += dot_t(back, back)
        ids = [(lanes + base_ref[number // rows + t]).astype(F32) for t in range(chunk // rows)]
        mask = jnp.concatenate(
            [
                jnp.concatenate([jnp.where(want == i, 1.0, 0.0).astype(BF) for i in ids], axis=1)
                for want in wanted
            ],
            axis=0,
        )
        pick_ref[...] += dot(mask, hidden)

    over_rows(first)
    smat = smat_ref[...]
    s_hi, s_lo = halves(smat)
    kmat = jnp.zeros((width, width), F32)
    wfq = jnp.zeros((cuts[0].shape[1], width), F32)
    sums = jnp.sum(smat * smat) / groups / (2.0 * pairs)
    for g, ref in enumerate(feats):
        feat = ref[:rows, :]
        f32feat = feat.astype(F32)
        diff = f32feat - GAMMA * ref[rows : 2 * rows, :].astype(F32)
        d_hi, d_lo = halves(diff)
        hidden = pick_ref[g * rows : (g + 1) * rows, :].astype(BF)
        raw, scale, back = embed(hidden)
        ob = back.astype(F32)
        ds = dot(d_hi, s_hi) + dot(d_lo, s_hi) + dot(d_hi, s_lo)
        db = jnp.sum(diff * ob, axis=-1, keepdims=True)
        coef = db * (1.0 / pairs) + 1.0 / total
        norm = jnp.sum(ob * ob, axis=-1, keepdims=True)
        grad_f = (ds * (1.0 / pairs) - coef * ob).astype(BF)
        wfq = wfq + dot_t(cuts[g][CUT_AT[g] * rows : (CUT_AT[g] + 1) * rows, :], grad_f)
        kmat = kmat + dot_t(d_hi, feat) + dot_t(d_lo, feat)
        sums = sums + (
            (jnp.sum(diff * ds) - jnp.sum(db * db) - LAMBDA * jnp.sum(norm * norm)) / (2.0 * pairs)
            - (jnp.sum(f32feat * ob) + LAMBDA * jnp.sum(norm)) / total
        )
        grad_own = through(
            -coef * f32feat - (norm * (2.0 * LAMBDA / pairs) + 2.0 * LAMBDA / total) * ob, raw, scale
        )
        wbq_ref[...] += dot_t(hidden, grad_own)
    wfq_ref[...] = wfq
    a_hi, a_lo = halves((kmat + (2.0 * LAMBDA / groups) * smat) * (1.0 / pairs))

    def second(ref, start, number, chunk):
        raw = raw_ref[at(number, chunk), :]
        scale = lax.rsqrt(jnp.mean(raw * raw, axis=-1, keepdims=True) + EPS)
        back = back_ref[at(number, chunk), :]
        grad = through(dot(back, a_hi) + dot(back, a_lo), raw, scale)
        wbq_ref[...] += dot_t(ref[at(start, chunk), :], grad)

    over_rows(second)
    quarter, mine = place_ref[0], place_ref[1]
    wf_rows = wfq_ref.shape[0] // 4
    wb_rows = wbq_ref.shape[0] // 16
    size = wf_rows + wb_rows

    def block(t):
        return (
            wfq_ref[pl.ds(pl.multiple_of(t * wf_rows, wf_rows), wf_rows), :],
            wbq_ref[pl.ds(pl.multiple_of((quarter * 4 + t) * wb_rows, wb_rows), wb_rows), :],
        )

    keep_ref[:wf_rows, :], keep_ref[wf_rows:size, :] = block(mine)
    note = jnp.full((PAD, width), sums, F32)
    keep_ref[size:, :] = note
    line = lax.broadcasted_iota(jnp.int32, (PAD, width), 0)
    n_hi = note.astype(BF)
    n_mid, n_lo = halves(note - n_hi.astype(F32))
    coded = jnp.where(
        line == 0,
        n_hi.astype(F32),
        jnp.where(line == 1, n_mid.astype(F32), jnp.where(line == 2, n_lo.astype(F32), 0.0)),
    ).astype(BF)
    for ref, (_, turn) in zip(sends, LINE):
        part_f, part_b = block(mine ^ turn)
        ref[:wf_rows, :] = part_f.astype(BF)
        ref[wf_rows:size, :] = part_b.astype(BF)
        ref[size:, :] = coded


def assemble_kernel(place_ref, *refs, wf_rows, wb_rows, factor_f, factor_b):
    place = place_ref[0]
    wf_ref, wb_ref = refs[4:]
    for offset, ref in zip((0, 4, 8, 12), refs):
        for e, turn in enumerate((0,) + tuple(turn for _, turn in LINE)):
            to = place ^ (offset + turn)
            wf_ref[pl.ds(pl.multiple_of(to * wf_rows, wf_rows), wf_rows), :] = (
                ref[e, :wf_rows, :].astype(F32) * factor_f
            )
            wb_ref[pl.ds(pl.multiple_of(to * wb_rows, wb_rows), wb_rows), :] = (
                ref[e, wf_rows:, :].astype(F32) * factor_b
            )


SMEM = pl.BlockSpec(memory_space=pltpu.SMEM)
VMEM = pl.BlockSpec(memory_space=pltpu.VMEM)
HBM = pl.BlockSpec(memory_space=pltpu.HBM)


def body(hidden_f, hidden_t, hidden_b, w_f, w_t, w_b, latents, latent_ids, positives):
    rows, high = hidden_f.shape
    wide = hidden_b.shape[1]
    width = w_f.shape[1]
    size = lax.axis_size("fa")
    bits = size.bit_length() - 1
    beyond = [1 << k for k in range(4, bits)]
    me = lax.axis_index("fa")
    total = size * rows
    cut = high // 4
    span = total // 16
    assert bits >= 4 and size == 1 << bits and cut == width == wide

    quarters = [reverse_bits((me ^ m) & 3, 2).astype(jnp.int32) for m in GROUP]
    cut0, cut2, cut1, cut3 = [
        lax.dynamic_slice_in_dim(hidden_f, q * cut, cut, 1) for q in quarters
    ]
    head0 = hidden_b
    for mask in reversed(beyond):
        head0 = jnp.concatenate([head0, swap(head0, mask, size)], axis=0)
    tail0 = jnp.concatenate([swap(head0, mask, size) for mask, _ in LINE], axis=0)
    mail2 = swap(jnp.concatenate([cut2, cut3, head0], axis=0), 2, size)
    mail1 = swap(jnp.concatenate([cut1, head0], axis=0), 1, size)
    mail3 = swap(mail2, 1, size)
    ff0 = pl.pallas_call(
        feature_kernel,
        in_specs=[HBM] * 7,
        out_specs=VMEM,
        out_shape=jax.ShapeDtypeStruct((2 * rows + PAD, width), BF),
        scratch_shapes=[
            pltpu.VMEM(hidden_f.shape, BF),
            pltpu.VMEM(hidden_t.shape, BF),
            pltpu.VMEM(w_f.shape, BF),
            pltpu.VMEM(w_t.shape, BF),
            pltpu.VMEM(latents.shape, BF),
            pltpu.VMEM((1, rows), jnp.int32),
            pltpu.VMEM((1, rows), jnp.int32),
            pltpu.SemaphoreType.DMA((7,)),
        ],
        compiler_params=pltpu.CompilerParams(vmem_limit_bytes=24 * 2**20),
        cost_estimate=pl.CostEstimate(
            flops=4 * rows * high * width, bytes_accessed=4 * high * (rows + width), transcendentals=0
        ),
    )(
        hidden_f,
        hidden_t,
        w_f,
        w_t,
        latents,
        latent_ids.reshape(1, rows),
        positives.reshape(1, rows),
    )
    ff2 = swap(ff0, 2, size)
    ff1 = swap(ff0, 1, size)
    tail2 = swap(tail0, 2, size)
    tail1 = swap(tail0, 1, size)
    ff3 = swap(ff2, 1, size)
    tail3 = swap(tail2, 1, size)

    inner = reverse_bits(jnp.arange(size // 16, dtype=jnp.int32), bits - 4) << 4
    bases = jnp.concatenate(
        [(me ^ m ^ o ^ inner) * rows for m in GROUP for o in (0,) + tuple(o for o, _ in LINE)]
    ).astype(jnp.int32)
    place = reverse_bits(me & 15, 4).astype(jnp.int32)
    places = jnp.stack([quarters[0], place & 3])
    each = cut // 4 + wide // 16
    keep, *sends = pl.pallas_call(
        functools.partial(pair_kernel, rows=rows, total=total),
        in_specs=[SMEM] * 2 + [VMEM] * 14,
        out_specs=[VMEM] * 4,
        out_shape=[jax.ShapeDtypeStruct((each + PAD, width), F32)]
        + [jax.ShapeDtypeStruct((each + PAD, width), BF)] * 3,
        scratch_shapes=[
            pltpu.VMEM((total, width), F32),
            pltpu.VMEM((total, width), BF),
            pltpu.VMEM((width, width), F32),
            pltpu.VMEM((4 * rows, wide), F32),
            pltpu.VMEM((cut, width), F32),
            pltpu.VMEM((wide, width), F32),
        ],
        compiler_params=pltpu.CompilerParams(vmem_limit_bytes=52 * 2**20),
    )(
        bases,
        places,
        head0,
        cut0,
        mail2,
        mail1,
        mail3,
        tail0,
        tail2,
        tail1,
        tail3,
        ff0,
        ff2,
        ff1,
        ff3,
        w_b,
    )

    got = [swap(part, mask, size).astype(F32) for part, (mask, _) in zip(sends, LINE)]
    current = keep[:each] + (got[0][:each] + got[1][:each] + got[2][:each])
    note = keep[each, :1]
    for part in got:
        note = note + (part[each, :1] + part[each + 1, :1] + part[each + 2, :1])
    for mask in beyond:
        current = current + swap(current, mask, size)
        note = note + swap(note, mask, size)
    result = current.astype(BF).reshape(1, each, width)
    pieces = [result] + [swap(result, mask, size) for mask, _ in LINE]
    crossed = [swap(piece, 2, size) for piece in pieces]
    near = jnp.concatenate(pieces, axis=0)
    near_y = jnp.concatenate(crossed, axis=0)
    far = swap(near, 1, size)
    far_y = swap(near_y, 1, size)
    grad_wf, grad_wb = pl.pallas_call(
        functools.partial(
            assemble_kernel,
            wf_rows=cut // 4,
            wb_rows=wide // 16,
            factor_f=math.sqrt(high),
            factor_b=math.sqrt(wide),
        ),
        in_specs=[SMEM] + [VMEM] * 4,
        out_specs=[VMEM] * 2,
        out_shape=[
            jax.ShapeDtypeStruct((high, width), F32),
            jax.ShapeDtypeStruct((wide, width), F32),
        ],
        compiler_params=pltpu.CompilerParams(vmem_limit_bytes=16 * 2**20),
    )(place.reshape(1), near, near_y, far, far_y)
    return (grad_wf, grad_wb, note / width)


def solution(mesh):
    placed = (
        P(("grp", "fa"), None),
        P(("grp", "fa"), None),
        P(("grp", "fa"), None),
        P(),
        P(),
        P(),
        P("grp", None),
        P(("grp", "fa")),
        P(("grp", "fa")),
    )
    return jax.shard_map(
        body,
        mesh=mesh,
        in_specs=placed,
        out_specs=(P("grp", None), P("grp", None), P("grp")),
        check_vma=False,
    )
```

```python
import functools
import math

import jax
import jax.numpy as jnp
from jax import lax
from jax.experimental import pallas as pl
from jax.experimental.pallas import tpu as pltpu
from jax.sharding import PartitionSpec as P

GAMMA = 0.98
LAMBDA = 1.0
EPS = 1e-06
BF = jnp.bfloat16
F32 = jnp.float32
GROUP = (0, 2, 1, 3)
CUT_AT = (0, 0, 0, 1)
HEAD_AT = (1, 2, 1, 2)
FEAT_AT = (2, 3, 2, 3)
PAD = 16
LINE = ((12, 3), (8, 1), (4, 2))


def dot(left, right):
    return jnp.dot(left, right, preferred_element_type=F32)


def dot_t(left, right):
    return lax.dot_general(left, right, (((0,), (0,)), ((), ())), preferred_element_type=F32)


def halves(array):
    high = array.astype(BF)
    return high, (array - high.astype(F32)).astype(BF)


def swap(array, mask, size):
    return lax.ppermute(array, "fa", [(i, i ^ mask) for i in range(size)])


def reverse_bits(value, bits):
    out = value * 0
    for k in range(bits):
        out = out + (((value >> k) & 1) << (bits - 1 - k))
    return out


def columns_of(row, rows):
    return jnp.transpose(jnp.broadcast_to(row, (rows, rows)))


def feature_kernel(
    quarter_ref,
    hf_hbm,
    ht_hbm,
    hb_hbm,
    wf_hbm,
    wt_hbm,
    wb_hbm,
    lat_hbm,
    ids_hbm,
    pos_hbm,
    far_ref,
    near_ref,
    cut_ref,
    head_ref,
    wb_ref,
    hf,
    ht,
    wf,
    wt,
    lat,
    ids,
    pos,
    sems,
):
    rows = hf.shape[0]
    width = wf.shape[1]
    moves = [
        pltpu.make_async_copy(source, target, sems.at[k])
        for k, (source, target) in enumerate(
            (
                (ids_hbm, ids),
                (pos_hbm, pos),
                (lat_hbm, lat),
                (hf_hbm, hf),
                (wf_hbm, wf),
                (ht_hbm, ht),
                (wt_hbm, wt),
                (hb_hbm, head_ref),
                (wb_hbm, wb_ref),
            )
        )
    ]
    for move in moves:
        move.start()
    for move in moves[:3]:
        move.wait()
    who = columns_of(ids[...].astype(F32), rows)
    lanes = lax.broadcasted_iota(jnp.int32, (rows, rows), 1).astype(F32)
    tiles = [
        jnp.where(who == lanes + float(t * rows), 1.0, 0.0).astype(BF) for t in range(lat.shape[0] // rows)
    ]
    zrows = dot(jnp.concatenate(tiles, axis=1), lat[...])
    place = pos[...]
    line = lax.broadcasted_iota(jnp.int32, (PAD, rows), 0)
    high = jnp.broadcast_to(lax.shift_right_logical(place, 7).astype(F32), (PAD, rows))
    low = jnp.broadcast_to((place & 127).astype(F32), (PAD, rows))
    coded = jnp.where(line == 0, high, jnp.where(line == 1, low, 0.0)).astype(BF)
    coded = jnp.concatenate([coded] + [jnp.zeros((PAD, width - rows), BF)] * (width > rows), axis=1)

    def piece(slot):
        return hf[:, pl.ds(pl.multiple_of(quarter_ref[slot] * width, width), width)]

    moves[3].wait()
    cut_ref[...] = piece(0)
    far_ref[:rows, :] = piece(1)
    near_ref[:rows, :] = piece(2)
    far_ref[rows : 2 * rows, :] = piece(3)
    moves[4].wait()
    feat = (dot(hf[...], wf[...]) + zrows).astype(BF)
    moves[5].wait()
    moves[6].wait()
    feat_t = (dot(ht[...], wt[...]) + zrows).astype(BF)
    moves[7].wait()
    head = head_ref[...]
    for ref, at in ((far_ref, HEAD_AT[1]), (near_ref, HEAD_AT[2])):
        ref[at * rows : (at + 1) * rows, :] = head
        ref[(at + 1) * rows : (at + 2) * rows, :] = feat
        ref[(at + 2) * rows : (at + 3) * rows, :] = feat_t
        ref[(at + 3) * rows :, :] = coded
    moves[8].wait()


def pair_kernel(*refs, rows, total):
    base_ref, place_ref = refs[:2]
    mails, tails, cut_ref, wb_ref = refs[2:6], refs[6:10], refs[10], refs[11]
    keep_ref, sends = refs[12], refs[13:16]
    raw_ref, back_ref, smat_ref, pick_ref, wfq_ref, wbq_ref = refs[16:]
    width = wb_ref.shape[1]
    pairs = float(total * (total - 1))
    groups = total // (4 * rows)
    span = total // 4
    wb = wb_ref[...]
    wanted = []
    for g, ref in enumerate(mails):
        code = ref[(FEAT_AT[g] + 2) * rows :, :rows].astype(F32)
        wanted.append(columns_of(code[0:1] * 128.0 + code[1:2], rows))
    lanes = lax.broadcasted_iota(jnp.int32, (rows, rows), 1)

    def embed(hidden):
        raw = dot(hidden, wb)
        scale = lax.rsqrt(jnp.mean(raw * raw, axis=-1, keepdims=True) + EPS)
        return raw, scale, (raw * scale).astype(BF)

    def through(grad, raw, scale):
        along = jnp.sum(grad * raw, axis=-1, keepdims=True)
        return (scale * grad - scale * scale * scale * (1.0 / width) * along * raw).astype(BF)

    def over_rows(step):
        for g in range(4):
            step(mails[g], HEAD_AT[g] * rows, g * span, rows)
            first = g * span + rows
            if span == 4 * rows:
                step(tails[g], 0, first, 3 * rows)
            else:

                def one(i, carry, ref=tails[g], first=first):
                    step(ref, i * rows, first + i * rows, rows)
                    return carry

                lax.fori_loop(0, span // rows - 1, one, 0)

    def at(start, chunk):
        return pl.ds(pl.multiple_of(start, rows), chunk)

    smat_ref[...] = jnp.zeros_like(smat_ref)
    pick_ref[...] = jnp.zeros_like(pick_ref)
    wbq_ref[...] = jnp.zeros_like(wbq_ref)

    def first(ref, start, number, chunk):
        hidden = ref[at(start, chunk), :]
        raw, _, back = embed(hidden)
        raw_ref[at(number, chunk), :] = raw
        back_ref[at(number, chunk), :] = back
        smat_ref[...] += dot_t(back, back)
        ids = [(lanes + base_ref[number // rows + t]).astype(F32) for t in range(chunk // rows)]
        mask = jnp.concatenate(
            [
                jnp.concatenate([jnp.where(want == i, 1.0, 0.0).astype(BF) for i in ids], axis=1)
                for want in wanted
            ],
            axis=0,
        )
        pick_ref[...] += dot(mask, hidden)

    over_rows(first)
    smat = smat_ref[...]
    s_hi, s_lo = halves(smat)
    kmat = jnp.zeros((width, width), F32)
    wfq = jnp.zeros((cut_ref.shape[1], width), F32)
    sums = jnp.sum(smat * smat) / groups / (2.0 * pairs)
    for g, ref in enumerate(mails):
        start = FEAT_AT[g] * rows
        feat = ref[start : start + rows, :]
        f32feat = feat.astype(F32)
        diff = f32feat - GAMMA * ref[start + rows : start + 2 * rows, :].astype(F32)
        d_hi, d_lo = halves(diff)
        hidden = pick_ref[g * rows : (g + 1) * rows, :].astype(BF)
        raw, scale, back = embed(hidden)
        ob = back.astype(F32)
        ds = dot(d_hi, s_hi) + dot(d_lo, s_hi) + dot(d_hi, s_lo)
        db = jnp.sum(diff * ob, axis=-1, keepdims=True)
        coef = db * (1.0 / pairs) + 1.0 / total
        norm = jnp.sum(ob * ob, axis=-1, keepdims=True)
        grad_f = (ds * (1.0 / pairs) - coef * ob).astype(BF)
        cut = (cut_ref if g == 0 else ref)[CUT_AT[g] * rows : (CUT_AT[g] + 1) * rows, :]
        wfq = wfq + dot_t(cut, grad_f)
        kmat = kmat + dot_t(d_hi, feat) + dot_t(d_lo, feat)
        sums = sums + (
            (jnp.sum(diff * ds) - jnp.sum(db * db) - LAMBDA * jnp.sum(norm * norm)) / (2.0 * pairs)
            - (jnp.sum(f32feat * ob) + LAMBDA * jnp.sum(norm)) / total
        )
        grad_own = through(
            -coef * f32feat - (norm * (2.0 * LAMBDA / pairs) + 2.0 * LAMBDA / total) * ob, raw, scale
        )
        wbq_ref[...] += dot_t(hidden, grad_own)
    wfq_ref[...] = wfq
    a_hi, a_lo = halves((kmat + (2.0 * LAMBDA / groups) * smat) * (1.0 / pairs))

    def second(ref, start, number, chunk):
        raw = raw_ref[at(number, chunk), :]
        scale = lax.rsqrt(jnp.mean(raw * raw, axis=-1, keepdims=True) + EPS)
        back = back_ref[at(number, chunk), :]
        grad = through(dot(back, a_hi) + dot(back, a_lo), raw, scale)
        wbq_ref[...] += dot_t(ref[at(start, chunk), :], grad)

    over_rows(second)
    quarter, mine = place_ref[0], place_ref[1]
    wf_rows = wfq_ref.shape[0] // 4
    wb_rows = wbq_ref.shape[0] // 16
    size = wf_rows + wb_rows

    def block(t):
        return (
            wfq_ref[pl.ds(pl.multiple_of(t * wf_rows, wf_rows), wf_rows), :],
            wbq_ref[pl.ds(pl.multiple_of((quarter * 4 + t) * wb_rows, wb_rows), wb_rows), :],
        )

    keep_ref[:wf_rows, :], keep_ref[wf_rows:size, :] = block(mine)
    note = jnp.full((PAD, width), sums, F32)
    keep_ref[size:, :] = note
    line = lax.broadcasted_iota(jnp.int32, (PAD, width), 0)
    n_hi = note.astype(BF)
    n_mid, n_lo = halves(note - n_hi.astype(F32))
    coded = jnp.where(
        line == 0,
        n_hi.astype(F32),
        jnp.where(line == 1, n_mid.astype(F32), jnp.where(line == 2, n_lo.astype(F32), 0.0)),
    ).astype(BF)
    for ref, (_, turn) in zip(sends, LINE):
        part_f, part_b = block(mine ^ turn)
        ref[:wf_rows, :] = part_f.astype(BF)
        ref[wf_rows:size, :] = part_b.astype(BF)
        ref[size:, :] = coded


def add_kernel(keep_ref, *refs):
    sum_ref, note_ref = refs[3:]
    size, width = sum_ref.shape
    total = keep_ref[:size, :]
    note = keep_ref[size : size + 1, :1]
    for ref in refs[:3]:
        total = total + ref[:size, :].astype(F32)
        coded = ref[size:, :].astype(F32)
        note = note + (coded[0:1, :1] + coded[1:2, :1] + coded[2:3, :1])
    sum_ref[...] = total.astype(sum_ref.dtype)
    note_ref[...] = note * (1.0 / width)


def assemble_kernel(place_ref, *refs, wf_rows, wb_rows, factor_f, factor_b):
    place = place_ref[0]
    wf_ref, wb_ref = refs[4:]
    for offset, ref in zip((0, 4, 8, 12), refs):
        for e, turn in enumerate((0,) + tuple(turn for _, turn in LINE)):
            to = place ^ (offset + turn)
            wf_ref[pl.ds(pl.multiple_of(to * wf_rows, wf_rows), wf_rows), :] = (
                ref[e, :wf_rows, :].astype(F32) * factor_f
            )
            wb_ref[pl.ds(pl.multiple_of(to * wb_rows, wb_rows), wb_rows), :] = (
                ref[e, wf_rows:, :].astype(F32) * factor_b
            )


SMEM = pl.BlockSpec(memory_space=pltpu.SMEM)
VMEM = pl.BlockSpec(memory_space=pltpu.VMEM)
HBM = pl.BlockSpec(memory_space=pltpu.HBM)


def body(hidden_f, hidden_t, hidden_b, w_f, w_t, w_b, latents, latent_ids, positives):
    rows, high = hidden_f.shape
    wide = hidden_b.shape[1]
    width = w_f.shape[1]
    size = lax.axis_size("fa")
    bits = size.bit_length() - 1
    beyond = [1 << k for k in range(4, bits)]
    me = lax.axis_index("fa")
    total = size * rows
    assert bits >= 4 and size == 1 << bits and high // 4 == width == wide

    quarters = [reverse_bits((me ^ m) & 3, 2).astype(jnp.int32) for m in GROUP]
    ends = [(at + 2) * rows + PAD for at in FEAT_AT]
    far, near, cut, head, wb_copy = pl.pallas_call(
        feature_kernel,
        in_specs=[SMEM] + [HBM] * 9,
        out_specs=[VMEM] * 5,
        out_shape=[
            jax.ShapeDtypeStruct((ends[1], width), BF),
            jax.ShapeDtypeStruct((ends[2], width), BF),
            jax.ShapeDtypeStruct((rows, width), BF),
            jax.ShapeDtypeStruct(hidden_b.shape, BF),
            jax.ShapeDtypeStruct(w_b.shape, BF),
        ],
        scratch_shapes=[
            pltpu.VMEM(hidden_f.shape, BF),
            pltpu.VMEM(hidden_t.shape, BF),
            pltpu.VMEM(w_f.shape, BF),
            pltpu.VMEM(w_t.shape, BF),
            pltpu.VMEM(latents.shape, BF),
            pltpu.VMEM((1, rows), jnp.int32),
            pltpu.VMEM((1, rows), jnp.int32),
            pltpu.SemaphoreType.DMA((9,)),
        ],
        compiler_params=pltpu.CompilerParams(vmem_limit_bytes=60 * 2**20),
    )(
        jnp.stack(quarters),
        hidden_f,
        hidden_t,
        hidden_b,
        w_f,
        w_t,
        w_b,
        latents,
        latent_ids.reshape(1, rows),
        positives.reshape(1, rows),
    )
    far2 = swap(far, 2, size)
    for mask in reversed(beyond):
        head = jnp.concatenate([head, swap(head, mask, size)], axis=0)
    tail0 = jnp.concatenate(
        [head[rows:]] * (len(beyond) > 0) + [swap(head, mask, size) for mask, _ in LINE], axis=0
    )
    near1 = swap(near, 1, size)
    tail2 = swap(tail0, 2, size)
    tail1 = swap(tail0, 1, size)
    far3 = swap(far2, 1, size)
    tail3 = swap(tail2, 1, size)

    inner = reverse_bits(jnp.arange(size // 16, dtype=jnp.int32), bits - 4) << 4
    bases = jnp.concatenate(
        [(me ^ m ^ o ^ inner) * rows for m in GROUP for o in (0,) + tuple(o for o, _ in LINE)]
    ).astype(jnp.int32)
    place = reverse_bits(me & 15, 4).astype(jnp.int32)
    places = jnp.stack([quarters[0], place & 3])
    wf_rows, wb_rows = high // 16, wide // 16
    each = wf_rows + wb_rows
    keep, *sends = pl.pallas_call(
        functools.partial(pair_kernel, rows=rows, total=total),
        in_specs=[SMEM] * 2 + [VMEM] * 10,
        out_specs=[VMEM] * 4,
        out_shape=[jax.ShapeDtypeStruct((each + PAD, width), F32)]
        + [jax.ShapeDtypeStruct((each + PAD, width), BF)] * 3,
        scratch_shapes=[
            pltpu.VMEM((total, width), F32),
            pltpu.VMEM((total, width), BF),
            pltpu.VMEM((width, width), F32),
            pltpu.VMEM((4 * rows, wide), F32),
            pltpu.VMEM((width, width), F32),
            pltpu.VMEM((wide, width), F32),
        ],
        compiler_params=pltpu.CompilerParams(vmem_limit_bytes=12 * 2**20 + total * width * 8),
    )(bases, places, near, far2, near1, far3, tail0, tail2, tail1, tail3, cut, wb_copy)

    got = [swap(part, mask, size) for part, (mask, _) in zip(sends, LINE)]
    result, note = pl.pallas_call(
        add_kernel,
        in_specs=[VMEM] * 4,
        out_specs=[VMEM] * 2,
        out_shape=[
            jax.ShapeDtypeStruct((each, width), F32 if beyond else BF),
            jax.ShapeDtypeStruct((1, 1), F32),
        ],
        compiler_params=pltpu.CompilerParams(vmem_limit_bytes=8 * 2**20),
    )(keep, *got)
    for mask in beyond:
        result = result + swap(result, mask, size)
        note = note + swap(note, mask, size)
    result = result.astype(BF).reshape(1, each, width)
    near = jnp.concatenate([result] + [swap(result, mask, size) for mask, _ in LINE], axis=0)
    near_y = swap(near, 2, size)
    far = swap(near, 1, size)
    far_y = swap(near_y, 1, size)
    grad_wf, grad_wb = pl.pallas_call(
        functools.partial(
            assemble_kernel,
            wf_rows=wf_rows,
            wb_rows=wb_rows,
            factor_f=math.sqrt(high),
            factor_b=math.sqrt(wide),
        ),
        in_specs=[SMEM] + [VMEM] * 4,
        out_specs=[VMEM] * 2,
        out_shape=[
            jax.ShapeDtypeStruct((high, width), F32),
            jax.ShapeDtypeStruct((wide, width), F32),
        ],
        compiler_params=pltpu.CompilerParams(vmem_limit_bytes=16 * 2**20),
    )(place.reshape(1), near, near_y, far, far_y)
    return (grad_wf, grad_wb, note.reshape(1))


def solution(mesh):
    placed = (
        P(("grp", "fa"), None),
        P(("grp", "fa"), None),
        P(("grp", "fa"), None),
        P(),
        P(),
        P(),
        P("grp", None),
        P(("grp", "fa")),
        P(("grp", "fa")),
    )
    return jax.shard_map(
        body,
        mesh=mesh,
        in_specs=placed,
        out_specs=(P("grp", None), P("grp", None), P("grp")),
        check_vma=False,
    )
```

```python
import functools
import math

import jax
import jax.numpy as jnp
from jax import lax
from jax.experimental import pallas as pl
from jax.experimental.pallas import tpu as pltpu
from jax.sharding import PartitionSpec as P

GAMMA = 0.98
LAMBDA = 1.0
EPS = 1e-06
BF = jnp.bfloat16
F32 = jnp.float32
GROUP = (0, 1)
HEAD_AT = 2
FEAT_AT = 3
PAD = 16
LINE = ((12, 3), (8, 1), (4, 2))
TURNS = (0, 3, 1, 2, 4, 7, 5, 6)


def dot(left, right):
    return jnp.dot(left, right, preferred_element_type=F32)


def dot_t(left, right):
    return lax.dot_general(left, right, (((0,), (0,)), ((), ())), preferred_element_type=F32)


def halves(array):
    high = array.astype(BF)
    return high, (array - high.astype(F32)).astype(BF)


def swap(array, mask, size):
    return lax.ppermute(array, "fa", [(i, i ^ mask) for i in range(size)])


def reverse_bits(value, bits):
    out = value * 0
    for k in range(bits):
        out = out + (((value >> k) & 1) << (bits - 1 - k))
    return out


def columns_of(row, rows):
    return jnp.transpose(jnp.broadcast_to(row, (rows, rows)))


def feature_kernel(
    core_ref,
    hf_hbm,
    ht_hbm,
    hb_hbm,
    wf_hbm,
    wt_hbm,
    wb_hbm,
    lat_hbm,
    ids_hbm,
    pos_hbm,
    near_ref,
    cut_ref,
    head_ref,
    wb_ref,
    hf,
    ht,
    wf,
    wt,
    lat,
    ids,
    pos,
    sems,
):
    rows = hf.shape[0]
    width = wf.shape[1]
    moves = [
        pltpu.make_async_copy(source, target, sems.at[k])
        for k, (source, target) in enumerate(
            (
                (ids_hbm, ids),
                (pos_hbm, pos),
                (lat_hbm, lat),
                (hf_hbm, hf),
                (wf_hbm, wf),
                (ht_hbm, ht),
                (wt_hbm, wt),
                (hb_hbm, head_ref),
                (wb_hbm, wb_ref),
            )
        )
    ]
    for move in moves:
        move.start()
    for move in moves[:3]:
        move.wait()
    who = columns_of(ids[...].astype(F32), rows)
    lanes = lax.broadcasted_iota(jnp.int32, (rows, rows), 1).astype(F32)
    tiles = [
        jnp.where(who == lanes + float(t * rows), 1.0, 0.0).astype(BF) for t in range(lat.shape[0] // rows)
    ]
    zrows = dot(jnp.concatenate(tiles, axis=1), lat[...])
    place = pos[...]
    line = lax.broadcasted_iota(jnp.int32, (PAD, rows), 0)
    high = jnp.broadcast_to(lax.shift_right_logical(place, 7).astype(F32), (PAD, rows))
    low = jnp.broadcast_to((place & 127).astype(F32), (PAD, rows))
    coded = jnp.where(line == 0, high, jnp.where(line == 1, low, 0.0)).astype(BF)
    coded = jnp.concatenate([coded] + [jnp.zeros((PAD, width - rows), BF)] * (width > rows), axis=1)

    moves[3].wait()
    core = core_ref[0]
    for t in range(2):
        for ref, half in ((cut_ref, core), (near_ref, 1 - core)):
            ref[t * rows : (t + 1) * rows, :] = hf[
                :, pl.ds(pl.multiple_of((half * 2 + t) * width, width), width)
            ]
    moves[4].wait()
    feat = (dot(hf[...], wf[...]) + zrows).astype(BF)
    moves[5].wait()
    moves[6].wait()
    feat_t = (dot(ht[...], wt[...]) + zrows).astype(BF)
    moves[7].wait()
    near_ref[HEAD_AT * rows : FEAT_AT * rows, :] = head_ref[...]
    near_ref[FEAT_AT * rows : (FEAT_AT + 1) * rows, :] = feat
    near_ref[(FEAT_AT + 1) * rows : (FEAT_AT + 2) * rows, :] = feat_t
    near_ref[(FEAT_AT + 2) * rows :, :] = coded
    moves[8].wait()


def pair_kernel(*refs, rows, total):
    base_ref, place_ref = refs[:2]
    mails, tails, cut_ref, wb_ref = refs[2:4], refs[4:6], refs[6], refs[7]
    keep_ref, send_ref = refs[8:10]
    raw_ref, back_ref, smat_ref, pick_ref, wfq_ref, wbq_ref = refs[10:]
    width = wb_ref.shape[1]
    pairs = float(total * (total - 1))
    groups = total // (2 * rows)
    span = total // 2
    wb = wb_ref[...]
    wanted = []
    for ref in mails:
        code = ref[(FEAT_AT + 2) * rows :, :rows].astype(F32)
        wanted.append(columns_of(code[0:1] * 128.0 + code[1:2], rows))
    lanes = lax.broadcasted_iota(jnp.int32, (rows, rows), 1)

    def embed(hidden):
        raw = dot(hidden, wb)
        scale = lax.rsqrt(jnp.mean(raw * raw, axis=-1, keepdims=True) + EPS)
        return raw, scale, (raw * scale).astype(BF)

    def through(grad, raw, scale):
        along = jnp.sum(grad * raw, axis=-1, keepdims=True)
        return (scale * grad - scale * scale * scale * (1.0 / width) * along * raw).astype(BF)

    def over_rows(step):
        for g in range(2):
            step(mails[g], HEAD_AT * rows, g * span, rows)
            first = g * span + rows
            if span == 8 * rows:
                step(tails[g], 0, first, 4 * rows)
                step(tails[g], 4 * rows, first + 4 * rows, 3 * rows)
            else:

                def one(i, carry, ref=tails[g], first=first):
                    step(ref, i * rows, first + i * rows, rows)
                    return carry

                lax.fori_loop(0, span // rows - 1, one, 0)

    def at(start, chunk):
        return pl.ds(pl.multiple_of(start, rows), chunk)

    smat_ref[...] = jnp.zeros_like(smat_ref)
    pick_ref[...] = jnp.zeros_like(pick_ref)
    wbq_ref[...] = jnp.zeros_like(wbq_ref)

    def first(ref, start, number, chunk):
        hidden = ref[at(start, chunk), :]
        raw, _, back = embed(hidden)
        raw_ref[at(number, chunk), :] = raw
        back_ref[at(number, chunk), :] = back
        smat_ref[...] += dot_t(back, back)
        ids = [(lanes + base_ref[number // rows + t]).astype(F32) for t in range(chunk // rows)]
        mask = jnp.concatenate(
            [
                jnp.concatenate([jnp.where(want == i, 1.0, 0.0).astype(BF) for i in ids], axis=1)
                for want in wanted
            ],
            axis=0,
        )
        pick_ref[...] += dot(mask, hidden)

    over_rows(first)
    smat = smat_ref[...]
    s_hi, s_lo = halves(smat)
    kmat = jnp.zeros((width, width), F32)
    wfq = [jnp.zeros((width, width), F32)] * 2
    sums = jnp.sum(smat * smat) / groups / (2.0 * pairs)
    for g, ref in enumerate(mails):
        start = FEAT_AT * rows
        feat = ref[start : start + rows, :]
        f32feat = feat.astype(F32)
        diff = f32feat - GAMMA * ref[start + rows : start + 2 * rows, :].astype(F32)
        d_hi, d_lo = halves(diff)
        hidden = pick_ref[g * rows : (g + 1) * rows, :].astype(BF)
        raw, scale, back = embed(hidden)
        ob = back.astype(F32)
        ds = dot(d_hi, s_hi) + dot(d_lo, s_hi) + dot(d_hi, s_lo)
        db = jnp.sum(diff * ob, axis=-1, keepdims=True)
        coef = db * (1.0 / pairs) + 1.0 / total
        norm = jnp.sum(ob * ob, axis=-1, keepdims=True)
        grad_f = (ds * (1.0 / pairs) - coef * ob).astype(BF)
        cut_from = cut_ref if g == 0 else ref
        wfq = [wfq[t] + dot_t(cut_from[t * rows : (t + 1) * rows, :], grad_f) for t in range(2)]
        kmat = kmat + dot_t(d_hi, feat) + dot_t(d_lo, feat)
        sums = sums + (
            (jnp.sum(diff * ds) - jnp.sum(db * db) - LAMBDA * jnp.sum(norm * norm)) / (2.0 * pairs)
            - (jnp.sum(f32feat * ob) + LAMBDA * jnp.sum(norm)) / total
        )
        grad_own = through(
            -coef * f32feat - (norm * (2.0 * LAMBDA / pairs) + 2.0 * LAMBDA / total) * ob, raw, scale
        )
        wbq_ref[...] += dot_t(hidden, grad_own)
    wfq_ref[:width, :] = wfq[0]
    wfq_ref[width:, :] = wfq[1]
    a_hi, a_lo = halves((kmat + (2.0 * LAMBDA / groups) * smat) * (1.0 / pairs))

    def second(ref, start, number, chunk):
        raw = raw_ref[at(number, chunk), :]
        scale = lax.rsqrt(jnp.mean(raw * raw, axis=-1, keepdims=True) + EPS)
        back = back_ref[at(number, chunk), :]
        grad = through(dot(back, a_hi) + dot(back, a_lo), raw, scale)
        wbq_ref[...] += dot_t(ref[at(start, chunk), :], grad)

    over_rows(second)
    core, mine = place_ref[0], place_ref[1]
    wf_rows = wfq_ref.shape[0] // 8
    wb_rows = wbq_ref.shape[0] // 16
    size = wf_rows + wb_rows
    for ref, half in ((keep_ref, mine), (send_ref, 1 - mine)):
        for t in range(4):
            at_f, at_b = half * 4 + t, core * 8 + half * 4 + t
            ref[t * size : t * size + wf_rows, :] = wfq_ref[
                pl.ds(pl.multiple_of(at_f * wf_rows, wf_rows), wf_rows), :
            ].astype(ref.dtype)
            ref[t * size + wf_rows : (t + 1) * size, :] = wbq_ref[
                pl.ds(pl.multiple_of(at_b * wb_rows, wb_rows), wb_rows), :
            ].astype(ref.dtype)
    note = jnp.full((PAD, width), sums, F32)
    keep_ref[4 * size :, :] = note
    send_ref[4 * size :, :] = coded_note(note)


def coded_note(note):
    line = lax.broadcasted_iota(jnp.int32, note.shape, 0)
    high = note.astype(BF)
    middle, low = halves(note - high.astype(F32))
    return jnp.where(
        line == 0,
        high.astype(F32),
        jnp.where(line == 1, middle.astype(F32), jnp.where(line == 2, low.astype(F32), 0.0)),
    ).astype(BF)


def read_note(coded):
    return coded[0:1, :] + coded[1:2, :] + coded[2:3, :]


def cross_kernel(place_ref, keep_ref, got_ref, own_ref, *sends):
    mine = place_ref[0]
    size = own_ref.shape[0] - PAD
    note = keep_ref[4 * size : 4 * size + 1, :] + read_note(got_ref[4 * size :, :].astype(F32))
    note = jnp.broadcast_to(note, (PAD, note.shape[1]))

    def block(t):
        rows = pl.ds(pl.multiple_of(t * size, PAD), size)
        return keep_ref[rows, :] + got_ref[rows, :].astype(F32)

    own_ref[:size, :] = block(mine)
    own_ref[size:, :] = note
    coded = coded_note(note)
    for ref, (_, turn) in zip(sends, LINE):
        ref[:size, :] = block(mine ^ turn).astype(BF)
        ref[size:, :] = coded


def add_kernel(keep_ref, *refs):
    sum_ref, note_ref = refs[3:]
    size, width = sum_ref.shape
    total = keep_ref[:size, :]
    note = keep_ref[size : size + 1, :1]
    for ref in refs[:3]:
        total = total + ref[:size, :].astype(F32)
        note = note + read_note(ref[size:, :].astype(F32))[:, :1]
    sum_ref[...] = total.astype(sum_ref.dtype)
    note_ref[...] = note * (1.0 / width)


def assemble_kernel(place_ref, *refs, wf_rows, wb_rows, factor_f, factor_b):
    place = place_ref[0]
    wf_ref, wb_ref = refs[4:]
    for offset, ref in zip((0, 4, 8, 12), refs):
        for e, turn in enumerate((0,) + tuple(turn for _, turn in LINE)):
            to = place ^ (offset + turn)
            wf_ref[pl.ds(pl.multiple_of(to * wf_rows, wf_rows), wf_rows), :] = (
                ref[e, :wf_rows, :].astype(F32) * factor_f
            )
            wb_ref[pl.ds(pl.multiple_of(to * wb_rows, wb_rows), wb_rows), :] = (
                ref[e, wf_rows:, :].astype(F32) * factor_b
            )


def assemble_kernel(place_ref, *refs, wf_rows, wb_rows, factor_f, factor_b):
    place = place_ref[0]
    wf_ref, wb_ref = refs[2:]
    for offset, ref in zip((0, 8), refs):
        for e, turn in enumerate(TURNS):
            to = place ^ (offset + turn)
            wf_ref[pl.ds(pl.multiple_of(to * wf_rows, wf_rows), wf_rows), :] = (
                ref[e, :wf_rows, :].astype(F32) * factor_f
            )
            wb_ref[pl.ds(pl.multiple_of(to * wb_rows, wb_rows), wb_rows), :] = (
                ref[e, wf_rows:, :].astype(F32) * factor_b
            )


SMEM = pl.BlockSpec(memory_space=pltpu.SMEM)
VMEM = pl.BlockSpec(memory_space=pltpu.VMEM)
HBM = pl.BlockSpec(memory_space=pltpu.HBM)


def body(hidden_f, hidden_t, hidden_b, w_f, w_t, w_b, latents, latent_ids, positives):
    rows, high = hidden_f.shape
    wide = hidden_b.shape[1]
    width = w_f.shape[1]
    size = lax.axis_size("fa")
    bits = size.bit_length() - 1
    beyond = [1 << k for k in range(4, bits)]
    me = lax.axis_index("fa")
    total = size * rows
    assert bits >= 4 and size == 1 << bits and high // 4 == width == wide

    core = (me & 1).astype(jnp.int32)
    near, cut, head, wb_copy = pl.pallas_call(
        feature_kernel,
        in_specs=[SMEM] + [HBM] * 9,
        out_specs=[VMEM] * 4,
        out_shape=[
            jax.ShapeDtypeStruct(((FEAT_AT + 2) * rows + PAD, width), BF),
            jax.ShapeDtypeStruct((2 * rows, width), BF),
            jax.ShapeDtypeStruct(hidden_b.shape, BF),
            jax.ShapeDtypeStruct(w_b.shape, BF),
        ],
        scratch_shapes=[
            pltpu.VMEM(hidden_f.shape, BF),
            pltpu.VMEM(hidden_t.shape, BF),
            pltpu.VMEM(w_f.shape, BF),
            pltpu.VMEM(w_t.shape, BF),
            pltpu.VMEM(latents.shape, BF),
            pltpu.VMEM((1, rows), jnp.int32),
            pltpu.VMEM((1, rows), jnp.int32),
            pltpu.SemaphoreType.DMA((9,)),
        ],
        compiler_params=pltpu.CompilerParams(vmem_limit_bytes=60 * 2**20),
    )(
        core.reshape(1),
        hidden_f,
        hidden_t,
        hidden_b,
        w_f,
        w_t,
        w_b,
        latents,
        latent_ids.reshape(1, rows),
        positives.reshape(1, rows),
    )
    for mask in reversed(beyond):
        head = jnp.concatenate([head, swap(head, mask, size)], axis=0)
    pieces = [head] + [swap(head, mask, size) for mask, _ in LINE]
    pieces = pieces + [swap(piece, 2, size) for piece in pieces]
    tail0 = jnp.concatenate([head[rows:]] * (len(beyond) > 0) + pieces[1:], axis=0)
    near1 = swap(near, 1, size)
    tail1 = swap(tail0, 1, size)

    inner = reverse_bits(jnp.arange(size // 16, dtype=jnp.int32), bits - 4) << 4
    along = (0,) + tuple(mask for mask, _ in LINE)
    bases = jnp.concatenate(
        [(me ^ m ^ y ^ z ^ inner) * rows for m in GROUP for y in (0, 2) for z in along]
    ).astype(jnp.int32)
    place = reverse_bits(me & 15, 4).astype(jnp.int32)
    places = jnp.stack([core, (place >> 2) & 1])
    wf_rows, wb_rows = high // 16, wide // 16
    each = wf_rows + wb_rows
    keep, send = pl.pallas_call(
        functools.partial(pair_kernel, rows=rows, total=total),
        in_specs=[SMEM] * 2 + [VMEM] * 6,
        out_specs=[VMEM] * 2,
        out_shape=[
            jax.ShapeDtypeStruct((4 * each + PAD, width), F32),
            jax.ShapeDtypeStruct((4 * each + PAD, width), BF),
        ],
        scratch_shapes=[
            pltpu.VMEM((total, width), F32),
            pltpu.VMEM((total, width), BF),
            pltpu.VMEM((width, width), F32),
            pltpu.VMEM((2 * rows, wide), F32),
            pltpu.VMEM((2 * width, width), F32),
            pltpu.VMEM((wide, width), F32),
        ],
        compiler_params=pltpu.CompilerParams(vmem_limit_bytes=12 * 2**20 + total * width * 8),
    )(bases, places, near, near1, tail0, tail1, cut, wb_copy)
    keep, *sends = pl.pallas_call(
        cross_kernel,
        in_specs=[SMEM] + [VMEM] * 2,
        out_specs=[VMEM] * 4,
        out_shape=[jax.ShapeDtypeStruct((each + PAD, width), F32)]
        + [jax.ShapeDtypeStruct((each + PAD, width), BF)] * 3,
        compiler_params=pltpu.CompilerParams(vmem_limit_bytes=8 * 2**20),
    )((place & 3).reshape(1), keep, swap(send, 2, size))

    got = [swap(part, mask, size) for part, (mask, _) in zip(sends, LINE)]
    result, note = pl.pallas_call(
        add_kernel,
        in_specs=[VMEM] * 4,
        out_specs=[VMEM] * 2,
        out_shape=[
            jax.ShapeDtypeStruct((each, width), F32 if beyond else BF),
            jax.ShapeDtypeStruct((1, 1), F32),
        ],
        compiler_params=pltpu.CompilerParams(vmem_limit_bytes=8 * 2**20),
    )(keep, *got)
    for mask in beyond:
        result = result + swap(result, mask, size)
        note = note + swap(note, mask, size)
    result = result.astype(BF).reshape(1, each, width)
    pieces = [result] + [swap(result, mask, size) for mask, _ in LINE]
    near = jnp.concatenate(pieces + [swap(piece, 2, size) for piece in pieces], axis=0)
    far = swap(near, 1, size)
    grad_wf, grad_wb = pl.pallas_call(
        functools.partial(
            assemble_kernel,
            wf_rows=wf_rows,
            wb_rows=wb_rows,
            factor_f=math.sqrt(high),
            factor_b=math.sqrt(wide),
        ),
        in_specs=[SMEM] + [VMEM] * 2,
        out_specs=[VMEM] * 2,
        out_shape=[
            jax.ShapeDtypeStruct((high, width), F32),
            jax.ShapeDtypeStruct((wide, width), F32),
        ],
        compiler_params=pltpu.CompilerParams(vmem_limit_bytes=16 * 2**20),
    )(place.reshape(1), near, far)
    return (grad_wf, grad_wb, note.reshape(1))


def solution(mesh):
    placed = (
        P(("grp", "fa"), None),
        P(("grp", "fa"), None),
        P(("grp", "fa"), None),
        P(),
        P(),
        P(),
        P("grp", None),
        P(("grp", "fa")),
        P(("grp", "fa")),
    )
    return jax.shard_map(
        body,
        mesh=mesh,
        in_specs=placed,
        out_specs=(P("grp", None), P("grp", None), P("grp")),
        check_vma=False,
    )
```

```python
import functools
import math

import jax
import jax.numpy as jnp
from jax import lax
from jax.experimental import pallas as pl
from jax.experimental.pallas import tpu as pltpu
from jax.sharding import PartitionSpec as P

GAMMA = 0.98
LAMBDA = 1.0
EPS = 1e-06
BF = jnp.bfloat16
F32 = jnp.float32
GROUP = (0, 2, 1, 3)
PAD = 16
LINE = ((12, 3), (8, 1), (4, 2))
TURNS = (0, 3, 1, 2, 4, 7, 5, 6)


def dot(left, right):
    return jnp.dot(left, right, preferred_element_type=F32)


def dot_t(left, right):
    return lax.dot_general(left, right, (((0,), (0,)), ((), ())), preferred_element_type=F32)


def halves(array):
    high = array.astype(BF)
    return high, (array - high.astype(F32)).astype(BF)


def swap(array, mask, size):
    return lax.ppermute(array, "fa", [(i, i ^ mask) for i in range(size)])


def reverse_bits(value, bits):
    out = value * 0
    for k in range(bits):
        out = out + (((value >> k) & 1) << (bits - 1 - k))
    return out


def columns_of(row, rows):
    return jnp.transpose(jnp.broadcast_to(row, (rows, rows)))


def message_kernel(me_ref, hf_hbm, hb_hbm, wb_hbm, far_ref, near_ref, cut_ref, wb_ref, sems):
    rows, width = cut_ref.shape
    me = me_ref[0]

    def columns(mask):
        other = me ^ mask
        quarter = (other & 1) * 2 + ((other >> 1) & 1)
        return hf_hbm.at[:, pl.ds(pl.multiple_of(quarter * width, width), width)]

    moves = [
        pltpu.make_async_copy(source, target, sems.at[k])
        for k, (source, target) in enumerate(
            (
                (columns(2), far_ref.at[:rows, :]),
                (columns(3), far_ref.at[rows : 2 * rows, :]),
                (hb_hbm, far_ref.at[2 * rows :, :]),
                (columns(1), near_ref.at[:rows, :]),
                (hb_hbm, near_ref.at[rows:, :]),
                (columns(0), cut_ref),
                (wb_hbm, wb_ref),
            )
        )
    ]
    for move in moves:
        move.start()
    for move in moves:
        move.wait()


def feature_kernel(
    hf_hbm,
    ht_hbm,
    wf_hbm,
    wt_hbm,
    lat_hbm,
    ids_hbm,
    pos_hbm,
    out_ref,
    hf,
    ht,
    wf,
    wt,
    lat,
    ids,
    pos,
    sems,
):
    rows = hf.shape[0]
    width = wf.shape[1]
    moves = [
        pltpu.make_async_copy(source, target, sems.at[k])
        for k, (source, target) in enumerate(
            (
                (ids_hbm, ids),
                (pos_hbm, pos),
                (lat_hbm, lat),
                (hf_hbm, hf),
                (wf_hbm, wf),
                (ht_hbm, ht),
                (wt_hbm, wt),
            )
        )
    ]
    for move in moves:
        move.start()
    for move in moves[:3]:
        move.wait()
    who = columns_of(ids[...].astype(F32), rows)
    lanes = lax.broadcasted_iota(jnp.int32, (rows, rows), 1).astype(F32)
    tiles = [
        jnp.where(who == lanes + float(t * rows), 1.0, 0.0).astype(BF) for t in range(lat.shape[0] // rows)
    ]
    zrows = dot(jnp.concatenate(tiles, axis=1), lat[...])
    place = pos[...]
    line = lax.broadcasted_iota(jnp.int32, (PAD, rows), 0)
    high = jnp.broadcast_to(lax.shift_right_logical(place, 7).astype(F32), (PAD, rows))
    low = jnp.broadcast_to((place & 127).astype(F32), (PAD, rows))
    coded = jnp.where(line == 0, high, jnp.where(line == 1, low, 0.0)).astype(BF)
    coded = jnp.concatenate([coded] + [jnp.zeros((PAD, width - rows), BF)] * (width > rows), axis=1)

    out_ref[2 * rows :, :] = coded
    moves[3].wait()
    moves[4].wait()
    out_ref[:rows, :] = (dot(hf[...], wf[...]) + zrows).astype(BF)
    moves[5].wait()
    moves[6].wait()
    out_ref[rows : 2 * rows, :] = (dot(ht[...], wt[...]) + zrows).astype(BF)


def pack_kernel(near_ref, feats_ref, piece_ref, over_y_ref, to_core_ref):
    end = feats_ref.shape[0]
    over_y_ref[:end, :] = feats_ref[...]
    over_y_ref[end:, :] = piece_ref[...]
    at = 0
    for ref in (near_ref, feats_ref):
        to_core_ref[at : at + ref.shape[0], :] = ref[...]
        at = at + ref.shape[0]


def pair_kernel(*refs, rows, total):
    base_ref, place_ref = refs[:2]
    near_ref, far_ref, core_ref, far3_ref, feats_ref = refs[2:7]
    second_refs, rest_refs = refs[7:9], refs[9:11]
    cut_ref, wb_ref, keep_ref, sends = refs[11], refs[12], refs[13], refs[14:17]
    raw_ref, back_ref, smat_ref, pick_ref, wfq_ref, wbq_ref = refs[17:]
    width = wb_ref.shape[1]
    pairs = float(total * (total - 1))
    groups = total // (4 * rows)
    span = total // 16
    wb = wb_ref[...]
    end = 2 * rows + PAD
    feats = ((feats_ref, 0), (second_refs[0], 0), (core_ref, 2 * rows), (second_refs[1], 0))
    cuts = ((cut_ref, 0), (far_ref, 0), (core_ref, 0), (far3_ref, rows))
    segments = []
    for own, far, second, rest in (
        (near_ref, far_ref, second_refs[0], rest_refs[0]),
        (core_ref, far3_ref, second_refs[1], rest_refs[1]),
    ):
        segments += [
            (own, rows, rows),
            (rest, 0, 4 * span - rows),
            (far, 2 * rows, rows),
            (second, end, span),
            (rest, 4 * span - rows, 3 * span - rows),
        ]
    wanted = []
    for ref, start in feats:
        code = ref[start + 2 * rows : start + end, :rows].astype(F32)
        wanted.append(columns_of(code[0:1] * 128.0 + code[1:2], rows))
    lanes = lax.broadcasted_iota(jnp.int32, (rows, rows), 1)

    def embed(hidden):
        raw = dot(hidden, wb)
        scale = lax.rsqrt(jnp.mean(raw * raw, axis=-1, keepdims=True) + EPS)
        return raw, scale, (raw * scale).astype(BF)

    def through(grad, raw, scale):
        along = jnp.sum(grad * raw, axis=-1, keepdims=True)
        return (scale * grad - scale * scale * scale * (1.0 / width) * along * raw).astype(BF)

    def over_rows(step):
        first = 0
        for ref, start, length in segments:
            if length <= 4 * rows:
                step(ref, start, first, length)
            else:

                def one(i, carry, ref=ref, start=start, first=first):
                    step(ref, start + i * rows, first + i * rows, rows)
                    return carry

                lax.fori_loop(0, length // rows, one, 0)
            first = first + length

    def at(start, chunk):
        return pl.ds(pl.multiple_of(start, PAD), chunk)

    smat_ref[...] = jnp.zeros_like(smat_ref)
    pick_ref[...] = jnp.zeros_like(pick_ref)
    wbq_ref[...] = jnp.zeros_like(wbq_ref)

    def first(ref, start, number, chunk):
        hidden = ref[at(start, chunk), :]
        raw, _, back = embed(hidden)
        raw_ref[at(number, chunk), :] = raw
        back_ref[at(number, chunk), :] = back
        smat_ref[...] += dot_t(back, back)
        ids = [(lanes + base_ref[number // rows + t]).astype(F32) for t in range(chunk // rows)]
        mask = jnp.concatenate(
            [
                jnp.concatenate([jnp.where(want == i, 1.0, 0.0).astype(BF) for i in ids], axis=1)
                for want in wanted
            ],
            axis=0,
        )
        pick_ref[...] += dot(mask, hidden)

    over_rows(first)
    smat = smat_ref[...]
    s_hi, s_lo = halves(smat)
    kmat = jnp.zeros((width, width), F32)
    wfq = jnp.zeros((cut_ref.shape[1], width), F32)
    sums = jnp.sum(smat * smat) / groups / (2.0 * pairs)
    for g, (ref, start) in enumerate(feats):
        feat = ref[start : start + rows, :]
        f32feat = feat.astype(F32)
        diff = f32feat - GAMMA * ref[start + rows : start + 2 * rows, :].astype(F32)
        d_hi, d_lo = halves(diff)
        hidden = pick_ref[g * rows : (g + 1) * rows, :].astype(BF)
        raw, scale, back = embed(hidden)
        ob = back.astype(F32)
        ds = dot(d_hi, s_hi) + dot(d_lo, s_hi) + dot(d_hi, s_lo)
        db = jnp.sum(diff * ob, axis=-1, keepdims=True)
        coef = db * (1.0 / pairs) + 1.0 / total
        norm = jnp.sum(ob * ob, axis=-1, keepdims=True)
        grad_f = (ds * (1.0 / pairs) - coef * ob).astype(BF)
        cut = cuts[g][0][cuts[g][1] : cuts[g][1] + rows, :]
        wfq = wfq + dot_t(cut, grad_f)
        kmat = kmat + dot_t(d_hi, feat) + dot_t(d_lo, feat)
        sums = sums + (
            (jnp.sum(diff * ds) - jnp.sum(db * db) - LAMBDA * jnp.sum(norm * norm)) / (2.0 * pairs)
            - (jnp.sum(f32feat * ob) + LAMBDA * jnp.sum(norm)) / total
        )
        grad_own = through(
            -coef * f32feat - (norm * (2.0 * LAMBDA / pairs) + 2.0 * LAMBDA / total) * ob, raw, scale
        )
        wbq_ref[...] += dot_t(hidden, grad_own)
    wfq_ref[...] = wfq
    a_hi, a_lo = halves((kmat + (2.0 * LAMBDA / groups) * smat) * (1.0 / pairs))

    def second(ref, start, number, chunk):
        raw = raw_ref[at(number, chunk), :]
        scale = lax.rsqrt(jnp.mean(raw * raw, axis=-1, keepdims=True) + EPS)
        back = back_ref[at(number, chunk), :]
        grad = through(dot(back, a_hi) + dot(back, a_lo), raw, scale)
        wbq_ref[...] += dot_t(ref[at(start, chunk), :], grad)

    over_rows(second)
    quarter, mine = place_ref[0], place_ref[1]
    wf_rows = wfq_ref.shape[0] // 4
    wb_rows = wbq_ref.shape[0] // 16
    size = wf_rows + wb_rows

    def block(t):
        return (
            wfq_ref[pl.ds(pl.multiple_of(t * wf_rows, wf_rows), wf_rows), :],
            wbq_ref[pl.ds(pl.multiple_of((quarter * 4 + t) * wb_rows, wb_rows), wb_rows), :],
        )

    keep_ref[:wf_rows, :], keep_ref[wf_rows:size, :] = block(mine)
    note = jnp.full((PAD, width), sums, F32)
    keep_ref[size:, :] = note
    line = lax.broadcasted_iota(jnp.int32, (PAD, width), 0)
    n_hi = note.astype(BF)
    n_mid, n_lo = halves(note - n_hi.astype(F32))
    coded = jnp.where(
        line == 0,
        n_hi.astype(F32),
        jnp.where(line == 1, n_mid.astype(F32), jnp.where(line == 2, n_lo.astype(F32), 0.0)),
    ).astype(BF)
    for ref, (_, turn) in zip(sends, LINE):
        part_f, part_b = block(mine ^ turn)
        ref[:wf_rows, :] = part_f.astype(BF)
        ref[wf_rows:size, :] = part_b.astype(BF)
        ref[size:, :] = coded


def add_kernel(keep_ref, *refs):
    sum_ref, note_ref = refs[3:]
    size, width = sum_ref.shape
    total = keep_ref[:size, :]
    note = keep_ref[size : size + 1, :1]
    for ref in refs[:3]:
        total = total + ref[:size, :].astype(F32)
        coded = ref[size:, :].astype(F32)
        note = note + (coded[0:1, :1] + coded[1:2, :1] + coded[2:3, :1])
    sum_ref[...] = total.astype(sum_ref.dtype)
    note_ref[...] = note * (1.0 / width)


def assemble_kernel(place_ref, *refs, wf_rows, wb_rows, factor_f, factor_b):
    place = place_ref[0]
    wf_ref, wb_ref = refs[4:]
    for offset, ref in zip((0, 4, 8, 12), refs):
        for e, turn in enumerate((0,) + tuple(turn for _, turn in LINE)):
            to = place ^ (offset + turn)
            wf_ref[pl.ds(pl.multiple_of(to * wf_rows, wf_rows), wf_rows), :] = (
                ref[e, :wf_rows, :].astype(F32) * factor_f
            )
            wb_ref[pl.ds(pl.multiple_of(to * wb_rows, wb_rows), wb_rows), :] = (
                ref[e, wf_rows:, :].astype(F32) * factor_b
            )


def assemble_kernel(place_ref, *refs, wf_rows, wb_rows, factor_f, factor_b):
    place = place_ref[0]
    wf_ref, wb_ref = refs[2:]
    for offset, ref in zip((0, 8), refs):
        for e, turn in enumerate(TURNS):
            to = place ^ (offset + turn)
            wf_ref[pl.ds(pl.multiple_of(to * wf_rows, wf_rows), wf_rows), :] = (
                ref[e, :wf_rows, :].astype(F32) * factor_f
            )
            wb_ref[pl.ds(pl.multiple_of(to * wb_rows, wb_rows), wb_rows), :] = (
                ref[e, wf_rows:, :].astype(F32) * factor_b
            )


SMEM = pl.BlockSpec(memory_space=pltpu.SMEM)
VMEM = pl.BlockSpec(memory_space=pltpu.VMEM)
HBM = pl.BlockSpec(memory_space=pltpu.HBM)


def body(hidden_f, hidden_t, hidden_b, w_f, w_t, w_b, latents, latent_ids, positives):
    rows, high = hidden_f.shape
    wide = hidden_b.shape[1]
    width = w_f.shape[1]
    size = lax.axis_size("fa")
    bits = size.bit_length() - 1
    beyond = [1 << k for k in range(4, bits)]
    me = lax.axis_index("fa")
    total = size * rows
    assert bits >= 4 and size == 1 << bits and high // 4 == width == wide

    head = hidden_b
    for mask in reversed(beyond):
        head = jnp.concatenate([head, swap(head, mask, size)], axis=0)
    piece12, piece8, piece4 = [swap(head, mask, size) for mask, _ in LINE]
    far, near, cut, wb_copy = pl.pallas_call(
        message_kernel,
        in_specs=[SMEM] + [HBM] * 3,
        out_specs=[VMEM] * 4,
        out_shape=[
            jax.ShapeDtypeStruct((3 * rows, width), BF),
            jax.ShapeDtypeStruct((2 * rows, width), BF),
            jax.ShapeDtypeStruct((rows, width), BF),
            jax.ShapeDtypeStruct(w_b.shape, BF),
        ],
        scratch_shapes=[pltpu.SemaphoreType.DMA((7,))],
        compiler_params=pltpu.CompilerParams(vmem_limit_bytes=60 * 2**20),
    )(me.astype(jnp.int32).reshape(1), hidden_f, hidden_b, w_b)
    feats0 = pl.pallas_call(
        feature_kernel,
        in_specs=[HBM] * 7,
        out_specs=VMEM,
        out_shape=jax.ShapeDtypeStruct((2 * rows + PAD, width), BF),
        scratch_shapes=[
            pltpu.VMEM(hidden_f.shape, BF),
            pltpu.VMEM(hidden_t.shape, BF),
            pltpu.VMEM(w_f.shape, BF),
            pltpu.VMEM(w_t.shape, BF),
            pltpu.VMEM(latents.shape, BF),
            pltpu.VMEM((1, rows), jnp.int32),
            pltpu.VMEM((1, rows), jnp.int32),
            pltpu.SemaphoreType.DMA((7,)),
        ],
        compiler_params=pltpu.CompilerParams(vmem_limit_bytes=60 * 2**20),
        cost_estimate=pl.CostEstimate(
            flops=4 * rows * high * width, bytes_accessed=4 * high * (rows + width), transcendentals=0
        ),
    )(
        hidden_f,
        hidden_t,
        w_f,
        w_t,
        latents,
        latent_ids.reshape(1, rows),
        positives.reshape(1, rows),
    )
    far2 = swap(far, 2, size)
    second, to_core = pl.pallas_call(
        pack_kernel,
        in_specs=[VMEM] * 3,
        out_specs=[VMEM] * 2,
        out_shape=[
            jax.ShapeDtypeStruct((feats0.shape[0] + piece4.shape[0], width), BF),
            jax.ShapeDtypeStruct((2 * rows + feats0.shape[0], width), BF),
        ],
        compiler_params=pltpu.CompilerParams(vmem_limit_bytes=16 * 2**20),
    )(near, feats0, piece4)
    second2 = swap(second, 2, size)
    over_y = [swap(piece, 2, size) for piece in (piece8, piece12)]
    more = [head[rows:]] * (len(beyond) > 0)
    rest0 = jnp.concatenate(
        [piece4, piece8, piece12] + more + over_y + [swap(piece, 2, size) for piece in more], axis=0
    )
    from_core = swap(to_core, 1, size)
    far3 = swap(far2, 1, size)
    second3 = swap(second2, 1, size)
    rest1 = swap(rest0, 1, size)

    inner = reverse_bits(jnp.arange(size // 16, dtype=jnp.int32), bits - 4) << 4
    first, others = inner[:1], inner[1:]
    bases = []
    for core in (0, 1):
        bases += [core ^ first] + [core ^ mask ^ inner for mask in (4, 8, 12)] + [core ^ others]
        core = core ^ 2
        bases += [core ^ first] + [core ^ mask ^ inner for mask in (4, 8, 12)] + [core ^ others]
    bases = ((me ^ jnp.concatenate(bases)) * rows).astype(jnp.int32)
    place = reverse_bits(me & 15, 4).astype(jnp.int32)
    places = jnp.stack([place >> 2, place & 3])
    wf_rows, wb_rows = high // 16, wide // 16
    each = wf_rows + wb_rows
    keep, *sends = pl.pallas_call(
        functools.partial(pair_kernel, rows=rows, total=total),
        in_specs=[SMEM] * 2 + [VMEM] * 11,
        out_specs=[VMEM] * 4,
        out_shape=[jax.ShapeDtypeStruct((each + PAD, width), F32)]
        + [jax.ShapeDtypeStruct((each + PAD, width), BF)] * 3,
        scratch_shapes=[
            pltpu.VMEM((total, width), F32),
            pltpu.VMEM((total, width), BF),
            pltpu.VMEM((width, width), F32),
            pltpu.VMEM((4 * rows, wide), F32),
            pltpu.VMEM((width, width), F32),
            pltpu.VMEM((wide, width), F32),
        ],
        compiler_params=pltpu.CompilerParams(vmem_limit_bytes=12 * 2**20 + total * width * 8),
    )(bases, places, near, far2, from_core, far3, feats0, second2, second3, rest0, rest1, cut, wb_copy)

    got = [swap(part, mask, size) for part, (mask, _) in zip(sends, LINE)]
    result, note = pl.pallas_call(
        add_kernel,
        in_specs=[VMEM] * 4,
        out_specs=[VMEM] * 2,
        out_shape=[
            jax.ShapeDtypeStruct((each, width), F32 if beyond else BF),
            jax.ShapeDtypeStruct((1, 1), F32),
        ],
        compiler_params=pltpu.CompilerParams(vmem_limit_bytes=8 * 2**20),
    )(keep, *got)
    for mask in beyond:
        result = result + swap(result, mask, size)
        note = note + swap(note, mask, size)
    result = result.astype(BF).reshape(1, each, width)
    pieces = [result] + [swap(result, mask, size) for mask, _ in LINE]
    near = jnp.concatenate(pieces + [swap(piece, 2, size) for piece in pieces], axis=0)
    far = swap(near, 1, size)
    grad_wf, grad_wb = pl.pallas_call(
        functools.partial(
            assemble_kernel,
            wf_rows=wf_rows,
            wb_rows=wb_rows,
            factor_f=math.sqrt(high),
            factor_b=math.sqrt(wide),
        ),
        in_specs=[SMEM] + [VMEM] * 2,
        out_specs=[VMEM] * 2,
        out_shape=[
            jax.ShapeDtypeStruct((high, width), F32),
            jax.ShapeDtypeStruct((wide, width), F32),
        ],
        compiler_params=pltpu.CompilerParams(vmem_limit_bytes=16 * 2**20),
    )(place.reshape(1), near, far)
    return (grad_wf, grad_wb, note.reshape(1))


def solution(mesh):
    placed = (
        P(("grp", "fa"), None),
        P(("grp", "fa"), None),
        P(("grp", "fa"), None),
        P(),
        P(),
        P(),
        P("grp", None),
        P(("grp", "fa")),
        P(("grp", "fa")),
    )
    return jax.shard_map(
        body,
        mesh=mesh,
        in_specs=placed,
        out_specs=(P("grp", None), P("grp", None), P("grp")),
        check_vma=False,
    )
```

```python
import functools
import math

import jax
import jax.numpy as jnp
from jax import lax
from jax.experimental import pallas as pl
from jax.experimental.pallas import tpu as pltpu
from jax.sharding import PartitionSpec as P

GAMMA = 0.98
LAMBDA = 1.0
EPS = 1e-06
BF = jnp.bfloat16
F32 = jnp.float32
GROUP = (0, 2, 1, 3)
PAD = 16
LINE = ((12, 3), (8, 1), (4, 2))
TURNS = (0, 3, 1, 2, 4, 7, 5, 6)


def dot(left, right):
    return jnp.dot(left, right, preferred_element_type=F32)


def dot_t(left, right):
    return lax.dot_general(left, right, (((0,), (0,)), ((), ())), preferred_element_type=F32)


def halves(array):
    high = array.astype(BF)
    return high, (array - high.astype(F32)).astype(BF)


def swap(array, mask, size):
    return lax.ppermute(array, "fa", [(i, i ^ mask) for i in range(size)])


def reverse_bits(value, bits):
    out = value * 0
    for k in range(bits):
        out = out + (((value >> k) & 1) << (bits - 1 - k))
    return out


def columns_of(row, rows):
    return jnp.transpose(jnp.broadcast_to(row, (rows, rows)))


def message_kernel(me_ref, hf_hbm, hb_hbm, wb_hbm, far_ref, near_ref, cut_ref, wb_ref, sems):
    rows, width = cut_ref.shape
    me = me_ref[0]

    def columns(mask):
        other = me ^ mask
        quarter = (other & 1) * 2 + ((other >> 1) & 1)
        return hf_hbm.at[:, pl.ds(pl.multiple_of(quarter * width, width), width)]

    moves = [
        pltpu.make_async_copy(source, target, sems.at[k])
        for k, (source, target) in enumerate(
            (
                (columns(2), far_ref.at[:rows, :]),
                (columns(3), far_ref.at[rows : 2 * rows, :]),
                (hb_hbm, far_ref.at[2 * rows :, :]),
                (columns(1), near_ref.at[:rows, :]),
                (hb_hbm, near_ref.at[rows:, :]),
                (columns(0), cut_ref),
                (wb_hbm, wb_ref),
            )
        )
    ]
    for move in moves:
        move.start()
    for move in moves:
        move.wait()


def feature_kernel(
    hf_hbm,
    ht_hbm,
    wf_hbm,
    wt_hbm,
    lat_hbm,
    ids_hbm,
    pos_hbm,
    out_ref,
    hf,
    ht,
    wf,
    wt,
    lat,
    ids,
    pos,
    sems,
):
    rows = hf.shape[0]
    width = wf.shape[1]
    moves = [
        pltpu.make_async_copy(source, target, sems.at[k])
        for k, (source, target) in enumerate(
            (
                (ids_hbm, ids),
                (pos_hbm, pos),
                (lat_hbm, lat),
                (hf_hbm, hf),
                (wf_hbm, wf),
                (ht_hbm, ht),
                (wt_hbm, wt),
            )
        )
    ]
    for move in moves:
        move.start()
    for move in moves[:3]:
        move.wait()
    who = columns_of(ids[...].astype(F32), rows)
    lanes = lax.broadcasted_iota(jnp.int32, (rows, rows), 1).astype(F32)
    tiles = [
        jnp.where(who == lanes + float(t * rows), 1.0, 0.0).astype(BF) for t in range(lat.shape[0] // rows)
    ]
    zrows = dot(jnp.concatenate(tiles, axis=1), lat[...])
    place = pos[...]
    line = lax.broadcasted_iota(jnp.int32, (PAD, rows), 0)
    high = jnp.broadcast_to(lax.shift_right_logical(place, 7).astype(F32), (PAD, rows))
    low = jnp.broadcast_to((place & 127).astype(F32), (PAD, rows))
    coded = jnp.where(line == 0, high, jnp.where(line == 1, low, 0.0)).astype(BF)
    coded = jnp.concatenate([coded] + [jnp.zeros((PAD, width - rows), BF)] * (width > rows), axis=1)

    out_ref[2 * rows :, :] = coded
    moves[3].wait()
    moves[4].wait()
    out_ref[:rows, :] = (dot(hf[...], wf[...]) + zrows).astype(BF)
    moves[5].wait()
    moves[6].wait()
    out_ref[rows : 2 * rows, :] = (dot(ht[...], wt[...]) + zrows).astype(BF)


def pack_kernel(near_ref, feats_ref, piece_ref, over_y_ref, to_core_ref):
    end = feats_ref.shape[0]
    over_y_ref[:end, :] = feats_ref[...]
    over_y_ref[end:, :] = piece_ref[...]
    at = 0
    for ref in (near_ref, feats_ref):
        to_core_ref[at : at + ref.shape[0], :] = ref[...]
        at = at + ref.shape[0]


def pair_kernel(*refs, rows, total):
    base_ref, place_ref = refs[:2]
    near_ref, far_ref, core_ref, far3_ref, feats_ref = refs[2:7]
    second_refs, rest_refs = refs[7:9], refs[9:11]
    cut_ref, wb_ref, keep_ref, sends = refs[11], refs[12], refs[13], refs[14:17]
    hid_ref, raw_ref, back_ref, mask_ref, smat_ref, pick_ref, own_ref, wfq_ref, wbq_ref = refs[17:]
    width = wb_ref.shape[1]
    pairs = float(total * (total - 1))
    groups = total // (4 * rows)
    span = total // 16
    wb = wb_ref[...]
    end = 2 * rows + PAD
    feats = ((feats_ref, 0), (second_refs[0], 0), (core_ref, 2 * rows), (second_refs[1], 0))
    cuts = ((cut_ref, 0), (far_ref, 0), (core_ref, 0), (far3_ref, rows))
    segments = []
    for own, far, second, rest in (
        (near_ref, far_ref, second_refs[0], rest_refs[0]),
        (core_ref, far3_ref, second_refs[1], rest_refs[1]),
    ):
        segments += [
            (own, rows, rows),
            (rest, 0, 4 * span - rows),
            (far, 2 * rows, rows),
            (second, end, span),
            (rest, 4 * span - rows, 3 * span - rows),
        ]
    first = 0
    for ref, start, length in segments:
        if length <= 4 * rows:
            hid_ref[first : first + length, :] = ref[start : start + length, :]
        else:

            def one(i, carry, ref=ref, start=start, first=first):
                hid_ref[pl.ds(pl.multiple_of(first + i * rows, PAD), rows), :] = ref[
                    pl.ds(pl.multiple_of(start + i * rows, PAD), rows), :
                ]
                return carry

            lax.fori_loop(0, length // rows, one, 0)
        first = first + length

    def embed(hidden):
        raw = dot(hidden, wb)
        scale = lax.rsqrt(jnp.mean(raw * raw, axis=-1, keepdims=True) + EPS)
        return raw, scale, (raw * scale).astype(BF)

    def through(grad, raw, scale):
        along = jnp.sum(grad * raw, axis=-1, keepdims=True)
        return (scale * grad - scale * scale * scale * (1.0 / width) * along * raw).astype(BF)

    big, small = mask_ref.shape[1], 4 * rows

    def over_rows(step):
        if big == total:
            step(0)
        else:
            lax.fori_loop(0, total // big, lambda i, carry: (step(i), carry)[1], 0)

    def at(start, length):
        return pl.ds(pl.multiple_of(start, rows), length)

    wanted = []
    for ref, start in feats:
        code = ref[start + 2 * rows : start + end, :rows].astype(F32)
        wanted.append(columns_of(code[0:1] * 128.0 + code[1:2], rows))
    lanes = lax.broadcasted_iota(jnp.int32, (rows, rows), 1)
    smat_ref[...] = jnp.zeros_like(smat_ref)
    pick_ref[...] = jnp.zeros_like(pick_ref)

    def first_pass(step):
        for i in range(big // small):
            here = at(step * big + i * small, small)
            raw, _, back = embed(hid_ref[here, :])
            raw_ref[here, :] = raw
            back_ref[here, :] = back
        for t in range(big // rows):
            ids = (lanes + base_ref[step * (big // rows) + t]).astype(F32)
            for g, want in enumerate(wanted):
                mask_ref[g * rows : (g + 1) * rows, t * rows : (t + 1) * rows] = jnp.where(
                    want == ids, 1.0, 0.0
                ).astype(BF)
        here = at(step * big, big)
        smat_ref[...] += dot_t(back_ref[here, :], back_ref[here, :])
        pick_ref[...] += dot(mask_ref[...], hid_ref[here, :])

    over_rows(first_pass)
    smat = smat_ref[...]
    s_hi, s_lo = halves(smat)
    quarter, mine = place_ref[0], place_ref[1]
    half = wbq_ref.shape[0]
    columns = pl.ds(pl.multiple_of((quarter >> 1) * half, half), half)

    def rows_of(places, offset):
        return jnp.concatenate([ref[at + offset : at + offset + rows, :] for ref, at in places], axis=0)

    feat = rows_of(feats, 0)
    f32feat = feat.astype(F32)
    diff = f32feat - GAMMA * rows_of(feats, rows).astype(F32)
    d_hi, d_lo = halves(diff)
    kmat = dot_t(d_hi, feat) + dot_t(d_lo, feat)
    hidden = pick_ref[...].astype(BF)
    own_ref[...] = hidden
    raw, scale, back = embed(hidden)
    ob = back.astype(F32)
    ds = dot(d_hi, s_hi) + dot(d_lo, s_hi) + dot(d_hi, s_lo)
    db = jnp.sum(diff * ob, axis=-1, keepdims=True)
    coef = db * (1.0 / pairs) + 1.0 / total
    norm = jnp.sum(ob * ob, axis=-1, keepdims=True)
    grad_f = (ds * (1.0 / pairs) - coef * ob).astype(BF)
    wfq_ref[...] = dot_t(rows_of(cuts, 0), grad_f)
    squares = jnp.sum(diff * ds) - jnp.sum(db * db)
    squares = squares + LAMBDA * (jnp.sum(smat * smat) / groups - jnp.sum(norm * norm))
    sums = squares / (2.0 * pairs) - (jnp.sum(f32feat * ob) + LAMBDA * jnp.sum(norm)) / total
    grad_own = through(
        -coef * f32feat - (norm * (2.0 * LAMBDA / pairs) + 2.0 * LAMBDA / total) * ob, raw, scale
    )
    wbq_ref[...] = dot_t(own_ref[:, columns], grad_own)
    a_hi, a_lo = halves((kmat + (2.0 * LAMBDA / groups) * smat) * (1.0 / pairs))

    def second_pass(step):
        for i in range(big // small):
            here = at(step * big + i * small, small)
            raw = raw_ref[here, :]
            scale = lax.rsqrt(jnp.mean(raw * raw, axis=-1, keepdims=True) + EPS)
            back = back_ref[here, :]
            back_ref[here, :] = through(dot(back, a_hi) + dot(back, a_lo), raw, scale)
        here = at(step * big, big)
        wbq_ref[...] += dot_t(hid_ref[here, columns], back_ref[here, :])

    over_rows(second_pass)
    wf_rows = wfq_ref.shape[0] // 4
    wb_rows = wbq_ref.shape[0] // 8
    size = wf_rows + wb_rows

    def block(t):
        return (
            wfq_ref[pl.ds(pl.multiple_of(t * wf_rows, wf_rows), wf_rows), :],
            wbq_ref[pl.ds(pl.multiple_of(((quarter & 1) * 4 + t) * wb_rows, wb_rows), wb_rows), :],
        )

    keep_ref[:wf_rows, :], keep_ref[wf_rows:size, :] = block(mine)
    note = jnp.full((PAD, width), sums, F32)
    keep_ref[size:, :] = note
    line = lax.broadcasted_iota(jnp.int32, (PAD, width), 0)
    n_hi = note.astype(BF)
    n_mid, n_lo = halves(note - n_hi.astype(F32))
    coded = jnp.where(
        line == 0,
        n_hi.astype(F32),
        jnp.where(line == 1, n_mid.astype(F32), jnp.where(line == 2, n_lo.astype(F32), 0.0)),
    ).astype(BF)
    for ref, (_, turn) in zip(sends, LINE):
        part_f, part_b = block(mine ^ turn)
        ref[:wf_rows, :] = part_f.astype(BF)
        ref[wf_rows:size, :] = part_b.astype(BF)
        ref[size:, :] = coded


def add_kernel(keep_ref, *refs):
    sum_ref, note_ref = refs[3:]
    size, width = sum_ref.shape
    total = keep_ref[:size, :]
    note = keep_ref[size : size + 1, :1]
    for ref in refs[:3]:
        total = total + ref[:size, :].astype(F32)
        coded = ref[size:, :].astype(F32)
        note = note + (coded[0:1, :1] + coded[1:2, :1] + coded[2:3, :1])
    sum_ref[...] = total.astype(sum_ref.dtype)
    note_ref[...] = note * (1.0 / width)


def assemble_kernel(place_ref, *refs, wf_rows, wb_rows, factor_f, factor_b):
    place = place_ref[0]
    wf_ref, wb_ref = refs[4:]
    for offset, ref in zip((0, 4, 8, 12), refs):
        for e, turn in enumerate((0,) + tuple(turn for _, turn in LINE)):
            to = place ^ (offset + turn)
            wf_ref[pl.ds(pl.multiple_of(to * wf_rows, wf_rows), wf_rows), :] = (
                ref[e, :wf_rows, :].astype(F32) * factor_f
            )
            wb_ref[pl.ds(pl.multiple_of(to * wb_rows, wb_rows), wb_rows), :] = (
                ref[e, wf_rows:, :].astype(F32) * factor_b
            )


def assemble_kernel(place_ref, *refs, wf_rows, wb_rows, factor_f, factor_b):
    place = place_ref[0]
    wf_ref, wb_ref = refs[2:]
    for offset, ref in zip((0, 8), refs):
        for e, turn in enumerate(TURNS):
            to = place ^ (offset + turn)
            wf_ref[pl.ds(pl.multiple_of(to * wf_rows, wf_rows), wf_rows), :] = (
                ref[e, :wf_rows, :].astype(F32) * factor_f
            )
            wb_ref[pl.ds(pl.multiple_of(to * wb_rows, wb_rows), wb_rows), :] = (
                ref[e, wf_rows:, :].astype(F32) * factor_b
            )


SMEM = pl.BlockSpec(memory_space=pltpu.SMEM)
VMEM = pl.BlockSpec(memory_space=pltpu.VMEM)
HBM = pl.BlockSpec(memory_space=pltpu.HBM)


def body(hidden_f, hidden_t, hidden_b, w_f, w_t, w_b, latents, latent_ids, positives):
    rows, high = hidden_f.shape
    wide = hidden_b.shape[1]
    width = w_f.shape[1]
    size = lax.axis_size("fa")
    bits = size.bit_length() - 1
    beyond = [1 << k for k in range(4, bits)]
    me = lax.axis_index("fa")
    total = size * rows
    assert bits >= 4 and size == 1 << bits and high // 4 == width == wide

    head = hidden_b
    for mask in reversed(beyond):
        head = jnp.concatenate([head, swap(head, mask, size)], axis=0)
    piece12, piece8, piece4 = [swap(head, mask, size) for mask, _ in LINE]
    far, near, cut, wb_copy = pl.pallas_call(
        message_kernel,
        in_specs=[SMEM] + [HBM] * 3,
        out_specs=[VMEM] * 4,
        out_shape=[
            jax.ShapeDtypeStruct((3 * rows, width), BF),
            jax.ShapeDtypeStruct((2 * rows, width), BF),
            jax.ShapeDtypeStruct((rows, width), BF),
            jax.ShapeDtypeStruct(w_b.shape, BF),
        ],
        scratch_shapes=[pltpu.SemaphoreType.DMA((7,))],
        compiler_params=pltpu.CompilerParams(vmem_limit_bytes=60 * 2**20),
    )(me.astype(jnp.int32).reshape(1), hidden_f, hidden_b, w_b)
    feats0 = pl.pallas_call(
        feature_kernel,
        in_specs=[HBM] * 7,
        out_specs=VMEM,
        out_shape=jax.ShapeDtypeStruct((2 * rows + PAD, width), BF),
        scratch_shapes=[
            pltpu.VMEM(hidden_f.shape, BF),
            pltpu.VMEM(hidden_t.shape, BF),
            pltpu.VMEM(w_f.shape, BF),
            pltpu.VMEM(w_t.shape, BF),
            pltpu.VMEM(latents.shape, BF),
            pltpu.VMEM((1, rows), jnp.int32),
            pltpu.VMEM((1, rows), jnp.int32),
            pltpu.SemaphoreType.DMA((7,)),
        ],
        compiler_params=pltpu.CompilerParams(vmem_limit_bytes=60 * 2**20),
        cost_estimate=pl.CostEstimate(
            flops=4 * rows * high * width, bytes_accessed=4 * high * (rows + width), transcendentals=0
        ),
    )(
        hidden_f,
        hidden_t,
        w_f,
        w_t,
        latents,
        latent_ids.reshape(1, rows),
        positives.reshape(1, rows),
    )
    far2 = swap(far, 2, size)
    second, to_core = pl.pallas_call(
        pack_kernel,
        in_specs=[VMEM] * 3,
        out_specs=[VMEM] * 2,
        out_shape=[
            jax.ShapeDtypeStruct((feats0.shape[0] + piece4.shape[0], width), BF),
            jax.ShapeDtypeStruct((2 * rows + feats0.shape[0], width), BF),
        ],
        compiler_params=pltpu.CompilerParams(vmem_limit_bytes=16 * 2**20),
    )(near, feats0, piece4)
    second2 = swap(second, 2, size)
    over_y = [swap(piece, 2, size) for piece in (piece8, piece12)]
    more = [head[rows:]] * (len(beyond) > 0)
    rest0 = jnp.concatenate(
        [piece4, piece8, piece12] + more + over_y + [swap(piece, 2, size) for piece in more], axis=0
    )
    from_core = swap(to_core, 1, size)
    far3 = swap(far2, 1, size)
    second3 = swap(second2, 1, size)
    rest1 = swap(rest0, 1, size)

    inner = reverse_bits(jnp.arange(size // 16, dtype=jnp.int32), bits - 4) << 4
    first, others = inner[:1], inner[1:]
    bases = []
    for core in (0, 1):
        bases += [core ^ first] + [core ^ mask ^ inner for mask in (4, 8, 12)] + [core ^ others]
        core = core ^ 2
        bases += [core ^ first] + [core ^ mask ^ inner for mask in (4, 8, 12)] + [core ^ others]
    bases = ((me ^ jnp.concatenate(bases)) * rows).astype(jnp.int32)
    place = reverse_bits(me & 15, 4).astype(jnp.int32)
    places = jnp.stack([place >> 2, place & 3])
    wf_rows, wb_rows = high // 16, wide // 16
    each = wf_rows + wb_rows
    keep, *sends = pl.pallas_call(
        functools.partial(pair_kernel, rows=rows, total=total),
        in_specs=[SMEM] * 2 + [VMEM] * 11,
        out_specs=[VMEM] * 4,
        out_shape=[jax.ShapeDtypeStruct((each + PAD, width), F32)]
        + [jax.ShapeDtypeStruct((each + PAD, width), BF)] * 3,
        scratch_shapes=[
            pltpu.VMEM((total, wide), BF),
            pltpu.VMEM((total, width), F32),
            pltpu.VMEM((total, width), BF),
            pltpu.VMEM((4 * rows, min(total, 16 * rows)), BF),
            pltpu.VMEM((width, width), F32),
            pltpu.VMEM((4 * rows, wide), F32),
            pltpu.VMEM((4 * rows, wide), BF),
            pltpu.VMEM((width, width), F32),
            pltpu.VMEM((wide // 2, width), F32),
        ],
        compiler_params=pltpu.CompilerParams(vmem_limit_bytes=15 * 2**20 + total * width * 10),
    )(bases, places, near, far2, from_core, far3, feats0, second2, second3, rest0, rest1, cut, wb_copy)

    got = [swap(part, mask, size) for part, (mask, _) in zip(sends, LINE)]
    result, note = pl.pallas_call(
        add_kernel,
        in_specs=[VMEM] * 4,
        out_specs=[VMEM] * 2,
        out_shape=[
            jax.ShapeDtypeStruct((each, width), F32 if beyond else BF),
            jax.ShapeDtypeStruct((1, 1), F32),
        ],
        compiler_params=pltpu.CompilerParams(vmem_limit_bytes=8 * 2**20),
    )(keep, *got)
    for mask in beyond:
        result = result + swap(result, mask, size)
        note = note + swap(note, mask, size)
    result = result.astype(BF).reshape(1, each, width)
    pieces = [result] + [swap(result, mask, size) for mask, _ in LINE]
    near = jnp.concatenate(pieces + [swap(piece, 2, size) for piece in pieces], axis=0)
    far = swap(near, 1, size)
    grad_wf, grad_wb = pl.pallas_call(
        functools.partial(
            assemble_kernel,
            wf_rows=wf_rows,
            wb_rows=wb_rows,
            factor_f=math.sqrt(high),
            factor_b=math.sqrt(wide),
        ),
        in_specs=[SMEM] + [VMEM] * 2,
        out_specs=[VMEM] * 2,
        out_shape=[
            jax.ShapeDtypeStruct((high, width), F32),
            jax.ShapeDtypeStruct((wide, width), F32),
        ],
        compiler_params=pltpu.CompilerParams(vmem_limit_bytes=16 * 2**20),
    )(place.reshape(1), near, far)
    return (grad_wf, grad_wb, note.reshape(1))


def solution(mesh):
    placed = (
        P(("grp", "fa"), None),
        P(("grp", "fa"), None),
        P(("grp", "fa"), None),
        P(),
        P(),
        P(),
        P("grp", None),
        P(("grp", "fa")),
        P(("grp", "fa")),
    )
    return jax.shard_map(
        body,
        mesh=mesh,
        in_specs=placed,
        out_specs=(P("grp", None), P("grp", None), P("grp")),
        check_vma=False,
    )
```

```python
import functools
import math

import jax
import jax.numpy as jnp
from jax import lax
from jax.experimental import pallas as pl
from jax.experimental.pallas import tpu as pltpu
from jax.sharding import PartitionSpec as P

GAMMA = 0.98
LAMBDA = 1.0
EPS = 1e-06
BF = jnp.bfloat16
F32 = jnp.float32
GROUP = (0, 2, 1, 3)
PAD = 16
LINE = ((12, 3), (8, 1), (4, 2))
TURNS = (0, 3, 1, 2, 4, 7, 5, 6)


def dot(left, right):
    return jnp.dot(left, right, preferred_element_type=F32)


def dot_t(left, right):
    return lax.dot_general(left, right, (((0,), (0,)), ((), ())), preferred_element_type=F32)


def halves(array):
    high = array.astype(BF)
    return high, (array - high.astype(F32)).astype(BF)


def swap(array, mask, size):
    return lax.ppermute(array, "fa", [(i, i ^ mask) for i in range(size)])


def reverse_bits(value, bits):
    out = value * 0
    for k in range(bits):
        out = out + (((value >> k) & 1) << (bits - 1 - k))
    return out


def columns_of(row, rows):
    return jnp.transpose(jnp.broadcast_to(row, (rows, rows)))


def message_kernel(me_ref, hf_hbm, hb_hbm, wb_hbm, far_ref, near_ref, cut_ref, head_ref, wb_ref, sems):
    rows, width = cut_ref.shape
    me = me_ref[0]

    def columns(mask):
        other = me ^ mask
        quarter = (other & 1) * 2 + ((other >> 1) & 1)
        return hf_hbm.at[:, pl.ds(pl.multiple_of(quarter * width, width), width)]

    moves = [
        pltpu.make_async_copy(source, target, sems.at[k])
        for k, (source, target) in enumerate(
            (
                (columns(2), far_ref.at[:rows, :]),
                (columns(3), far_ref.at[rows : 2 * rows, :]),
                (hb_hbm, far_ref.at[2 * rows :, :]),
                (columns(1), near_ref.at[:rows, :]),
                (hb_hbm, near_ref.at[rows:, :]),
                (columns(0), cut_ref),
                (hb_hbm, head_ref),
                (wb_hbm, wb_ref),
            )
        )
    ]
    for move in moves:
        move.start()
    for move in moves:
        move.wait()


def feature_kernel(
    hf_hbm,
    ht_hbm,
    wf_hbm,
    wt_hbm,
    lat_hbm,
    ids_hbm,
    pos_hbm,
    out_ref,
    hf,
    ht,
    wf,
    wt,
    lat,
    ids,
    pos,
    sems,
):
    rows = hf.shape[0]
    width = wf.shape[1]
    moves = [
        pltpu.make_async_copy(source, target, sems.at[k])
        for k, (source, target) in enumerate(
            (
                (ids_hbm, ids),
                (pos_hbm, pos),
                (lat_hbm, lat),
                (hf_hbm, hf),
                (wf_hbm, wf),
                (ht_hbm, ht),
                (wt_hbm, wt),
            )
        )
    ]
    for move in moves:
        move.start()
    for move in moves[:3]:
        move.wait()
    who = columns_of(ids[...].astype(F32), rows)
    lanes = lax.broadcasted_iota(jnp.int32, (rows, rows), 1).astype(F32)
    tiles = [
        jnp.where(who == lanes + float(t * rows), 1.0, 0.0).astype(BF) for t in range(lat.shape[0] // rows)
    ]
    zrows = dot(jnp.concatenate(tiles, axis=1), lat[...])
    place = pos[...]
    line = lax.broadcasted_iota(jnp.int32, (PAD, rows), 0)
    high = jnp.broadcast_to(lax.shift_right_logical(place, 7).astype(F32), (PAD, rows))
    low = jnp.broadcast_to((place & 127).astype(F32), (PAD, rows))
    coded = jnp.where(line == 0, high, jnp.where(line == 1, low, 0.0)).astype(BF)
    coded = jnp.concatenate([coded] + [jnp.zeros((PAD, width - rows), BF)] * (width > rows), axis=1)

    out_ref[2 * rows :, :] = coded
    moves[3].wait()
    moves[4].wait()
    out_ref[:rows, :] = (dot(hf[...], wf[...]) + zrows).astype(BF)
    moves[5].wait()
    moves[6].wait()
    out_ref[rows : 2 * rows, :] = (dot(ht[...], wt[...]) + zrows).astype(BF)


def pack_kernel(*refs):
    at = 0
    for ref in refs[:-2]:
        refs[-1][at : at + ref.shape[0], :] = ref[...]
        at = at + ref.shape[0]


def pack(*arrays, after):
    return pl.pallas_call(
        pack_kernel,
        in_specs=[VMEM] * (len(arrays) + 1),
        out_specs=VMEM,
        out_shape=jax.ShapeDtypeStruct((sum(x.shape[0] for x in arrays), arrays[0].shape[1]), BF),
        compiler_params=pltpu.CompilerParams(vmem_limit_bytes=20 * 2**20),
    )(*arrays, after)


def pair_kernel(*refs, rows, total):
    base_ref, place_ref = refs[:2]
    near_ref, far_ref, core_ref = refs[2:5]
    feats = [(ref, 0) for ref in refs[5:9]]
    cut_ref, wb_ref, keep_ref, sends = refs[9], refs[10], refs[11], refs[12:15]
    hid_ref, raw_ref, back_ref, mask_ref, smat_ref, pick_ref, own_ref, wfq_ref, wbq_ref = refs[15:]
    width = wb_ref.shape[1]
    pairs = float(total * (total - 1))
    groups = total // (4 * rows)
    span = total // 16
    wb = wb_ref[...]
    end = 2 * rows + PAD
    heads = ((near_ref, rows), (far_ref, 2 * rows), (core_ref, rows), (core_ref, 4 * rows))
    cuts = ((cut_ref, 0), (far_ref, 0), (core_ref, 0), (core_ref, 3 * rows))
    segments = []
    for (head, start), (line, _) in zip(heads, feats):
        segments += [(head, start, rows), (line, end, 4 * span - rows)]
    first = 0
    for ref, start, length in segments:
        if length <= 4 * rows:
            hid_ref[first : first + length, :] = ref[start : start + length, :]
        else:

            def one(i, carry, ref=ref, start=start, first=first):
                hid_ref[pl.ds(pl.multiple_of(first + i * rows, PAD), rows), :] = ref[
                    pl.ds(pl.multiple_of(start + i * rows, PAD), rows), :
                ]
                return carry

            lax.fori_loop(0, length // rows, one, 0)
        first = first + length

    def embed(hidden):
        raw = dot(hidden, wb)
        scale = lax.rsqrt(jnp.mean(raw * raw, axis=-1, keepdims=True) + EPS)
        return raw, scale, (raw * scale).astype(BF)

    def through(grad, raw, scale):
        along = jnp.sum(grad * raw, axis=-1, keepdims=True)
        return (scale * grad - scale * scale * scale * (1.0 / width) * along * raw).astype(BF)

    big, small = mask_ref.shape[1], 4 * rows

    def over_rows(step):
        if big == total:
            step(0)
        else:
            lax.fori_loop(0, total // big, lambda i, carry: (step(i), carry)[1], 0)

    def at(start, length):
        return pl.ds(pl.multiple_of(start, rows), length)

    wanted = []
    for ref, start in feats:
        code = ref[start + 2 * rows : start + end, :rows].astype(F32)
        wanted.append(columns_of(code[0:1] * 128.0 + code[1:2], rows))
    lanes = lax.broadcasted_iota(jnp.int32, (rows, rows), 1)
    smat_ref[...] = jnp.zeros_like(smat_ref)
    pick_ref[...] = jnp.zeros_like(pick_ref)

    def first_pass(step):
        for i in range(big // small):
            here = at(step * big + i * small, small)
            raw, _, back = embed(hid_ref[here, :])
            raw_ref[here, :] = raw
            back_ref[here, :] = back
        for t in range(big // rows):
            ids = (lanes + base_ref[step * (big // rows) + t]).astype(F32)
            for g, want in enumerate(wanted):
                mask_ref[g * rows : (g + 1) * rows, t * rows : (t + 1) * rows] = jnp.where(
                    want == ids, 1.0, 0.0
                ).astype(BF)
        here = at(step * big, big)
        smat_ref[...] += dot_t(back_ref[here, :], back_ref[here, :])
        pick_ref[...] += dot(mask_ref[...], hid_ref[here, :])

    over_rows(first_pass)
    smat = smat_ref[...]
    s_hi, s_lo = halves(smat)
    quarter, mine = place_ref[0], place_ref[1]
    half = wbq_ref.shape[0]
    columns = pl.ds(pl.multiple_of((quarter >> 1) * half, half), half)

    def rows_of(places, offset):
        return jnp.concatenate([ref[at + offset : at + offset + rows, :] for ref, at in places], axis=0)

    feat = rows_of(feats, 0)
    f32feat = feat.astype(F32)
    diff = f32feat - GAMMA * rows_of(feats, rows).astype(F32)
    d_hi, d_lo = halves(diff)
    kmat = dot_t(d_hi, feat) + dot_t(d_lo, feat)
    hidden = pick_ref[...].astype(BF)
    own_ref[...] = hidden
    raw, scale, back = embed(hidden)
    ob = back.astype(F32)
    ds = dot(d_hi, s_hi) + dot(d_lo, s_hi) + dot(d_hi, s_lo)
    db = jnp.sum(diff * ob, axis=-1, keepdims=True)
    coef = db * (1.0 / pairs) + 1.0 / total
    norm = jnp.sum(ob * ob, axis=-1, keepdims=True)
    grad_f = (ds * (1.0 / pairs) - coef * ob).astype(BF)
    wfq_ref[...] = dot_t(rows_of(cuts, 0), grad_f)
    squares = jnp.sum(diff * ds) - jnp.sum(db * db)
    squares = squares + LAMBDA * (jnp.sum(smat * smat) / groups - jnp.sum(norm * norm))
    sums = squares / (2.0 * pairs) - (jnp.sum(f32feat * ob) + LAMBDA * jnp.sum(norm)) / total
    grad_own = through(
        -coef * f32feat - (norm * (2.0 * LAMBDA / pairs) + 2.0 * LAMBDA / total) * ob, raw, scale
    )
    wbq_ref[...] = dot_t(own_ref[:, columns], grad_own)
    a_hi, a_lo = halves((kmat + (2.0 * LAMBDA / groups) * smat) * (1.0 / pairs))

    def second_pass(step):
        for i in range(big // small):
            here = at(step * big + i * small, small)
            raw = raw_ref[here, :]
            scale = lax.rsqrt(jnp.mean(raw * raw, axis=-1, keepdims=True) + EPS)
            back = back_ref[here, :]
            back_ref[here, :] = through(dot(back, a_hi) + dot(back, a_lo), raw, scale)
        here = at(step * big, big)
        wbq_ref[...] += dot_t(hid_ref[here, columns], back_ref[here, :])

    over_rows(second_pass)
    wf_rows = wfq_ref.shape[0] // 4
    wb_rows = wbq_ref.shape[0] // 8
    size = wf_rows + wb_rows

    def block(t):
        return (
            wfq_ref[pl.ds(pl.multiple_of(t * wf_rows, wf_rows), wf_rows), :],
            wbq_ref[pl.ds(pl.multiple_of(((quarter & 1) * 4 + t) * wb_rows, wb_rows), wb_rows), :],
        )

    keep_ref[:wf_rows, :], keep_ref[wf_rows:size, :] = block(mine)
    note = jnp.full((PAD, width), sums, F32)
    keep_ref[size:, :] = note
    line = lax.broadcasted_iota(jnp.int32, (PAD, width), 0)
    n_hi = note.astype(BF)
    n_mid, n_lo = halves(note - n_hi.astype(F32))
    coded = jnp.where(
        line == 0,
        n_hi.astype(F32),
        jnp.where(line == 1, n_mid.astype(F32), jnp.where(line == 2, n_lo.astype(F32), 0.0)),
    ).astype(BF)
    for ref, (_, turn) in zip(sends, LINE):
        part_f, part_b = block(mine ^ turn)
        ref[:wf_rows, :] = part_f.astype(BF)
        ref[wf_rows:size, :] = part_b.astype(BF)
        ref[size:, :] = coded


def add_kernel(keep_ref, *refs):
    sum_ref, note_ref = refs[3:]
    size, width = sum_ref.shape
    total = keep_ref[:size, :]
    note = keep_ref[size : size + 1, :1]
    for ref in refs[:3]:
        total = total + ref[:size, :].astype(F32)
        coded = ref[size:, :].astype(F32)
        note = note + (coded[0:1, :1] + coded[1:2, :1] + coded[2:3, :1])
    sum_ref[...] = total.astype(sum_ref.dtype)
    note_ref[...] = note * (1.0 / width)


def assemble_kernel(place_ref, *refs, wf_rows, wb_rows, factor_f, factor_b):
    place = place_ref[0]
    wf_ref, wb_ref = refs[4:]
    for offset, ref in zip((0, 4, 8, 12), refs):
        for e, turn in enumerate((0,) + tuple(turn for _, turn in LINE)):
            to = place ^ (offset + turn)
            wf_ref[pl.ds(pl.multiple_of(to * wf_rows, wf_rows), wf_rows), :] = (
                ref[e, :wf_rows, :].astype(F32) * factor_f
            )
            wb_ref[pl.ds(pl.multiple_of(to * wb_rows, wb_rows), wb_rows), :] = (
                ref[e, wf_rows:, :].astype(F32) * factor_b
            )


def assemble_kernel(place_ref, *refs, wf_rows, wb_rows, factor_f, factor_b):
    place = place_ref[0]
    wf_ref, wb_ref = refs[2:]
    for offset, ref in zip((0, 8), refs):
        for e, turn in enumerate(TURNS):
            to = place ^ (offset + turn)
            wf_ref[pl.ds(pl.multiple_of(to * wf_rows, wf_rows), wf_rows), :] = (
                ref[e, :wf_rows, :].astype(F32) * factor_f
            )
            wb_ref[pl.ds(pl.multiple_of(to * wb_rows, wb_rows), wb_rows), :] = (
                ref[e, wf_rows:, :].astype(F32) * factor_b
            )


SMEM = pl.BlockSpec(memory_space=pltpu.SMEM)
VMEM = pl.BlockSpec(memory_space=pltpu.VMEM)
HBM = pl.BlockSpec(memory_space=pltpu.HBM)


def body(hidden_f, hidden_t, hidden_b, w_f, w_t, w_b, latents, latent_ids, positives):
    rows, high = hidden_f.shape
    wide = hidden_b.shape[1]
    width = w_f.shape[1]
    size = lax.axis_size("fa")
    bits = size.bit_length() - 1
    beyond = [1 << k for k in range(4, bits)]
    me = lax.axis_index("fa")
    total = size * rows
    assert bits >= 4 and size == 1 << bits and high // 4 == width == wide

    far, near, cut, head, wb_copy = pl.pallas_call(
        message_kernel,
        in_specs=[SMEM] + [HBM] * 3,
        out_specs=[VMEM] * 5,
        out_shape=[
            jax.ShapeDtypeStruct((3 * rows, width), BF),
            jax.ShapeDtypeStruct((2 * rows, width), BF),
            jax.ShapeDtypeStruct((rows, width), BF),
            jax.ShapeDtypeStruct(hidden_b.shape, BF),
            jax.ShapeDtypeStruct(w_b.shape, BF),
        ],
        scratch_shapes=[pltpu.SemaphoreType.DMA((8,))],
        compiler_params=pltpu.CompilerParams(vmem_limit_bytes=59 * 2**20),
    )(me.astype(jnp.int32).reshape(1), hidden_f, hidden_b, w_b)
    feats0 = pl.pallas_call(
        feature_kernel,
        in_specs=[HBM] * 7,
        out_specs=VMEM,
        out_shape=jax.ShapeDtypeStruct((2 * rows + PAD, width), BF),
        scratch_shapes=[
            pltpu.VMEM(hidden_f.shape, BF),
            pltpu.VMEM(hidden_t.shape, BF),
            pltpu.VMEM(w_f.shape, BF),
            pltpu.VMEM(w_t.shape, BF),
            pltpu.VMEM(latents.shape, BF),
            pltpu.VMEM((1, rows), jnp.int32),
            pltpu.VMEM((1, rows), jnp.int32),
            pltpu.SemaphoreType.DMA((7,)),
        ],
        compiler_params=pltpu.CompilerParams(vmem_limit_bytes=59 * 2**20),
        cost_estimate=pl.CostEstimate(
            flops=4 * rows * high * width, bytes_accessed=4 * high * (rows + width), transcendentals=0
        ),
    )(
        hidden_f,
        hidden_t,
        w_f,
        w_t,
        latents,
        latent_ids.reshape(1, rows),
        positives.reshape(1, rows),
    )
    far2 = swap(far, 2, size)
    for mask in reversed(beyond):
        head = jnp.concatenate([head, swap(head, mask, size)], axis=0)
    piece12, piece8, piece4 = [swap(head, mask, size) for mask, _ in LINE]
    to_core = pack(near, far2, after=near)
    more = [head[rows:]] * (len(beyond) > 0)
    second0 = pack(feats0, piece4, piece8, piece12, *more, after=to_core)
    second2 = swap(second0, 2, size)
    from_core = swap(to_core, 1, size)
    second1 = swap(second0, 1, size)
    second3 = swap(second2, 1, size)

    inner = reverse_bits(jnp.arange(size // 16, dtype=jnp.int32), bits - 4) << 4
    first, others = inner[:1], inner[1:]
    bases = []
    for core in (0, 1):
        bases += [core ^ first] + [core ^ mask ^ inner for mask in (4, 8, 12)] + [core ^ others]
        core = core ^ 2
        bases += [core ^ first] + [core ^ mask ^ inner for mask in (4, 8, 12)] + [core ^ others]
    bases = ((me ^ jnp.concatenate(bases)) * rows).astype(jnp.int32)
    place = reverse_bits(me & 15, 4).astype(jnp.int32)
    places = jnp.stack([place >> 2, place & 3])
    wf_rows, wb_rows = high // 16, wide // 16
    each = wf_rows + wb_rows
    keep, *sends = pl.pallas_call(
        functools.partial(pair_kernel, rows=rows, total=total),
        in_specs=[SMEM] * 2 + [VMEM] * 9,
        out_specs=[VMEM] * 4,
        out_shape=[jax.ShapeDtypeStruct((each + PAD, width), F32)]
        + [jax.ShapeDtypeStruct((each + PAD, width), BF)] * 3,
        scratch_shapes=[
            pltpu.VMEM((total, wide), BF),
            pltpu.VMEM((total, width), F32),
            pltpu.VMEM((total, width), BF),
            pltpu.VMEM((4 * rows, min(total, 16 * rows)), BF),
            pltpu.VMEM((width, width), F32),
            pltpu.VMEM((4 * rows, wide), F32),
            pltpu.VMEM((4 * rows, wide), BF),
            pltpu.VMEM((width, width), F32),
            pltpu.VMEM((wide // 2, width), F32),
        ],
        compiler_params=pltpu.CompilerParams(vmem_limit_bytes=15 * 2**20 + total * width * 10),
    )(bases, places, near, far2, from_core, second0, second2, second1, second3, cut, wb_copy)

    got = [swap(part, mask, size) for part, (mask, _) in zip(sends, LINE)]
    result, note = pl.pallas_call(
        add_kernel,
        in_specs=[VMEM] * 4,
        out_specs=[VMEM] * 2,
        out_shape=[
            jax.ShapeDtypeStruct((each, width), F32 if beyond else BF),
            jax.ShapeDtypeStruct((1, 1), F32),
        ],
        compiler_params=pltpu.CompilerParams(vmem_limit_bytes=8 * 2**20),
    )(keep, *got)
    for mask in beyond:
        result = result + swap(result, mask, size)
        note = note + swap(note, mask, size)
    result = result.astype(BF).reshape(1, each, width)
    pieces = [result] + [swap(result, mask, size) for mask, _ in LINE]
    near = jnp.concatenate(pieces + [swap(piece, 2, size) for piece in pieces], axis=0)
    far = swap(near, 1, size)
    grad_wf, grad_wb = pl.pallas_call(
        functools.partial(
            assemble_kernel,
            wf_rows=wf_rows,
            wb_rows=wb_rows,
            factor_f=math.sqrt(high),
            factor_b=math.sqrt(wide),
        ),
        in_specs=[SMEM] + [VMEM] * 2,
        out_specs=[VMEM] * 2,
        out_shape=[
            jax.ShapeDtypeStruct((high, width), F32),
            jax.ShapeDtypeStruct((wide, width), F32),
        ],
        compiler_params=pltpu.CompilerParams(vmem_limit_bytes=16 * 2**20),
    )(place.reshape(1), near, far)
    return (grad_wf, grad_wb, note.reshape(1))


def solution(mesh):
    placed = (
        P(("grp", "fa"), None),
        P(("grp", "fa"), None),
        P(("grp", "fa"), None),
        P(),
        P(),
        P(),
        P("grp", None),
        P(("grp", "fa")),
        P(("grp", "fa")),
    )
    return jax.shard_map(
        body,
        mesh=mesh,
        in_specs=placed,
        out_specs=(P("grp", None), P("grp", None), P("grp")),
        check_vma=False,
    )
```

```python
import functools
import math

import jax
import jax.numpy as jnp
from jax import lax
from jax.experimental import pallas as pl
from jax.experimental.pallas import tpu as pltpu
from jax.sharding import PartitionSpec as P

GAMMA = 0.98
LAMBDA = 1.0
EPS = 1e-06
BF = jnp.bfloat16
F32 = jnp.float32
FEAT_AT = 2
PAD = 16
LINE = ((12, 3), (8, 1), (4, 2))
OTHERS = ((14, 7), (12, 3), (10, 5), (8, 1), (6, 6), (4, 2), (2, 4))
TURNS = (0, 3, 1, 2, 4, 7, 5, 6)


def dot(left, right):
    return jnp.dot(left, right, preferred_element_type=F32)


def dot_t(left, right):
    return lax.dot_general(left, right, (((0,), (0,)), ((), ())), preferred_element_type=F32)


def halves(array):
    high = array.astype(BF)
    return high, (array - high.astype(F32)).astype(BF)


def swap(array, mask, size):
    return lax.ppermute(array, "fa", [(i, i ^ mask) for i in range(size)])


def reverse_bits(value, bits):
    out = value * 0
    for k in range(bits):
        out = out + (((value >> k) & 1) << (bits - 1 - k))
    return out


def columns_of(row, rows):
    return jnp.transpose(jnp.broadcast_to(row, (rows, rows)))


def feature_kernel(
    core_ref,
    hf_hbm,
    ht_hbm,
    wf_hbm,
    wt_hbm,
    wb_hbm,
    lat_hbm,
    ids_hbm,
    pos_hbm,
    near_ref,
    cut_ref,
    wb_ref,
    hf,
    ht,
    wf,
    wt,
    lat,
    ids,
    pos,
    sems,
):
    rows = hf.shape[0]
    width = wf.shape[1]
    moves = [
        pltpu.make_async_copy(source, target, sems.at[k])
        for k, (source, target) in enumerate(
            (
                (ids_hbm, ids),
                (pos_hbm, pos),
                (lat_hbm, lat),
                (hf_hbm, hf),
                (wf_hbm, wf),
                (ht_hbm, ht),
                (wt_hbm, wt),
                (wb_hbm, wb_ref),
            )
        )
    ]
    for move in moves:
        move.start()
    for move in moves[:3]:
        move.wait()
    who = columns_of(ids[...].astype(F32), rows)
    lanes = lax.broadcasted_iota(jnp.int32, (rows, rows), 1).astype(F32)
    tiles = [
        jnp.where(who == lanes + float(t * rows), 1.0, 0.0).astype(BF) for t in range(lat.shape[0] // rows)
    ]
    zrows = dot(jnp.concatenate(tiles, axis=1), lat[...])
    place = pos[...]
    line = lax.broadcasted_iota(jnp.int32, (PAD, rows), 0)
    high = jnp.broadcast_to(lax.shift_right_logical(place, 7).astype(F32), (PAD, rows))
    low = jnp.broadcast_to((place & 127).astype(F32), (PAD, rows))
    coded = jnp.where(line == 0, high, jnp.where(line == 1, low, 0.0)).astype(BF)
    coded = jnp.concatenate([coded] + [jnp.zeros((PAD, width - rows), BF)] * (width > rows), axis=1)

    moves[3].wait()
    core = core_ref[0]
    for t in range(2):
        for ref, half in ((cut_ref, core), (near_ref, 1 - core)):
            ref[t * rows : (t + 1) * rows, :] = hf[
                :, pl.ds(pl.multiple_of((half * 2 + t) * width, width), width)
            ]
    moves[4].wait()
    feat = (dot(hf[...], wf[...]) + zrows).astype(BF)
    moves[5].wait()
    moves[6].wait()
    feat_t = (dot(ht[...], wt[...]) + zrows).astype(BF)
    near_ref[FEAT_AT * rows : (FEAT_AT + 1) * rows, :] = feat
    near_ref[(FEAT_AT + 1) * rows : (FEAT_AT + 2) * rows, :] = feat_t
    near_ref[(FEAT_AT + 2) * rows :, :] = coded
    moves[7].wait()


def pack_kernel(*refs):
    at = 0
    for ref in refs[:-2]:
        refs[-1][at : at + ref.shape[0], :] = ref[...]
        at = at + ref.shape[0]


def pack(*arrays, after):
    return pl.pallas_call(
        pack_kernel,
        in_specs=[VMEM] * (len(arrays) + 1),
        out_specs=VMEM,
        out_shape=jax.ShapeDtypeStruct((sum(x.shape[0] for x in arrays), arrays[0].shape[1]), BF),
        compiler_params=pltpu.CompilerParams(vmem_limit_bytes=20 * 2**20),
    )(*arrays, after)


def pair_kernel(*refs, rows, total):
    base_ref, place_ref = refs[:2]
    nears, lines, cut_ref, wb_ref = refs[2:4], refs[4:8], refs[8], refs[9]
    keep_ref, sends = refs[10], refs[11:18]
    hid_ref, raw_ref, back_ref, mask_ref, smat_ref, pick_ref, own_ref, wfq_ref, wbq_ref = refs[18:]
    width = wb_ref.shape[1]
    pairs = float(total * (total - 1))
    groups = total // (2 * rows)
    wb = wb_ref[...]
    end = 2 * rows + PAD
    feats = [(ref, FEAT_AT * rows) for ref in nears]
    cuts = ((cut_ref, 0), (nears[1], 0))
    length = total // 4
    for i, ref in enumerate(lines):
        if length <= 8 * rows:
            hid_ref[i * length : (i + 1) * length, :] = ref[...]
        else:

            def one(k, carry, ref=ref, first=i * length):
                hid_ref[pl.ds(pl.multiple_of(first + k * rows, rows), rows), :] = ref[
                    pl.ds(pl.multiple_of(k * rows, rows), rows), :
                ]
                return carry

            lax.fori_loop(0, length // rows, one, 0)

    def embed(hidden):
        raw = dot(hidden, wb)
        scale = lax.rsqrt(jnp.mean(raw * raw, axis=-1, keepdims=True) + EPS)
        return raw, scale, (raw * scale).astype(BF)

    def through(grad, raw, scale):
        along = jnp.sum(grad * raw, axis=-1, keepdims=True)
        return (scale * grad - scale * scale * scale * (1.0 / width) * along * raw).astype(BF)

    big, small = mask_ref.shape[1], 4 * rows

    def over_rows(step):
        if big == total:
            step(0)
        else:
            lax.fori_loop(0, total // big, lambda i, carry: (step(i), carry)[1], 0)

    def at(start, length):
        return pl.ds(pl.multiple_of(start, rows), length)

    wanted = []
    for ref, start in feats:
        code = ref[start + 2 * rows : start + end, :rows].astype(F32)
        wanted.append(columns_of(code[0:1] * 128.0 + code[1:2], rows))
    lanes = lax.broadcasted_iota(jnp.int32, (rows, rows), 1)
    smat_ref[...] = jnp.zeros_like(smat_ref)
    pick_ref[...] = jnp.zeros_like(pick_ref)

    def first_pass(step):
        for i in range(big // small):
            here = at(step * big + i * small, small)
            raw, _, back = embed(hid_ref[here, :])
            raw_ref[here, :] = raw
            back_ref[here, :] = back
        for t in range(big // rows):
            ids = (lanes + base_ref[step * (big // rows) + t]).astype(F32)
            for g, want in enumerate(wanted):
                mask_ref[g * rows : (g + 1) * rows, t * rows : (t + 1) * rows] = jnp.where(
                    want == ids, 1.0, 0.0
                ).astype(BF)
        here = at(step * big, big)
        smat_ref[...] += dot_t(back_ref[here, :], back_ref[here, :])
        pick_ref[...] += dot(mask_ref[...], hid_ref[here, :])

    over_rows(first_pass)
    smat = smat_ref[...]
    s_hi, s_lo = halves(smat)
    core, mine = place_ref[0], place_ref[1]
    half = wbq_ref.shape[0]
    columns = pl.ds(pl.multiple_of(core * half, half), half)

    def rows_of(places, offset):
        return jnp.concatenate([ref[at + offset : at + offset + rows, :] for ref, at in places], axis=0)

    feat = rows_of(feats, 0)
    f32feat = feat.astype(F32)
    diff = f32feat - GAMMA * rows_of(feats, rows).astype(F32)
    d_hi, d_lo = halves(diff)
    kmat = dot_t(d_hi, feat) + dot_t(d_lo, feat)
    hidden = pick_ref[...].astype(BF)
    own_ref[...] = hidden
    raw, scale, back = embed(hidden)
    ob = back.astype(F32)
    ds = dot(d_hi, s_hi) + dot(d_lo, s_hi) + dot(d_hi, s_lo)
    db = jnp.sum(diff * ob, axis=-1, keepdims=True)
    coef = db * (1.0 / pairs) + 1.0 / total
    norm = jnp.sum(ob * ob, axis=-1, keepdims=True)
    grad_f = (ds * (1.0 / pairs) - coef * ob).astype(BF)
    for t in range(2):
        wfq_ref[t * width : (t + 1) * width, :] = dot_t(rows_of(cuts, t * rows), grad_f)
    squares = jnp.sum(diff * ds) - jnp.sum(db * db)
    squares = squares + LAMBDA * (jnp.sum(smat * smat) / groups - jnp.sum(norm * norm))
    sums = squares / (2.0 * pairs) - (jnp.sum(f32feat * ob) + LAMBDA * jnp.sum(norm)) / total
    grad_own = through(
        -coef * f32feat - (norm * (2.0 * LAMBDA / pairs) + 2.0 * LAMBDA / total) * ob, raw, scale
    )
    wbq_ref[...] = dot_t(own_ref[:, columns], grad_own)
    a_hi, a_lo = halves((kmat + (2.0 * LAMBDA / groups) * smat) * (1.0 / pairs))

    def second_pass(step):
        for i in range(big // small):
            here = at(step * big + i * small, small)
            raw = raw_ref[here, :]
            scale = lax.rsqrt(jnp.mean(raw * raw, axis=-1, keepdims=True) + EPS)
            back = back_ref[here, :]
            back_ref[here, :] = through(dot(back, a_hi) + dot(back, a_lo), raw, scale)
        here = at(step * big, big)
        wbq_ref[...] += dot_t(hid_ref[here, columns], back_ref[here, :])

    over_rows(second_pass)
    wf_rows = wfq_ref.shape[0] // 8
    wb_rows = wbq_ref.shape[0] // 8
    size = wf_rows + wb_rows

    def block(t):
        return (
            wfq_ref[pl.ds(pl.multiple_of(t * wf_rows, wf_rows), wf_rows), :],
            wbq_ref[pl.ds(pl.multiple_of(t * wb_rows, wb_rows), wb_rows), :],
        )

    keep_ref[:wf_rows, :], keep_ref[wf_rows:size, :] = block(mine)
    note = jnp.full((PAD, width), sums, F32)
    keep_ref[size:, :] = note
    line = lax.broadcasted_iota(jnp.int32, (PAD, width), 0)
    n_hi = note.astype(BF)
    n_mid, n_lo = halves(note - n_hi.astype(F32))
    coded = jnp.where(
        line == 0,
        n_hi.astype(F32),
        jnp.where(line == 1, n_mid.astype(F32), jnp.where(line == 2, n_lo.astype(F32), 0.0)),
    ).astype(BF)
    for ref, (_, turn) in zip(sends, OTHERS):
        part_f, part_b = block(mine ^ turn)
        ref[:wf_rows, :] = part_f.astype(BF)
        ref[wf_rows:size, :] = part_b.astype(BF)
        ref[size:, :] = coded


def add_kernel(keep_ref, *refs):
    sum_ref, note_ref = refs[7:]
    size, width = sum_ref.shape
    total = keep_ref[:size, :]
    note = keep_ref[size : size + 1, :1]
    for ref in refs[:7]:
        total = total + ref[:size, :].astype(F32)
        coded = ref[size:, :].astype(F32)
        note = note + (coded[0:1, :1] + coded[1:2, :1] + coded[2:3, :1])
    sum_ref[...] = total.astype(sum_ref.dtype)
    note_ref[...] = note * (1.0 / width)


def assemble_kernel(place_ref, *refs, wf_rows, wb_rows, factor_f, factor_b):
    place = place_ref[0]
    wf_ref, wb_ref = refs[4:]
    for offset, ref in zip((0, 4, 8, 12), refs):
        for e, turn in enumerate((0,) + tuple(turn for _, turn in LINE)):
            to = place ^ (offset + turn)
            wf_ref[pl.ds(pl.multiple_of(to * wf_rows, wf_rows), wf_rows), :] = (
                ref[e, :wf_rows, :].astype(F32) * factor_f
            )
            wb_ref[pl.ds(pl.multiple_of(to * wb_rows, wb_rows), wb_rows), :] = (
                ref[e, wf_rows:, :].astype(F32) * factor_b
            )


def assemble_kernel(place_ref, *refs, wf_rows, wb_rows, factor_f, factor_b):
    place = place_ref[0]
    wf_ref, wb_ref = refs[2:]
    for offset, ref in zip((0, 8), refs):
        for e, turn in enumerate(TURNS):
            to = place ^ (offset + turn)
            wf_ref[pl.ds(pl.multiple_of(to * wf_rows, wf_rows), wf_rows), :] = (
                ref[e, :wf_rows, :].astype(F32) * factor_f
            )
            wb_ref[pl.ds(pl.multiple_of(to * wb_rows, wb_rows), wb_rows), :] = (
                ref[e, wf_rows:, :].astype(F32) * factor_b
            )


SMEM = pl.BlockSpec(memory_space=pltpu.SMEM)
VMEM = pl.BlockSpec(memory_space=pltpu.VMEM)
HBM = pl.BlockSpec(memory_space=pltpu.HBM)


def body(hidden_f, hidden_t, hidden_b, w_f, w_t, w_b, latents, latent_ids, positives):
    rows, high = hidden_f.shape
    wide = hidden_b.shape[1]
    width = w_f.shape[1]
    size = lax.axis_size("fa")
    bits = size.bit_length() - 1
    beyond = [1 << k for k in range(4, bits)]
    me = lax.axis_index("fa")
    total = size * rows
    assert bits >= 4 and size == 1 << bits and high // 4 == width == wide

    head = hidden_b
    for mask in reversed(beyond):
        head = jnp.concatenate([head, swap(head, mask, size)], axis=0)
    pieces = [swap(head, mask, size) for mask, _ in LINE]
    core = (me & 1).astype(jnp.int32)
    near, cut, wb_copy = pl.pallas_call(
        feature_kernel,
        in_specs=[SMEM] + [HBM] * 8,
        out_specs=[VMEM] * 3,
        out_shape=[
            jax.ShapeDtypeStruct(((FEAT_AT + 2) * rows + PAD, width), BF),
            jax.ShapeDtypeStruct((2 * rows, width), BF),
            jax.ShapeDtypeStruct(w_b.shape, BF),
        ],
        scratch_shapes=[
            pltpu.VMEM(hidden_f.shape, BF),
            pltpu.VMEM(hidden_t.shape, BF),
            pltpu.VMEM(w_f.shape, BF),
            pltpu.VMEM(w_t.shape, BF),
            pltpu.VMEM(latents.shape, BF),
            pltpu.VMEM((1, rows), jnp.int32),
            pltpu.VMEM((1, rows), jnp.int32),
            pltpu.SemaphoreType.DMA((8,)),
        ],
        compiler_params=pltpu.CompilerParams(vmem_limit_bytes=60 * 2**20),
    )(
        core.reshape(1),
        hidden_f,
        hidden_t,
        w_f,
        w_t,
        w_b,
        latents,
        latent_ids.reshape(1, rows),
        positives.reshape(1, rows),
    )
    near1 = swap(near, 1, size)
    line0 = pack(head, *pieces, after=near)
    line2 = swap(line0, 2, size)
    line1 = swap(line0, 1, size)
    line3 = swap(line2, 1, size)

    inner = reverse_bits(jnp.arange(size // 16, dtype=jnp.int32), bits - 4) << 4
    bases = []
    for way in (0, 2, 1, 3):
        bases += [way ^ inner] + [way ^ mask ^ inner for mask, _ in LINE]
    bases = ((me ^ jnp.concatenate(bases)) * rows).astype(jnp.int32)
    place = reverse_bits(me & 15, 4).astype(jnp.int32)
    places = jnp.stack([core, place & 7])
    wf_rows, wb_rows = high // 16, wide // 16
    each = wf_rows + wb_rows
    keep, *sends = pl.pallas_call(
        functools.partial(pair_kernel, rows=rows, total=total),
        in_specs=[SMEM] * 2 + [VMEM] * 8,
        out_specs=[VMEM] * 8,
        out_shape=[jax.ShapeDtypeStruct((each + PAD, width), F32)]
        + [jax.ShapeDtypeStruct((each + PAD, width), BF)] * 7,
        scratch_shapes=[
            pltpu.VMEM((total, wide), BF),
            pltpu.VMEM((total, width), F32),
            pltpu.VMEM((total, width), BF),
            pltpu.VMEM((2 * rows, min(total, 16 * rows)), BF),
            pltpu.VMEM((width, width), F32),
            pltpu.VMEM((2 * rows, wide), F32),
            pltpu.VMEM((2 * rows, wide), BF),
            pltpu.VMEM((2 * width, width), F32),
            pltpu.VMEM((wide // 2, width), F32),
        ],
        compiler_params=pltpu.CompilerParams(vmem_limit_bytes=15 * 2**20 + total * width * 10),
    )(bases, places, near, near1, line0, line2, line1, line3, cut, wb_copy)

    got = [swap(part, mask, size) for part, (mask, _) in zip(sends, OTHERS)]
    result, note = pl.pallas_call(
        add_kernel,
        in_specs=[VMEM] * 8,
        out_specs=[VMEM] * 2,
        out_shape=[
            jax.ShapeDtypeStruct((each, width), F32 if beyond else BF),
            jax.ShapeDtypeStruct((1, 1), F32),
        ],
        compiler_params=pltpu.CompilerParams(vmem_limit_bytes=8 * 2**20),
    )(keep, *got)
    for mask in beyond:
        result = result + swap(result, mask, size)
        note = note + swap(note, mask, size)
    result = result.astype(BF).reshape(1, each, width)
    pieces = [result] + [swap(result, mask, size) for mask, _ in LINE]
    near = jnp.concatenate(pieces + [swap(piece, 2, size) for piece in pieces], axis=0)
    far = swap(near, 1, size)
    grad_wf, grad_wb = pl.pallas_call(
        functools.partial(
            assemble_kernel,
            wf_rows=wf_rows,
            wb_rows=wb_rows,
            factor_f=math.sqrt(high),
            factor_b=math.sqrt(wide),
        ),
        in_specs=[SMEM] + [VMEM] * 2,
        out_specs=[VMEM] * 2,
        out_shape=[
            jax.ShapeDtypeStruct((high, width), F32),
            jax.ShapeDtypeStruct((wide, width), F32),
        ],
        compiler_params=pltpu.CompilerParams(vmem_limit_bytes=16 * 2**20),
    )(place.reshape(1), near, far)
    return (grad_wf, grad_wb, note.reshape(1))


def solution(mesh):
    placed = (
        P(("grp", "fa"), None),
        P(("grp", "fa"), None),
        P(("grp", "fa"), None),
        P(),
        P(),
        P(),
        P("grp", None),
        P(("grp", "fa")),
        P(("grp", "fa")),
    )
    return jax.shard_map(
        body,
        mesh=mesh,
        in_specs=placed,
        out_specs=(P("grp", None), P("grp", None), P("grp")),
        check_vma=False,
    )
```

```python
import functools
import math

import jax
import jax.numpy as jnp
from jax import lax
from jax.experimental import pallas as pl
from jax.experimental.pallas import tpu as pltpu
from jax.sharding import PartitionSpec as P

GAMMA = 0.98
LAMBDA = 1.0
EPS = 1e-06
BF = jnp.bfloat16
F32 = jnp.float32
GROUP = (0, 2, 1, 3)
CUT_AT = (0, 0, 0, 1)
HEAD_AT = (1, 2, 1, 2)
FEAT_AT = (2, 3, 2, 3)
PAD = 16
LINE = ((12, 3), (8, 1), (4, 2))
TURNS = (0, 3, 1, 2, 4, 7, 5, 6)


def dot(left, right):
    return jnp.dot(left, right, preferred_element_type=F32)


def dot_t(left, right):
    return lax.dot_general(left, right, (((0,), (0,)), ((), ())), preferred_element_type=F32)


def halves(array):
    high = array.astype(BF)
    return high, (array - high.astype(F32)).astype(BF)


def swap(array, mask, size):
    return lax.ppermute(array, "fa", [(i, i ^ mask) for i in range(size)])


def reverse_bits(value, bits):
    out = value * 0
    for k in range(bits):
        out = out + (((value >> k) & 1) << (bits - 1 - k))
    return out


def columns_of(row, rows):
    return jnp.transpose(jnp.broadcast_to(row, (rows, rows)))


def feature_kernel(
    me_ref,
    hf_hbm,
    ht_hbm,
    hb_hbm,
    wf_hbm,
    wt_hbm,
    wb_hbm,
    lat_hbm,
    ids_hbm,
    pos_hbm,
    far_ref,
    near_ref,
    cut_ref,
    head_ref,
    wb_ref,
    hf,
    ht,
    wf,
    wt,
    lat,
    ids,
    pos,
    sems,
):
    rows = hf.shape[0]
    width = wf.shape[1]
    moves = [
        pltpu.make_async_copy(source, target, sems.at[k])
        for k, (source, target) in enumerate(
            (
                (ids_hbm, ids),
                (pos_hbm, pos),
                (lat_hbm, lat),
                (hf_hbm, hf),
                (wf_hbm, wf),
                (ht_hbm, ht),
                (wt_hbm, wt),
                (hb_hbm, head_ref),
                (wb_hbm, wb_ref),
            )
        )
    ]
    for move in moves:
        move.start()
    for move in moves[:3]:
        move.wait()
    who = columns_of(ids[...].astype(F32), rows)
    lanes = lax.broadcasted_iota(jnp.int32, (rows, rows), 1).astype(F32)
    tiles = [
        jnp.where(who == lanes + float(t * rows), 1.0, 0.0).astype(BF) for t in range(lat.shape[0] // rows)
    ]
    zrows = dot(jnp.concatenate(tiles, axis=1), lat[...])
    place = pos[...]
    line = lax.broadcasted_iota(jnp.int32, (PAD, rows), 0)
    high = jnp.broadcast_to(lax.shift_right_logical(place, 7).astype(F32), (PAD, rows))
    low = jnp.broadcast_to((place & 127).astype(F32), (PAD, rows))
    coded = jnp.where(line == 0, high, jnp.where(line == 1, low, 0.0)).astype(BF)
    coded = jnp.concatenate([coded] + [jnp.zeros((PAD, width - rows), BF)] * (width > rows), axis=1)

    def piece(slot):
        other = me_ref[0] ^ GROUP[slot]
        quarter = (other & 1) * 2 + ((other >> 1) & 1)
        return hf[:, pl.ds(pl.multiple_of(quarter * width, width), width)]

    moves[3].wait()
    cut_ref[...] = piece(0)
    far_ref[:rows, :] = piece(1)
    near_ref[:rows, :] = piece(2)
    far_ref[rows : 2 * rows, :] = piece(3)
    moves[4].wait()
    feat = (dot(hf[...], wf[...]) + zrows).astype(BF)
    moves[5].wait()
    moves[6].wait()
    feat_t = (dot(ht[...], wt[...]) + zrows).astype(BF)
    moves[7].wait()
    head = head_ref[...]
    for ref, at in ((far_ref, HEAD_AT[1]), (near_ref, HEAD_AT[2])):
        ref[at * rows : (at + 1) * rows, :] = head
        ref[(at + 1) * rows : (at + 2) * rows, :] = feat
        ref[(at + 2) * rows : (at + 3) * rows, :] = feat_t
        ref[(at + 3) * rows :, :] = coded
    moves[8].wait()


def pack_kernel(*refs):
    at = 0
    for ref in refs[:-2]:
        refs[-1][at : at + ref.shape[0], :] = ref[...]
        at = at + ref.shape[0]


def pack(*arrays, after):
    return pl.pallas_call(
        pack_kernel,
        in_specs=[VMEM] * (len(arrays) + 1),
        out_specs=VMEM,
        out_shape=jax.ShapeDtypeStruct((sum(x.shape[0] for x in arrays), arrays[0].shape[1]), BF),
        compiler_params=pltpu.CompilerParams(vmem_limit_bytes=20 * 2**20),
    )(*arrays, after)


def pair_kernel(*refs, rows, total):
    me_ref = refs[0]
    mails, lines, cut_ref, wb_ref = refs[1:5], refs[5:9], refs[9], refs[10]
    keep_ref, sends = refs[11], refs[12:15]
    hid_ref, raw_ref, back_ref, mask_ref, smat_ref, pick_ref, own_ref, wfq_ref, wbq_ref = refs[15:]
    width = wb_ref.shape[1]
    pairs = float(total * (total - 1))
    groups = total // (4 * rows)
    wb = wb_ref[...]
    end = 2 * rows + PAD
    me = me_ref[0]
    feats = [(ref, at * rows) for ref, at in zip(mails, FEAT_AT)]
    cuts = [(ref, at * rows) for ref, at in zip((cut_ref,) + mails[1:], CUT_AT)]
    length = total // 4
    for i, (mail, line) in enumerate(zip(mails, lines)):
        first, start = i * length, HEAD_AT[i] * rows
        hid_ref[first : first + rows, :] = mail[start : start + rows, :]
        if length <= 8 * rows:
            hid_ref[first + rows : first + length, :] = line[...]
        else:

            def one(k, carry, line=line, first=first + rows):
                hid_ref[pl.ds(pl.multiple_of(first + k * rows, rows), rows), :] = line[
                    pl.ds(pl.multiple_of(k * rows, rows), rows), :
                ]
                return carry

            lax.fori_loop(0, length // rows - 1, one, 0)

    def base(block):
        per = total // (16 * rows)
        way, along, within = block // (4 * per), (block // per) % 4, block % per
        other = (way >> 1) | ((way & 1) << 1) | ((16 - 4 * along) & 15)
        return (me ^ (other | (reverse_bits(within, per.bit_length() - 1) << 4))) * rows

    def embed(hidden):
        raw = dot(hidden, wb)
        scale = lax.rsqrt(jnp.mean(raw * raw, axis=-1, keepdims=True) + EPS)
        return raw, scale, (raw * scale).astype(BF)

    def through(grad, raw, scale):
        along = jnp.sum(grad * raw, axis=-1, keepdims=True)
        return (scale * grad - scale * scale * scale * (1.0 / width) * along * raw).astype(BF)

    big, small = mask_ref.shape[1], 4 * rows

    def over_rows(step):
        if big == total:
            step(0)
        else:
            lax.fori_loop(0, total // big, lambda i, carry: (step(i), carry)[1], 0)

    def at(start, length):
        return pl.ds(pl.multiple_of(start, rows), length)

    wanted = []
    for ref, start in feats:
        code = ref[start + 2 * rows : start + end, :rows].astype(F32)
        wanted.append(columns_of(code[0:1] * 128.0 + code[1:2], rows))
    lanes = lax.broadcasted_iota(jnp.int32, (rows, rows), 1)
    smat_ref[...] = jnp.zeros_like(smat_ref)
    pick_ref[...] = jnp.zeros_like(pick_ref)

    def first_pass(step):
        for i in range(big // small):
            here = at(step * big + i * small, small)
            raw, _, back = embed(hid_ref[here, :])
            raw_ref[here, :] = raw
            back_ref[here, :] = back
        for t in range(big // rows):
            ids = (lanes + base(step * (big // rows) + t)).astype(F32)
            for g, want in enumerate(wanted):
                mask_ref[g * rows : (g + 1) * rows, t * rows : (t + 1) * rows] = jnp.where(
                    want == ids, 1.0, 0.0
                ).astype(BF)
        here = at(step * big, big)
        smat_ref[...] += dot_t(back_ref[here, :], back_ref[here, :])
        pick_ref[...] += dot(mask_ref[...], hid_ref[here, :])

    over_rows(first_pass)
    smat = smat_ref[...]
    s_hi, s_lo = halves(smat)
    place = reverse_bits(me & 15, 4)
    quarter, mine = place >> 2, place & 3
    half = wbq_ref.shape[0]
    columns = pl.ds(pl.multiple_of((quarter >> 1) * half, half), half)

    def rows_of(places, offset):
        return jnp.concatenate([ref[at + offset : at + offset + rows, :] for ref, at in places], axis=0)

    feat = rows_of(feats, 0)
    f32feat = feat.astype(F32)
    diff = f32feat - GAMMA * rows_of(feats, rows).astype(F32)
    d_hi, d_lo = halves(diff)
    kmat = dot_t(d_hi, feat) + dot_t(d_lo, feat)
    hidden = pick_ref[...].astype(BF)
    own_ref[...] = hidden
    raw, scale, back = embed(hidden)
    ob = back.astype(F32)
    ds = dot(d_hi, s_hi) + dot(d_lo, s_hi) + dot(d_hi, s_lo)
    db = jnp.sum(diff * ob, axis=-1, keepdims=True)
    coef = db * (1.0 / pairs) + 1.0 / total
    norm = jnp.sum(ob * ob, axis=-1, keepdims=True)
    grad_f = (ds * (1.0 / pairs) - coef * ob).astype(BF)
    wfq_ref[...] = dot_t(rows_of(cuts, 0), grad_f)
    squares = jnp.sum(diff * ds) - jnp.sum(db * db)
    squares = squares + LAMBDA * (jnp.sum(smat * smat) / groups - jnp.sum(norm * norm))
    sums = squares / (2.0 * pairs) - (jnp.sum(f32feat * ob) + LAMBDA * jnp.sum(norm)) / total
    grad_own = through(
        -coef * f32feat - (norm * (2.0 * LAMBDA / pairs) + 2.0 * LAMBDA / total) * ob, raw, scale
    )
    wbq_ref[...] = dot_t(own_ref[:, columns], grad_own)
    a_hi, a_lo = halves((kmat + (2.0 * LAMBDA / groups) * smat) * (1.0 / pairs))

    def second_pass(step):
        for i in range(big // small):
            here = at(step * big + i * small, small)
            raw = raw_ref[here, :]
            scale = lax.rsqrt(jnp.mean(raw * raw, axis=-1, keepdims=True) + EPS)
            back = back_ref[here, :]
            back_ref[here, :] = through(dot(back, a_hi) + dot(back, a_lo), raw, scale)
        here = at(step * big, big)
        wbq_ref[...] += dot_t(hid_ref[here, columns], back_ref[here, :])

    over_rows(second_pass)
    wf_rows = wfq_ref.shape[0] // 4
    wb_rows = wbq_ref.shape[0] // 8
    size = wf_rows + wb_rows

    def block(t):
        return (
            wfq_ref[pl.ds(pl.multiple_of(t * wf_rows, wf_rows), wf_rows), :],
            wbq_ref[pl.ds(pl.multiple_of(((quarter & 1) * 4 + t) * wb_rows, wb_rows), wb_rows), :],
        )

    keep_ref[:wf_rows, :], keep_ref[wf_rows:size, :] = block(mine)
    note = jnp.full((PAD, width), sums, F32)
    keep_ref[size:, :] = note
    line = lax.broadcasted_iota(jnp.int32, (PAD, width), 0)
    n_hi = note.astype(BF)
    n_mid, n_lo = halves(note - n_hi.astype(F32))
    coded = jnp.where(
        line == 0,
        n_hi.astype(F32),
        jnp.where(line == 1, n_mid.astype(F32), jnp.where(line == 2, n_lo.astype(F32), 0.0)),
    ).astype(BF)
    for ref, (_, turn) in zip(sends, LINE):
        part_f, part_b = block(mine ^ turn)
        ref[:wf_rows, :] = part_f.astype(BF)
        ref[wf_rows:size, :] = part_b.astype(BF)
        ref[size:, :] = coded


def add_kernel(keep_ref, *refs):
    sum_ref, note_ref = refs[3:]
    size, width = sum_ref.shape
    total = keep_ref[:size, :]
    note = keep_ref[size : size + 1, :1]
    for ref in refs[:3]:
        total = total + ref[:size, :].astype(F32)
        coded = ref[size:, :].astype(F32)
        note = note + (coded[0:1, :1] + coded[1:2, :1] + coded[2:3, :1])
    sum_ref[...] = total.astype(sum_ref.dtype)
    note_ref[...] = note * (1.0 / width)


def assemble_kernel(me_ref, *refs, wf_rows, wb_rows, factor_f, factor_b):
    place = reverse_bits(me_ref[0] & 15, 4)
    wf_ref, wb_ref = refs[2:]
    for offset, ref in zip((0, 8), refs):
        for e, turn in enumerate(TURNS):
            to = place ^ (offset + turn)
            wf_ref[pl.ds(pl.multiple_of(to * wf_rows, wf_rows), wf_rows), :] = (
                ref[e, :wf_rows, :].astype(F32) * factor_f
            )
            wb_ref[pl.ds(pl.multiple_of(to * wb_rows, wb_rows), wb_rows), :] = (
                ref[e, wf_rows:, :].astype(F32) * factor_b
            )


SMEM = pl.BlockSpec(memory_space=pltpu.SMEM)
VMEM = pl.BlockSpec(memory_space=pltpu.VMEM)
HBM = pl.BlockSpec(memory_space=pltpu.HBM)


def body(hidden_f, hidden_t, hidden_b, w_f, w_t, w_b, latents, latent_ids, positives):
    rows, high = hidden_f.shape
    wide = hidden_b.shape[1]
    width = w_f.shape[1]
    size = lax.axis_size("fa")
    bits = size.bit_length() - 1
    beyond = [1 << k for k in range(4, bits)]
    me = lax.axis_index("fa")
    total = size * rows
    assert bits >= 4 and size == 1 << bits and high // 4 == width == wide

    me = me.astype(jnp.int32).reshape(1)
    ends = [(at + 2) * rows + PAD for at in FEAT_AT]
    far, near, cut, head, wb_copy = pl.pallas_call(
        feature_kernel,
        in_specs=[SMEM] + [HBM] * 9,
        out_specs=[VMEM] * 5,
        out_shape=[
            jax.ShapeDtypeStruct((ends[1], width), BF),
            jax.ShapeDtypeStruct((ends[2], width), BF),
            jax.ShapeDtypeStruct((rows, width), BF),
            jax.ShapeDtypeStruct(hidden_b.shape, BF),
            jax.ShapeDtypeStruct(w_b.shape, BF),
        ],
        scratch_shapes=[
            pltpu.VMEM(hidden_f.shape, BF),
            pltpu.VMEM(hidden_t.shape, BF),
            pltpu.VMEM(w_f.shape, BF),
            pltpu.VMEM(w_t.shape, BF),
            pltpu.VMEM(latents.shape, BF),
            pltpu.VMEM((1, rows), jnp.int32),
            pltpu.VMEM((1, rows), jnp.int32),
            pltpu.SemaphoreType.DMA((9,)),
        ],
        compiler_params=pltpu.CompilerParams(vmem_limit_bytes=60 * 2**20),
        cost_estimate=pl.CostEstimate(
            flops=4 * rows * high * width, bytes_accessed=4 * high * (rows + width), transcendentals=0
        ),
    )(
        me,
        hidden_f,
        hidden_t,
        hidden_b,
        w_f,
        w_t,
        w_b,
        latents,
        latent_ids.reshape(1, rows),
        positives.reshape(1, rows),
    )
    for mask in reversed(beyond):
        head = jnp.concatenate([head, swap(head, mask, size)], axis=0)
    line = [head[rows:]] * (len(beyond) > 0) + [swap(head, mask, size) for mask, _ in LINE]
    far2 = swap(far, 2, size)
    line0 = pack(*line, after=far2)
    line2 = swap(line0, 2, size)
    near1 = swap(near, 1, size)
    far3 = swap(far2, 1, size)
    line1 = swap(line0, 1, size)
    line3 = swap(line2, 1, size)

    wf_rows, wb_rows = high // 16, wide // 16
    each = wf_rows + wb_rows
    keep, *sends = pl.pallas_call(
        functools.partial(pair_kernel, rows=rows, total=total),
        in_specs=[SMEM] + [VMEM] * 10,
        out_specs=[VMEM] * 4,
        out_shape=[jax.ShapeDtypeStruct((each + PAD, width), F32)]
        + [jax.ShapeDtypeStruct((each + PAD, width), BF)] * 3,
        scratch_shapes=[
            pltpu.VMEM((total, wide), BF),
            pltpu.VMEM((total, width), F32),
            pltpu.VMEM((total, width), BF),
            pltpu.VMEM((4 * rows, min(total, 16 * rows)), BF),
            pltpu.VMEM((width, width), F32),
            pltpu.VMEM((4 * rows, wide), F32),
            pltpu.VMEM((4 * rows, wide), BF),
            pltpu.VMEM((width, width), F32),
            pltpu.VMEM((wide // 2, width), F32),
        ],
        compiler_params=pltpu.CompilerParams(vmem_limit_bytes=15 * 2**20 + total * width * 10),
    )(me, near, far2, near1, far3, line0, line2, line1, line3, cut, wb_copy)

    got = [swap(part, mask, size) for part, (mask, _) in zip(sends, LINE)]
    result, note = pl.pallas_call(
        add_kernel,
        in_specs=[VMEM] * 4,
        out_specs=[VMEM] * 2,
        out_shape=[
            jax.ShapeDtypeStruct((each, width), F32 if beyond else BF),
            jax.ShapeDtypeStruct((1, 1), F32),
        ],
        compiler_params=pltpu.CompilerParams(vmem_limit_bytes=8 * 2**20),
    )(keep, *got)
    for mask in beyond:
        result = result + swap(result, mask, size)
        note = note + swap(note, mask, size)
    result = result.astype(BF).reshape(1, each, width)
    pieces = [result] + [swap(result, mask, size) for mask, _ in LINE]
    near = jnp.concatenate(pieces + [swap(piece, 2, size) for piece in pieces], axis=0)
    far = swap(near, 1, size)
    grad_wf, grad_wb = pl.pallas_call(
        functools.partial(
            assemble_kernel,
            wf_rows=wf_rows,
            wb_rows=wb_rows,
            factor_f=math.sqrt(high),
            factor_b=math.sqrt(wide),
        ),
        in_specs=[SMEM] + [VMEM] * 2,
        out_specs=[VMEM] * 2,
        out_shape=[
            jax.ShapeDtypeStruct((high, width), F32),
            jax.ShapeDtypeStruct((wide, width), F32),
        ],
        compiler_params=pltpu.CompilerParams(vmem_limit_bytes=16 * 2**20),
    )(me, near, far)
    return (grad_wf, grad_wb, note.reshape(1))


def solution(mesh):
    placed = (
        P(("grp", "fa"), None),
        P(("grp", "fa"), None),
        P(("grp", "fa"), None),
        P(),
        P(),
        P(),
        P("grp", None),
        P(("grp", "fa")),
        P(("grp", "fa")),
    )
    return jax.shard_map(
        body,
        mesh=mesh,
        in_specs=placed,
        out_specs=(P("grp", None), P("grp", None), P("grp")),
        check_vma=False,
    )
```

```python
import functools
import math

import jax
import jax.numpy as jnp
from jax import lax
from jax.experimental import pallas as pl
from jax.experimental.pallas import tpu as pltpu
from jax.sharding import PartitionSpec as P

GAMMA = 0.98
LAMBDA = 1.0
EPS = 1e-06
BF = jnp.bfloat16
F32 = jnp.float32
GROUP = (0, 2, 1, 3)
CUT_AT = (0, 0, 0, 1)
HEAD_AT = (1, 2, 1, 2)
FEAT_AT = (2, 3, 2, 3)
PAD = 16
LINE = ((12, 3), (8, 1), (4, 2))
TURNS = (0, 2, 1, 3, 4, 6, 5, 7)


def dot(left, right):
    return jnp.dot(left, right, preferred_element_type=F32)


def dot_t(left, right):
    return lax.dot_general(left, right, (((0,), (0,)), ((), ())), preferred_element_type=F32)


def halves(array):
    high = array.astype(BF)
    return high, (array - high.astype(F32)).astype(BF)


def swap(array, mask, size):
    return lax.ppermute(array, "fa", [(i, i ^ mask) for i in range(size)])


def reverse_bits(value, bits):
    out = value * 0
    for k in range(bits):
        out = out + (((value >> k) & 1) << (bits - 1 - k))
    return out


def columns_of(row, rows):
    return jnp.transpose(jnp.broadcast_to(row, (rows, rows)))


def feature_kernel(
    me_ref,
    hf_hbm,
    ht_hbm,
    hb_hbm,
    wf_hbm,
    wt_hbm,
    wb_hbm,
    lat_hbm,
    ids_hbm,
    pos_hbm,
    far_ref,
    near_ref,
    cut_ref,
    head_ref,
    wb_ref,
    hf,
    ht,
    wf,
    wt,
    lat,
    ids,
    pos,
    sems,
):
    rows = hf.shape[0]
    width = wf.shape[1]
    moves = [
        pltpu.make_async_copy(source, target, sems.at[k])
        for k, (source, target) in enumerate(
            (
                (ids_hbm, ids),
                (pos_hbm, pos),
                (lat_hbm, lat),
                (hf_hbm, hf),
                (wf_hbm, wf),
                (ht_hbm, ht),
                (wt_hbm, wt),
                (hb_hbm, head_ref),
                (wb_hbm, wb_ref),
            )
        )
    ]
    for move in moves:
        move.start()
    for move in moves[:3]:
        move.wait()
    who = columns_of(ids[...].astype(F32), rows)
    lanes = lax.broadcasted_iota(jnp.int32, (rows, rows), 1).astype(F32)
    tiles = [
        jnp.where(who == lanes + float(t * rows), 1.0, 0.0).astype(BF) for t in range(lat.shape[0] // rows)
    ]
    zrows = dot(jnp.concatenate(tiles, axis=1), lat[...])
    place = pos[...]
    line = lax.broadcasted_iota(jnp.int32, (PAD, rows), 0)
    high = jnp.broadcast_to(lax.shift_right_logical(place, 7).astype(F32), (PAD, rows))
    low = jnp.broadcast_to((place & 127).astype(F32), (PAD, rows))
    coded = jnp.where(line == 0, high, jnp.where(line == 1, low, 0.0)).astype(BF)
    coded = jnp.concatenate([coded] + [jnp.zeros((PAD, width - rows), BF)] * (width > rows), axis=1)

    def piece(slot):
        other = me_ref[0] ^ GROUP[slot]
        quarter = (other & 1) * 2 + ((other >> 1) & 1)
        return hf[:, pl.ds(pl.multiple_of(quarter * width, width), width)]

    moves[3].wait()
    cut_ref[...] = piece(0)
    far_ref[:rows, :] = piece(1)
    near_ref[:rows, :] = piece(2)
    far_ref[rows : 2 * rows, :] = piece(3)
    moves[4].wait()
    feat = (dot(hf[...], wf[...]) + zrows).astype(BF)
    moves[5].wait()
    moves[6].wait()
    feat_t = (dot(ht[...], wt[...]) + zrows).astype(BF)
    moves[7].wait()
    head = head_ref[...]
    for ref, at in ((far_ref, HEAD_AT[1]), (near_ref, HEAD_AT[2])):
        ref[at * rows : (at + 1) * rows, :] = head
        ref[(at + 1) * rows : (at + 2) * rows, :] = feat
        ref[(at + 2) * rows : (at + 3) * rows, :] = feat_t
        ref[(at + 3) * rows :, :] = coded
    moves[8].wait()


def pack_kernel(*refs):
    at = 0
    for ref in refs[:-2]:
        refs[-1][at : at + ref.shape[0], :] = ref[...]
        at = at + ref.shape[0]


def pack(*arrays, after):
    return pl.pallas_call(
        pack_kernel,
        in_specs=[VMEM] * (len(arrays) + 1),
        out_specs=VMEM,
        out_shape=jax.ShapeDtypeStruct((sum(x.shape[0] for x in arrays), arrays[0].shape[1]), BF),
        compiler_params=pltpu.CompilerParams(vmem_limit_bytes=20 * 2**20),
    )(*arrays, after)


def pair_kernel(*refs, rows, total):
    me_ref = refs[0]
    mails, lines, cut_ref, wb_ref = refs[1:5], refs[5:9], refs[9], refs[10]
    keep_ref, sends = refs[11], refs[12:15]
    hid_ref, raw_ref, back_ref, mask_ref, smat_ref, pick_ref, own_ref, wfq_ref, wbq_ref = refs[15:]
    width = wb_ref.shape[1]
    pairs = float(total * (total - 1))
    groups = total // (4 * rows)
    wb = wb_ref[...]
    end = 2 * rows + PAD
    me = me_ref[0]
    feats = [(ref, at * rows) for ref, at in zip(mails, FEAT_AT)]
    cuts = [(ref, at * rows) for ref, at in zip((cut_ref,) + mails[1:], CUT_AT)]
    length = total // 4
    for i, (mail, line) in enumerate(zip(mails, lines)):
        first, start = i * length, HEAD_AT[i] * rows
        hid_ref[first : first + rows, :] = mail[start : start + rows, :]
        if length <= 8 * rows:
            hid_ref[first + rows : first + length, :] = line[...]
        else:

            def one(k, carry, line=line, first=first + rows):
                hid_ref[pl.ds(pl.multiple_of(first + k * rows, rows), rows), :] = line[
                    pl.ds(pl.multiple_of(k * rows, rows), rows), :
                ]
                return carry

            lax.fori_loop(0, length // rows - 1, one, 0)

    def base(block):
        per = total // (16 * rows)
        way, along, within = block // (4 * per), (block // per) % 4, block % per
        other = (way >> 1) | ((way & 1) << 1) | ((16 - 4 * along) & 15)
        return (me ^ (other | (reverse_bits(within, per.bit_length() - 1) << 4))) * rows

    def embed(hidden):
        raw = dot(hidden, wb)
        scale = lax.rsqrt(jnp.mean(raw * raw, axis=-1, keepdims=True) + EPS)
        return raw, scale, (raw * scale).astype(BF)

    def through(grad, raw, scale):
        along = jnp.sum(grad * raw, axis=-1, keepdims=True)
        return (scale * grad - scale * scale * scale * (1.0 / width) * along * raw).astype(BF)

    big, small = mask_ref.shape[1], 4 * rows

    def over_rows(step):
        if big == total:
            step(0)
        else:
            lax.fori_loop(0, total // big, lambda i, carry: (step(i), carry)[1], 0)

    def at(start, length):
        return pl.ds(pl.multiple_of(start, rows), length)

    wanted = []
    for ref, start in feats:
        code = ref[start + 2 * rows : start + end, :rows].astype(F32)
        wanted.append(columns_of(code[0:1] * 128.0 + code[1:2], rows))
    lanes = lax.broadcasted_iota(jnp.int32, (rows, rows), 1)
    smat_ref[...] = jnp.zeros_like(smat_ref)
    pick_ref[...] = jnp.zeros_like(pick_ref)

    def first_pass(step):
        for i in range(big // small):
            here = at(step * big + i * small, small)
            raw, _, back = embed(hid_ref[here, :])
            raw_ref[here, :] = raw
            back_ref[here, :] = back
        for t in range(big // rows):
            ids = (lanes + base(step * (big // rows) + t)).astype(F32)
            for g, want in enumerate(wanted):
                mask_ref[g * rows : (g + 1) * rows, t * rows : (t + 1) * rows] = jnp.where(
                    want == ids, 1.0, 0.0
                ).astype(BF)
        here = at(step * big, big)
        smat_ref[...] += dot_t(back_ref[here, :], back_ref[here, :])
        pick_ref[...] += dot(mask_ref[...], hid_ref[here, :])

    over_rows(first_pass)
    smat = smat_ref[...]
    s_hi, s_lo = halves(smat)
    place = reverse_bits(me & 15, 4)
    quarter, mine = place >> 2, place & 3
    half = wbq_ref.shape[0]
    columns = pl.ds(pl.multiple_of((quarter >> 1) * half, half), half)

    def rows_of(places, offset):
        return jnp.concatenate([ref[at + offset : at + offset + rows, :] for ref, at in places], axis=0)

    feat = rows_of(feats, 0)
    f32feat = feat.astype(F32)
    diff = f32feat - GAMMA * rows_of(feats, rows).astype(F32)
    d_hi, d_lo = halves(diff)
    kmat = dot_t(d_hi, feat) + dot_t(d_lo, feat)
    hidden = pick_ref[...].astype(BF)
    own_ref[...] = hidden
    raw, scale, back = embed(hidden)
    ob = back.astype(F32)
    ds = dot(d_hi, s_hi) + dot(d_lo, s_hi) + dot(d_hi, s_lo)
    db = jnp.sum(diff * ob, axis=-1, keepdims=True)
    coef = db * (1.0 / pairs) + 1.0 / total
    norm = jnp.sum(ob * ob, axis=-1, keepdims=True)
    grad_f = (ds * (1.0 / pairs) - coef * ob).astype(BF)
    wfq_ref[...] = dot_t(rows_of(cuts, 0), grad_f)
    squares = jnp.sum(diff * ds) - jnp.sum(db * db)
    squares = squares + LAMBDA * (jnp.sum(smat * smat) / groups - jnp.sum(norm * norm))
    sums = squares / (2.0 * pairs) - (jnp.sum(f32feat * ob) + LAMBDA * jnp.sum(norm)) / total
    grad_own = through(
        -coef * f32feat - (norm * (2.0 * LAMBDA / pairs) + 2.0 * LAMBDA / total) * ob, raw, scale
    )
    wbq_ref[...] = dot_t(own_ref[:, columns], grad_own)
    a_hi, a_lo = halves((kmat + (2.0 * LAMBDA / groups) * smat) * (1.0 / pairs))

    def second_pass(step):
        for i in range(big // small):
            here = at(step * big + i * small, small)
            raw = raw_ref[here, :]
            scale = lax.rsqrt(jnp.mean(raw * raw, axis=-1, keepdims=True) + EPS)
            back = back_ref[here, :]
            back_ref[here, :] = through(dot(back, a_hi) + dot(back, a_lo), raw, scale)
        here = at(step * big, big)
        wbq_ref[...] += dot_t(hid_ref[here, columns], back_ref[here, :])

    over_rows(second_pass)
    wf_rows = wfq_ref.shape[0] // 4
    wb_rows = wbq_ref.shape[0] // 8
    size = wf_rows + wb_rows

    def block(t):
        return (
            wfq_ref[pl.ds(pl.multiple_of(t * wf_rows, wf_rows), wf_rows), :],
            wbq_ref[pl.ds(pl.multiple_of(((quarter & 1) * 4 + t) * wb_rows, wb_rows), wb_rows), :],
        )

    keep_ref[:wf_rows, :], keep_ref[wf_rows:size, :] = block(mine)
    note = jnp.full((PAD, width), sums, F32)
    keep_ref[size:, :] = note
    line = lax.broadcasted_iota(jnp.int32, (PAD, width), 0)
    n_hi = note.astype(BF)
    n_mid, n_lo = halves(note - n_hi.astype(F32))
    coded = jnp.where(
        line == 0,
        n_hi.astype(F32),
        jnp.where(line == 1, n_mid.astype(F32), jnp.where(line == 2, n_lo.astype(F32), 0.0)),
    ).astype(BF)
    for ref, (_, turn) in zip(sends, LINE):
        part_f, part_b = block(mine ^ turn)
        ref[:wf_rows, :] = part_f.astype(BF)
        ref[wf_rows:size, :] = part_b.astype(BF)
        ref[size:, :] = coded


def add_kernel(keep_ref, *refs):
    sum_ref, note_ref = refs[3:]
    size, width = sum_ref.shape
    total = keep_ref[:size, :]
    note = keep_ref[size : size + 1, :1]
    for ref in refs[:3]:
        total = total + ref[:size, :].astype(F32)
        coded = ref[size:, :].astype(F32)
        note = note + (coded[0:1, :1] + coded[1:2, :1] + coded[2:3, :1])
    sum_ref[...] = total.astype(sum_ref.dtype)
    note_ref[...] = note * (1.0 / width)


def assemble_kernel(me_ref, *refs, wf_rows, wb_rows, factor_f, factor_b):
    place = reverse_bits(me_ref[0] & 15, 4)
    wf_ref, wb_ref = refs[2:]
    for offset, ref in zip((0, 8), refs):
        for e, turn in enumerate(TURNS):
            to = place ^ (offset + turn)
            wf_ref[pl.ds(pl.multiple_of(to * wf_rows, wf_rows), wf_rows), :] = (
                ref[e, :wf_rows, :].astype(F32) * factor_f
            )
            wb_ref[pl.ds(pl.multiple_of(to * wb_rows, wb_rows), wb_rows), :] = (
                ref[e, wf_rows:, :].astype(F32) * factor_b
            )


SMEM = pl.BlockSpec(memory_space=pltpu.SMEM)
VMEM = pl.BlockSpec(memory_space=pltpu.VMEM)
HBM = pl.BlockSpec(memory_space=pltpu.HBM)


def body(hidden_f, hidden_t, hidden_b, w_f, w_t, w_b, latents, latent_ids, positives):
    rows, high = hidden_f.shape
    wide = hidden_b.shape[1]
    width = w_f.shape[1]
    size = lax.axis_size("fa")
    bits = size.bit_length() - 1
    beyond = [1 << k for k in range(4, bits)]
    me = lax.axis_index("fa")
    total = size * rows
    assert bits >= 4 and size == 1 << bits and high // 4 == width == wide

    me = me.astype(jnp.int32).reshape(1)
    ends = [(at + 2) * rows + PAD for at in FEAT_AT]
    far, near, cut, head, wb_copy = pl.pallas_call(
        feature_kernel,
        in_specs=[SMEM] + [HBM] * 9,
        out_specs=[VMEM] * 5,
        out_shape=[
            jax.ShapeDtypeStruct((ends[1], width), BF),
            jax.ShapeDtypeStruct((ends[2], width), BF),
            jax.ShapeDtypeStruct((rows, width), BF),
            jax.ShapeDtypeStruct(hidden_b.shape, BF),
            jax.ShapeDtypeStruct(w_b.shape, BF),
        ],
        scratch_shapes=[
            pltpu.VMEM(hidden_f.shape, BF),
            pltpu.VMEM(hidden_t.shape, BF),
            pltpu.VMEM(w_f.shape, BF),
            pltpu.VMEM(w_t.shape, BF),
            pltpu.VMEM(latents.shape, BF),
            pltpu.VMEM((1, rows), jnp.int32),
            pltpu.VMEM((1, rows), jnp.int32),
            pltpu.SemaphoreType.DMA((9,)),
        ],
        compiler_params=pltpu.CompilerParams(vmem_limit_bytes=60 * 2**20),
        cost_estimate=pl.CostEstimate(
            flops=4 * rows * high * width, bytes_accessed=4 * high * (rows + width), transcendentals=0
        ),
    )(
        me,
        hidden_f,
        hidden_t,
        hidden_b,
        w_f,
        w_t,
        w_b,
        latents,
        latent_ids.reshape(1, rows),
        positives.reshape(1, rows),
    )
    for mask in reversed(beyond):
        head = jnp.concatenate([head, swap(head, mask, size)], axis=0)
    line = [head[rows:]] * (len(beyond) > 0) + [swap(head, mask, size) for mask, _ in LINE]
    far2 = swap(far, 2, size)
    over = [swap(piece, 2, size) for piece in line[-2:]]
    gated = pack(*line[:-2], after=far2)
    line = [gated] + line[-2:]
    over = [swap(gated, 2, size)] + over
    near1 = swap(near, 1, size)
    far3 = swap(far2, 1, size)
    line0, line2 = [jnp.concatenate(part, axis=0) for part in (line, over)]
    line1 = swap(line0, 1, size)
    line3 = swap(line2, 1, size)

    wf_rows, wb_rows = high // 16, wide // 16
    each = wf_rows + wb_rows
    keep, *sends = pl.pallas_call(
        functools.partial(pair_kernel, rows=rows, total=total),
        in_specs=[SMEM] + [VMEM] * 10,
        out_specs=[VMEM] * 4,
        out_shape=[jax.ShapeDtypeStruct((each + PAD, width), F32)]
        + [jax.ShapeDtypeStruct((each + PAD, width), BF)] * 3,
        scratch_shapes=[
            pltpu.VMEM((total, wide), BF),
            pltpu.VMEM((total, width), F32),
            pltpu.VMEM((total, width), BF),
            pltpu.VMEM((4 * rows, min(total, 16 * rows)), BF),
            pltpu.VMEM((width, width), F32),
            pltpu.VMEM((4 * rows, wide), F32),
            pltpu.VMEM((4 * rows, wide), BF),
            pltpu.VMEM((width, width), F32),
            pltpu.VMEM((wide // 2, width), F32),
        ],
        compiler_params=pltpu.CompilerParams(vmem_limit_bytes=15 * 2**20 + total * width * 10),
    )(me, near, far2, near1, far3, line0, line2, line1, line3, cut, wb_copy)

    got = [swap(part, mask, size) for part, (mask, _) in zip(sends, LINE)]
    result, note = pl.pallas_call(
        add_kernel,
        in_specs=[VMEM] * 4,
        out_specs=[VMEM] * 2,
        out_shape=[
            jax.ShapeDtypeStruct((each, width), F32 if beyond else BF),
            jax.ShapeDtypeStruct((1, 1), F32),
        ],
        compiler_params=pltpu.CompilerParams(vmem_limit_bytes=8 * 2**20),
    )(keep, *got)
    for mask in beyond:
        result = result + swap(result, mask, size)
        note = note + swap(note, mask, size)
    result = result.astype(BF).reshape(1, each, width)
    pieces = [result] + [swap(result, mask, size) for mask, _ in reversed(LINE)]
    near = jnp.concatenate(pieces + [swap(piece, 2, size) for piece in pieces], axis=0)
    far = swap(near, 1, size)
    grad_wf, grad_wb = pl.pallas_call(
        functools.partial(
            assemble_kernel,
            wf_rows=wf_rows,
            wb_rows=wb_rows,
            factor_f=math.sqrt(high),
            factor_b=math.sqrt(wide),
        ),
        in_specs=[SMEM] + [VMEM] * 2,
        out_specs=[VMEM] * 2,
        out_shape=[
            jax.ShapeDtypeStruct((high, width), F32),
            jax.ShapeDtypeStruct((wide, width), F32),
        ],
        compiler_params=pltpu.CompilerParams(vmem_limit_bytes=16 * 2**20),
    )(me, near, far)
    return (grad_wf, grad_wb, note.reshape(1))


def solution(mesh):
    placed = (
        P(("grp", "fa"), None),
        P(("grp", "fa"), None),
        P(("grp", "fa"), None),
        P(),
        P(),
        P(),
        P("grp", None),
        P(("grp", "fa")),
        P(("grp", "fa")),
    )
    return jax.shard_map(
        body,
        mesh=mesh,
        in_specs=placed,
        out_specs=(P("grp", None), P("grp", None), P("grp")),
        check_vma=False,
    )
```

```python
import functools
import math

import jax
import jax.numpy as jnp
from jax import lax
from jax.experimental import pallas as pl
from jax.experimental.pallas import tpu as pltpu
from jax.sharding import PartitionSpec as P

GAMMA = 0.98
LAMBDA = 1.0
EPS = 1e-06
BF = jnp.bfloat16
F32 = jnp.float32
GROUP = (0, 2, 1, 3)
CUT_AT = (0, 0, 0, 1)
HEAD_AT = (1, 2, 1, 2)
FEAT_AT = (2, 3, 2, 3)
PAD = 16
LINE = ((12, 3), (8, 1), (4, 2))
TURNS = (0, 4, 2, 1, 3, 6, 5, 7)


def dot(left, right):
    return jnp.dot(left, right, preferred_element_type=F32)


def dot_t(left, right):
    return lax.dot_general(left, right, (((0,), (0,)), ((), ())), preferred_element_type=F32)


def halves(array):
    high = array.astype(BF)
    return high, (array - high.astype(F32)).astype(BF)


def swap(array, mask, size):
    return lax.ppermute(array, "fa", [(i, i ^ mask) for i in range(size)])


def reverse_bits(value, bits):
    out = value * 0
    for k in range(bits):
        out = out + (((value >> k) & 1) << (bits - 1 - k))
    return out


def columns_of(row, rows):
    return jnp.transpose(jnp.broadcast_to(row, (rows, rows)))


def feature_kernel(
    me_ref,
    hf_hbm,
    ht_hbm,
    hb_hbm,
    wf_hbm,
    wt_hbm,
    wb_hbm,
    lat_hbm,
    ids_hbm,
    pos_hbm,
    far_ref,
    near_ref,
    cut_ref,
    head_ref,
    wb_ref,
    hf,
    ht,
    wf,
    wt,
    lat,
    ids,
    pos,
    sems,
):
    rows = hf.shape[0]
    width = wf.shape[1]
    moves = [
        pltpu.make_async_copy(source, target, sems.at[k])
        for k, (source, target) in enumerate(
            (
                (ids_hbm, ids),
                (pos_hbm, pos),
                (lat_hbm, lat),
                (hf_hbm, hf),
                (wf_hbm, wf),
                (ht_hbm, ht),
                (wt_hbm, wt),
                (hb_hbm, head_ref),
                (wb_hbm, wb_ref),
            )
        )
    ]
    for move in moves:
        move.start()
    for move in moves[:3]:
        move.wait()
    who = columns_of(ids[...].astype(F32), rows)
    lanes = lax.broadcasted_iota(jnp.int32, (rows, rows), 1).astype(F32)
    tiles = [
        jnp.where(who == lanes + float(t * rows), 1.0, 0.0).astype(BF) for t in range(lat.shape[0] // rows)
    ]
    zrows = dot(jnp.concatenate(tiles, axis=1), lat[...])
    place = pos[...]
    line = lax.broadcasted_iota(jnp.int32, (PAD, rows), 0)
    high = jnp.broadcast_to(lax.shift_right_logical(place, 7).astype(F32), (PAD, rows))
    low = jnp.broadcast_to((place & 127).astype(F32), (PAD, rows))
    coded = jnp.where(line == 0, high, jnp.where(line == 1, low, 0.0)).astype(BF)
    coded = jnp.concatenate([coded] + [jnp.zeros((PAD, width - rows), BF)] * (width > rows), axis=1)

    def piece(slot):
        other = me_ref[0] ^ GROUP[slot]
        quarter = (other & 1) * 2 + ((other >> 1) & 1)
        return hf[:, pl.ds(pl.multiple_of(quarter * width, width), width)]

    moves[3].wait()
    cut_ref[...] = piece(0)
    far_ref[:rows, :] = piece(1)
    near_ref[:rows, :] = piece(2)
    far_ref[rows : 2 * rows, :] = piece(3)
    moves[4].wait()
    feat = (dot(hf[...], wf[...]) + zrows).astype(BF)
    moves[5].wait()
    moves[6].wait()
    feat_t = (dot(ht[...], wt[...]) + zrows).astype(BF)
    moves[7].wait()
    head = head_ref[...]
    for ref, at in ((far_ref, HEAD_AT[1]), (near_ref, HEAD_AT[2])):
        ref[at * rows : (at + 1) * rows, :] = head
        ref[(at + 1) * rows : (at + 2) * rows, :] = feat
        ref[(at + 2) * rows : (at + 3) * rows, :] = feat_t
        ref[(at + 3) * rows :, :] = coded
    moves[8].wait()


def pack_kernel(*refs):
    at = 0
    for ref in refs[:-2]:
        refs[-1][at : at + ref.shape[0], :] = ref[...]
        at = at + ref.shape[0]


def pack(*arrays, after):
    return pl.pallas_call(
        pack_kernel,
        in_specs=[VMEM] * (len(arrays) + 1),
        out_specs=VMEM,
        out_shape=jax.ShapeDtypeStruct((sum(x.shape[0] for x in arrays), arrays[0].shape[1]), BF),
        compiler_params=pltpu.CompilerParams(vmem_limit_bytes=20 * 2**20),
    )(*arrays, after)


def pair_kernel(*refs, rows, total):
    me_ref = refs[0]
    mails, lines, cut_ref, wb_ref = refs[1:5], refs[5:9], refs[9], refs[10]
    keep_ref, sends = refs[11], refs[12:15]
    hid_ref, raw_ref, back_ref, mask_ref, smat_ref, pick_ref, own_ref, wfq_ref, wbq_ref = refs[15:]
    width = wb_ref.shape[1]
    pairs = float(total * (total - 1))
    groups = total // (4 * rows)
    wb = wb_ref[...]
    end = 2 * rows + PAD
    me = me_ref[0]
    feats = [(ref, at * rows) for ref, at in zip(mails, FEAT_AT)]
    cuts = [(ref, at * rows) for ref, at in zip((cut_ref,) + mails[1:], CUT_AT)]
    length = total // 4
    for i, (mail, line) in enumerate(zip(mails, lines)):
        first, start = i * length, HEAD_AT[i] * rows
        hid_ref[first : first + rows, :] = mail[start : start + rows, :]
        if length <= 8 * rows:
            hid_ref[first + rows : first + length, :] = line[...]
        else:

            def one(k, carry, line=line, first=first + rows):
                hid_ref[pl.ds(pl.multiple_of(first + k * rows, rows), rows), :] = line[
                    pl.ds(pl.multiple_of(k * rows, rows), rows), :
                ]
                return carry

            lax.fori_loop(0, length // rows - 1, one, 0)

    def base(block):
        per = total // (16 * rows)
        way, along, within = block // (4 * per), (block // per) % 4, block % per
        other = (way >> 1) | ((way & 1) << 1) | (4 * along)
        return (me ^ (other | (reverse_bits(within, per.bit_length() - 1) << 4))) * rows

    def embed(hidden):
        raw = dot(hidden, wb)
        scale = lax.rsqrt(jnp.mean(raw * raw, axis=-1, keepdims=True) + EPS)
        return raw, scale, (raw * scale).astype(BF)

    def through(grad, raw, scale):
        along = jnp.sum(grad * raw, axis=-1, keepdims=True)
        return (scale * grad - scale * scale * scale * (1.0 / width) * along * raw).astype(BF)

    big, small = mask_ref.shape[1], 4 * rows

    def over_rows(step):
        if big == total:
            step(0)
        else:
            lax.fori_loop(0, total // big, lambda i, carry: (step(i), carry)[1], 0)

    def at(start, length):
        return pl.ds(pl.multiple_of(start, rows), length)

    wanted = []
    for ref, start in feats:
        code = ref[start + 2 * rows : start + end, :rows].astype(F32)
        wanted.append(columns_of(code[0:1] * 128.0 + code[1:2], rows))
    lanes = lax.broadcasted_iota(jnp.int32, (rows, rows), 1)
    smat_ref[...] = jnp.zeros_like(smat_ref)
    pick_ref[...] = jnp.zeros_like(pick_ref)

    def first_pass(step):
        for i in range(big // small):
            here = at(step * big + i * small, small)
            raw, _, back = embed(hid_ref[here, :])
            raw_ref[here, :] = raw
            back_ref[here, :] = back
        for t in range(big // rows):
            ids = (lanes + base(step * (big // rows) + t)).astype(F32)
            for g, want in enumerate(wanted):
                mask_ref[g * rows : (g + 1) * rows, t * rows : (t + 1) * rows] = jnp.where(
                    want == ids, 1.0, 0.0
                ).astype(BF)
        here = at(step * big, big)
        smat_ref[...] += dot_t(back_ref[here, :], back_ref[here, :])
        pick_ref[...] += dot(mask_ref[...], hid_ref[here, :])

    over_rows(first_pass)
    smat = smat_ref[...]
    s_hi, s_lo = halves(smat)
    place = reverse_bits(me & 15, 4)
    quarter, mine = place >> 2, place & 3
    half = wbq_ref.shape[0]
    columns = pl.ds(pl.multiple_of((quarter >> 1) * half, half), half)

    def rows_of(places, offset):
        return jnp.concatenate([ref[at + offset : at + offset + rows, :] for ref, at in places], axis=0)

    feat = rows_of(feats, 0)
    f32feat = feat.astype(F32)
    diff = f32feat - GAMMA * rows_of(feats, rows).astype(F32)
    d_hi, d_lo = halves(diff)
    kmat = dot_t(d_hi, feat) + dot_t(d_lo, feat)
    hidden = pick_ref[...].astype(BF)
    own_ref[...] = hidden
    raw, scale, back = embed(hidden)
    ob = back.astype(F32)
    ds = dot(d_hi, s_hi) + dot(d_lo, s_hi) + dot(d_hi, s_lo)
    db = jnp.sum(diff * ob, axis=-1, keepdims=True)
    coef = db * (1.0 / pairs) + 1.0 / total
    norm = jnp.sum(ob * ob, axis=-1, keepdims=True)
    grad_f = (ds * (1.0 / pairs) - coef * ob).astype(BF)
    wfq_ref[...] = dot_t(rows_of(cuts, 0), grad_f)
    squares = jnp.sum(diff * ds) - jnp.sum(db * db)
    squares = squares + LAMBDA * (jnp.sum(smat * smat) / groups - jnp.sum(norm * norm))
    sums = squares / (2.0 * pairs) - (jnp.sum(f32feat * ob) + LAMBDA * jnp.sum(norm)) / total
    grad_own = through(
        -coef * f32feat - (norm * (2.0 * LAMBDA / pairs) + 2.0 * LAMBDA / total) * ob, raw, scale
    )
    wbq_ref[...] = dot_t(own_ref[:, columns], grad_own)
    a_hi, a_lo = halves((kmat + (2.0 * LAMBDA / groups) * smat) * (1.0 / pairs))

    def second_pass(step):
        for i in range(big // small):
            here = at(step * big + i * small, small)
            raw = raw_ref[here, :]
            scale = lax.rsqrt(jnp.mean(raw * raw, axis=-1, keepdims=True) + EPS)
            back = back_ref[here, :]
            back_ref[here, :] = through(dot(back, a_hi) + dot(back, a_lo), raw, scale)
        here = at(step * big, big)
        wbq_ref[...] += dot_t(hid_ref[here, columns], back_ref[here, :])

    over_rows(second_pass)
    wf_rows = wfq_ref.shape[0] // 4
    wb_rows = wbq_ref.shape[0] // 8
    size = wf_rows + wb_rows

    def block(t):
        return (
            wfq_ref[pl.ds(pl.multiple_of(t * wf_rows, wf_rows), wf_rows), :],
            wbq_ref[pl.ds(pl.multiple_of(((quarter & 1) * 4 + t) * wb_rows, wb_rows), wb_rows), :],
        )

    keep_ref[:wf_rows, :], keep_ref[wf_rows:size, :] = block(mine)
    note = jnp.full((PAD, width), sums, F32)
    keep_ref[size:, :] = note
    line = lax.broadcasted_iota(jnp.int32, (PAD, width), 0)
    n_hi = note.astype(BF)
    n_mid, n_lo = halves(note - n_hi.astype(F32))
    coded = jnp.where(
        line == 0,
        n_hi.astype(F32),
        jnp.where(line == 1, n_mid.astype(F32), jnp.where(line == 2, n_lo.astype(F32), 0.0)),
    ).astype(BF)
    for ref, (_, turn) in zip(sends, LINE):
        part_f, part_b = block(mine ^ turn)
        ref[:wf_rows, :] = part_f.astype(BF)
        ref[wf_rows:size, :] = part_b.astype(BF)
        ref[size:, :] = coded


def add_kernel(keep_ref, *refs):
    sum_ref, note_ref = refs[3:]
    size, width = sum_ref.shape
    total = keep_ref[:size, :]
    note = keep_ref[size : size + 1, :1]
    for ref in refs[:3]:
        total = total + ref[:size, :].astype(F32)
        coded = ref[size:, :].astype(F32)
        note = note + (coded[0:1, :1] + coded[1:2, :1] + coded[2:3, :1])
    sum_ref[...] = total.astype(sum_ref.dtype)
    note_ref[...] = note * (1.0 / width)


def assemble_kernel(me_ref, *refs, wf_rows, wb_rows, factor_f, factor_b):
    place = reverse_bits(me_ref[0] & 15, 4)
    wf_ref, wb_ref = refs[2:]
    for offset, ref in zip((0, 8), refs):
        for e, turn in enumerate(TURNS):
            to = place ^ (offset + turn)
            wf_ref[pl.ds(pl.multiple_of(to * wf_rows, wf_rows), wf_rows), :] = (
                ref[e, :wf_rows, :].astype(F32) * factor_f
            )
            wb_ref[pl.ds(pl.multiple_of(to * wb_rows, wb_rows), wb_rows), :] = (
                ref[e, wf_rows:, :].astype(F32) * factor_b
            )


SMEM = pl.BlockSpec(memory_space=pltpu.SMEM)
VMEM = pl.BlockSpec(memory_space=pltpu.VMEM)
HBM = pl.BlockSpec(memory_space=pltpu.HBM)


def body(hidden_f, hidden_t, hidden_b, w_f, w_t, w_b, latents, latent_ids, positives):
    rows, high = hidden_f.shape
    wide = hidden_b.shape[1]
    width = w_f.shape[1]
    size = lax.axis_size("fa")
    bits = size.bit_length() - 1
    beyond = [1 << k for k in range(4, bits)]
    me = lax.axis_index("fa")
    total = size * rows
    assert bits >= 4 and size == 1 << bits and high // 4 == width == wide

    me = me.astype(jnp.int32).reshape(1)
    ends = [(at + 2) * rows + PAD for at in FEAT_AT]
    far, near, cut, head, wb_copy = pl.pallas_call(
        feature_kernel,
        in_specs=[SMEM] + [HBM] * 9,
        out_specs=[VMEM] * 5,
        out_shape=[
            jax.ShapeDtypeStruct((ends[1], width), BF),
            jax.ShapeDtypeStruct((ends[2], width), BF),
            jax.ShapeDtypeStruct((rows, width), BF),
            jax.ShapeDtypeStruct(hidden_b.shape, BF),
            jax.ShapeDtypeStruct(w_b.shape, BF),
        ],
        scratch_shapes=[
            pltpu.VMEM(hidden_f.shape, BF),
            pltpu.VMEM(hidden_t.shape, BF),
            pltpu.VMEM(w_f.shape, BF),
            pltpu.VMEM(w_t.shape, BF),
            pltpu.VMEM(latents.shape, BF),
            pltpu.VMEM((1, rows), jnp.int32),
            pltpu.VMEM((1, rows), jnp.int32),
            pltpu.SemaphoreType.DMA((9,)),
        ],
        compiler_params=pltpu.CompilerParams(vmem_limit_bytes=60 * 2**20),
        cost_estimate=pl.CostEstimate(
            flops=4 * rows * high * width, bytes_accessed=4 * high * (rows + width), transcendentals=0
        ),
    )(
        me,
        hidden_f,
        hidden_t,
        hidden_b,
        w_f,
        w_t,
        w_b,
        latents,
        latent_ids.reshape(1, rows),
        positives.reshape(1, rows),
    )
    for mask in reversed(beyond):
        head = jnp.concatenate([head, swap(head, mask, size)], axis=0)
    line = [swap(head, mask, size) for mask, _ in reversed(LINE)]
    line = [head[rows:]] * (len(beyond) > 0) + line
    far2 = swap(far, 2, size)
    over = [swap(piece, 2, size) for piece in line[-2:]]
    gated = pack(*line[:-2], after=far2)
    line = [gated] + line[-2:]
    over = [swap(gated, 2, size)] + over
    near1 = swap(near, 1, size)
    far3 = swap(far2, 1, size)
    line0, line2 = [jnp.concatenate(part, axis=0) for part in (line, over)]
    line1 = swap(line0, 1, size)
    line3 = swap(line2, 1, size)

    wf_rows, wb_rows = high // 16, wide // 16
    each = wf_rows + wb_rows
    keep, *sends = pl.pallas_call(
        functools.partial(pair_kernel, rows=rows, total=total),
        in_specs=[SMEM] + [VMEM] * 10,
        out_specs=[VMEM] * 4,
        out_shape=[jax.ShapeDtypeStruct((each + PAD, width), F32)]
        + [jax.ShapeDtypeStruct((each + PAD, width), BF)] * 3,
        scratch_shapes=[
            pltpu.VMEM((total, wide), BF),
            pltpu.VMEM((total, width), F32),
            pltpu.VMEM((total, width), BF),
            pltpu.VMEM((4 * rows, min(total, 16 * rows)), BF),
            pltpu.VMEM((width, width), F32),
            pltpu.VMEM((4 * rows, wide), F32),
            pltpu.VMEM((4 * rows, wide), BF),
            pltpu.VMEM((width, width), F32),
            pltpu.VMEM((wide // 2, width), F32),
        ],
        compiler_params=pltpu.CompilerParams(vmem_limit_bytes=15 * 2**20 + total * width * 10),
    )(me, near, far2, near1, far3, line0, line2, line1, line3, cut, wb_copy)

    got = [swap(part, mask, size) for part, (mask, _) in zip(sends, LINE)]
    result, note = pl.pallas_call(
        add_kernel,
        in_specs=[VMEM] * 4,
        out_specs=[VMEM] * 2,
        out_shape=[
            jax.ShapeDtypeStruct((each, width), F32 if beyond else BF),
            jax.ShapeDtypeStruct((1, 1), F32),
        ],
        compiler_params=pltpu.CompilerParams(vmem_limit_bytes=8 * 2**20),
    )(keep, *got)
    for mask in beyond:
        result = result + swap(result, mask, size)
        note = note + swap(note, mask, size)
    result = result.astype(BF).reshape(1, each, width)
    pieces = [swap(result, mask, size) for mask, _ in reversed(LINE)]
    near = [result, swap(result, 2, size)] + pieces + [swap(piece, 2, size) for piece in pieces]
    near = jnp.concatenate(near, axis=0)
    far = swap(near, 1, size)
    grad_wf, grad_wb = pl.pallas_call(
        functools.partial(
            assemble_kernel,
            wf_rows=wf_rows,
            wb_rows=wb_rows,
            factor_f=math.sqrt(high),
            factor_b=math.sqrt(wide),
        ),
        in_specs=[SMEM] + [VMEM] * 2,
        out_specs=[VMEM] * 2,
        out_shape=[
            jax.ShapeDtypeStruct((high, width), F32),
            jax.ShapeDtypeStruct((wide, width), F32),
        ],
        compiler_params=pltpu.CompilerParams(vmem_limit_bytes=16 * 2**20),
    )(me, near, far)
    return (grad_wf, grad_wb, note.reshape(1))


def solution(mesh):
    placed = (
        P(("grp", "fa"), None),
        P(("grp", "fa"), None),
        P(("grp", "fa"), None),
        P(),
        P(),
        P(),
        P("grp", None),
        P(("grp", "fa")),
        P(("grp", "fa")),
    )
    return jax.shard_map(
        body,
        mesh=mesh,
        in_specs=placed,
        out_specs=(P("grp", None), P("grp", None), P("grp")),
        check_vma=False,
    )
```

```python
import functools
import math

import jax
import jax.numpy as jnp
from jax import lax
from jax.experimental import pallas as pl
from jax.experimental.pallas import tpu as pltpu
from jax.sharding import PartitionSpec as P

GAMMA = 0.98
LAMBDA = 1.0
EPS = 1e-06
BF = jnp.bfloat16
F32 = jnp.float32
GROUP = (0, 2, 1, 3)
CUT_AT = (0, 0, 0, 1)
HEAD_AT = (1, 2, 1, 2)
FEAT_AT = (2, 3, 2, 3)
PAD = 16
LINE = ((12, 3), (8, 1), (4, 2))
TURNS = (0, 4, 2, 1, 3, 6, 5, 7)


def dot(left, right):
    return jnp.dot(left, right, preferred_element_type=F32)


def dot_t(left, right):
    return lax.dot_general(left, right, (((0,), (0,)), ((), ())), preferred_element_type=F32)


def halves(array):
    high = array.astype(BF)
    return high, (array - high.astype(F32)).astype(BF)


def swap(array, mask, size):
    return lax.ppermute(array, "fa", [(i, i ^ mask) for i in range(size)])


def reverse_bits(value, bits):
    out = value * 0
    for k in range(bits):
        out = out + (((value >> k) & 1) << (bits - 1 - k))
    return out


def columns_of(row, rows):
    return jnp.transpose(jnp.broadcast_to(row, (rows, rows)))


def feature_kernel(
    me_ref,
    hf_hbm,
    ht_hbm,
    hb_hbm,
    wf_hbm,
    wt_hbm,
    wb_hbm,
    lat_hbm,
    ids_hbm,
    pos_hbm,
    far_ref,
    near_ref,
    cut_ref,
    head_ref,
    wb_ref,
    hf,
    ht,
    wf,
    wt,
    lat,
    ids,
    pos,
    sems,
):
    rows = hf.shape[0]
    width = wf.shape[1]
    moves = [
        pltpu.make_async_copy(source, target, sems.at[k])
        for k, (source, target) in enumerate(
            (
                (ids_hbm, ids),
                (pos_hbm, pos),
                (lat_hbm, lat),
                (hf_hbm, hf),
                (wf_hbm, wf),
                (ht_hbm, ht),
                (wt_hbm, wt),
                (hb_hbm, head_ref),
                (wb_hbm, wb_ref),
            )
        )
    ]
    for move in moves:
        move.start()
    for move in moves[:3]:
        move.wait()
    who = columns_of(ids[...].astype(F32), rows)
    lanes = lax.broadcasted_iota(jnp.int32, (rows, rows), 1).astype(F32)
    tiles = [
        jnp.where(who == lanes + float(t * rows), 1.0, 0.0).astype(BF) for t in range(lat.shape[0] // rows)
    ]
    zrows = dot(jnp.concatenate(tiles, axis=1), lat[...])
    place = pos[...]
    line = lax.broadcasted_iota(jnp.int32, (PAD, rows), 0)
    high = jnp.broadcast_to(lax.shift_right_logical(place, 7).astype(F32), (PAD, rows))
    low = jnp.broadcast_to((place & 127).astype(F32), (PAD, rows))
    coded = jnp.where(line == 0, high, jnp.where(line == 1, low, 0.0)).astype(BF)
    coded = jnp.concatenate([coded] + [jnp.zeros((PAD, width - rows), BF)] * (width > rows), axis=1)

    def piece(slot):
        other = me_ref[0] ^ GROUP[slot]
        quarter = (other & 1) * 2 + ((other >> 1) & 1)
        return hf[:, pl.ds(pl.multiple_of(quarter * width, width), width)]

    moves[3].wait()
    cut_ref[...] = piece(0)
    far_ref[:rows, :] = piece(1)
    near_ref[:rows, :] = piece(2)
    far_ref[rows : 2 * rows, :] = piece(3)
    moves[4].wait()
    feat = (dot(hf[...], wf[...]) + zrows).astype(BF)
    moves[5].wait()
    moves[6].wait()
    feat_t = (dot(ht[...], wt[...]) + zrows).astype(BF)
    moves[7].wait()
    head = head_ref[...]
    for ref, at in ((far_ref, HEAD_AT[1]), (near_ref, HEAD_AT[2])):
        ref[at * rows : (at + 1) * rows, :] = head
        ref[(at + 1) * rows : (at + 2) * rows, :] = feat
        ref[(at + 2) * rows : (at + 3) * rows, :] = feat_t
        ref[(at + 3) * rows :, :] = coded
    moves[8].wait()


def pack_kernel(*refs):
    at = 0
    for ref in refs[:-2]:
        refs[-1][at : at + ref.shape[0], :] = ref[...]
        at = at + ref.shape[0]


def pack(*arrays, after):
    return pl.pallas_call(
        pack_kernel,
        in_specs=[VMEM] * (len(arrays) + 1),
        out_specs=VMEM,
        out_shape=jax.ShapeDtypeStruct((sum(x.shape[0] for x in arrays), arrays[0].shape[1]), BF),
        compiler_params=pltpu.CompilerParams(vmem_limit_bytes=20 * 2**20),
    )(*arrays, after)


def pair_kernel(*refs, rows, total):
    me_ref = refs[0]
    mails, lines, cut_ref, wb_ref = refs[1:5], refs[5:9], refs[9], refs[10]
    keep_ref, sends = refs[11], refs[12:15]
    hid_ref, raw_ref, back_ref, mask_ref, smat_ref, pick_ref, own_ref, wfq_ref, wbq_ref = refs[15:]
    width = wb_ref.shape[1]
    pairs = float(total * (total - 1))
    groups = total // (4 * rows)
    wb = wb_ref[...]
    end = 2 * rows + PAD
    me = me_ref[0]
    feats = [(ref, at * rows) for ref, at in zip(mails, FEAT_AT)]
    cuts = [(ref, at * rows) for ref, at in zip((cut_ref,) + mails[1:], CUT_AT)]
    length = total // 4
    for i, (mail, line) in enumerate(zip(mails, lines)):
        first, start = i * length, HEAD_AT[i] * rows
        hid_ref[first : first + rows, :] = mail[start : start + rows, :]
        if length <= 8 * rows:
            hid_ref[first + rows : first + length, :] = line[...]
        else:

            def one(k, carry, line=line, first=first + rows):
                hid_ref[pl.ds(pl.multiple_of(first + k * rows, rows), rows), :] = line[
                    pl.ds(pl.multiple_of(k * rows, rows), rows), :
                ]
                return carry

            lax.fori_loop(0, length // rows - 1, one, 0)

    def base(block):
        per = total // (16 * rows)
        way, along, within = block // (4 * per), (block // per) % 4, block % per
        other = (way >> 1) | ((way & 1) << 1) | (4 * along)
        return (me ^ (other | (reverse_bits(within, per.bit_length() - 1) << 4))) * rows

    def embed(hidden):
        raw = dot(hidden, wb)
        scale = lax.rsqrt(jnp.mean(raw * raw, axis=-1, keepdims=True) + EPS)
        return raw, scale, (raw * scale).astype(BF)

    def through(grad, raw, scale):
        along = jnp.sum(grad * raw, axis=-1, keepdims=True)
        return (scale * grad - scale * scale * scale * (1.0 / width) * along * raw).astype(BF)

    big, small = mask_ref.shape[1], 4 * rows

    def over_rows(step):
        if big == total:
            step(0)
        else:
            lax.fori_loop(0, total // big, lambda i, carry: (step(i), carry)[1], 0)

    def at(start, length):
        return pl.ds(pl.multiple_of(start, rows), length)

    wanted = []
    for ref, start in feats:
        code = ref[start + 2 * rows : start + end, :rows].astype(F32)
        wanted.append(columns_of(code[0:1] * 128.0 + code[1:2], rows))
    lanes = lax.broadcasted_iota(jnp.int32, (rows, rows), 1)
    smat_ref[...] = jnp.zeros_like(smat_ref)
    pick_ref[...] = jnp.zeros_like(pick_ref)

    def first_pass(step):
        for i in range(big // small):
            here = at(step * big + i * small, small)
            raw, _, back = embed(hid_ref[here, :])
            raw_ref[here, :] = raw
            back_ref[here, :] = back
        for t in range(big // rows):
            ids = (lanes + base(step * (big // rows) + t)).astype(F32)
            for g, want in enumerate(wanted):
                mask_ref[g * rows : (g + 1) * rows, t * rows : (t + 1) * rows] = jnp.where(
                    want == ids, 1.0, 0.0
                ).astype(BF)
        here = at(step * big, big)
        smat_ref[...] += dot_t(back_ref[here, :], back_ref[here, :])
        pick_ref[...] += dot(mask_ref[...], hid_ref[here, :])

    over_rows(first_pass)
    smat = smat_ref[...]
    s_hi, s_lo = halves(smat)
    place = reverse_bits(me & 15, 4)
    quarter, mine = place >> 2, place & 3
    half = wbq_ref.shape[0]
    columns = pl.ds(pl.multiple_of((quarter >> 1) * half, half), half)

    def rows_of(places, offset):
        return jnp.concatenate([ref[at + offset : at + offset + rows, :] for ref, at in places], axis=0)

    feat = rows_of(feats, 0)
    f32feat = feat.astype(F32)
    diff = f32feat - GAMMA * rows_of(feats, rows).astype(F32)
    d_hi, d_lo = halves(diff)
    kmat = dot_t(d_hi, feat) + dot_t(d_lo, feat)
    hidden = pick_ref[...].astype(BF)
    own_ref[...] = hidden
    raw, scale, back = embed(hidden)
    ob = back.astype(F32)
    ds = dot(d_hi, s_hi) + dot(d_lo, s_hi) + dot(d_hi, s_lo)
    db = jnp.sum(diff * ob, axis=-1, keepdims=True)
    coef = db * (1.0 / pairs) + 1.0 / total
    norm = jnp.sum(ob * ob, axis=-1, keepdims=True)
    grad_f = (ds * (1.0 / pairs) - coef * ob).astype(BF)
    wfq_ref[...] = dot_t(rows_of(cuts, 0), grad_f)
    squares = jnp.sum(diff * ds) - jnp.sum(db * db)
    squares = squares + LAMBDA * (jnp.sum(smat * smat) / groups - jnp.sum(norm * norm))
    sums = squares / (2.0 * pairs) - (jnp.sum(f32feat * ob) + LAMBDA * jnp.sum(norm)) / total
    grad_own = through(
        -coef * f32feat - (norm * (2.0 * LAMBDA / pairs) + 2.0 * LAMBDA / total) * ob, raw, scale
    )
    wbq_ref[...] = dot_t(own_ref[:, columns], grad_own)
    a_hi, a_lo = halves((kmat + (2.0 * LAMBDA / groups) * smat) * (1.0 / pairs))

    def second_pass(step):
        for i in range(big // small):
            here = at(step * big + i * small, small)
            raw = raw_ref[here, :]
            scale = lax.rsqrt(jnp.mean(raw * raw, axis=-1, keepdims=True) + EPS)
            back = back_ref[here, :]
            back_ref[here, :] = through(dot(back, a_hi) + dot(back, a_lo), raw, scale)
        here = at(step * big, big)
        wbq_ref[...] += dot_t(hid_ref[here, columns], back_ref[here, :])

    over_rows(second_pass)
    wf_rows = wfq_ref.shape[0] // 4
    wb_rows = wbq_ref.shape[0] // 8
    size = wf_rows + wb_rows

    def block(t):
        return (
            wfq_ref[pl.ds(pl.multiple_of(t * wf_rows, wf_rows), wf_rows), :],
            wbq_ref[pl.ds(pl.multiple_of(((quarter & 1) * 4 + t) * wb_rows, wb_rows), wb_rows), :],
        )

    keep_ref[:wf_rows, :], keep_ref[wf_rows:size, :] = block(mine)
    note = jnp.full((PAD, width), sums, F32)
    keep_ref[size:, :] = note
    line = lax.broadcasted_iota(jnp.int32, (PAD, width), 0)
    n_hi = note.astype(BF)
    n_mid, n_lo = halves(note - n_hi.astype(F32))
    coded = jnp.where(
        line == 0,
        n_hi.astype(F32),
        jnp.where(line == 1, n_mid.astype(F32), jnp.where(line == 2, n_lo.astype(F32), 0.0)),
    ).astype(BF)
    for ref, (_, turn) in zip(sends, LINE):
        part_f, part_b = block(mine ^ turn)
        ref[:wf_rows, :] = part_f.astype(BF)
        ref[wf_rows:size, :] = part_b.astype(BF)
        ref[size:, :] = coded


def add_kernel(keep_ref, *refs):
    sum_ref, note_ref = refs[3:]
    size, width = sum_ref.shape
    total = keep_ref[:size, :]
    note = keep_ref[size : size + 1, :1]
    for ref in refs[:3]:
        total = total + ref[:size, :].astype(F32)
        coded = ref[size:, :].astype(F32)
        note = note + (coded[0:1, :1] + coded[1:2, :1] + coded[2:3, :1])
    sum_ref[...] = total.astype(sum_ref.dtype)
    note_ref[...] = note * (1.0 / width)


def assemble_kernel(me_ref, part_ref, *refs, offset, wf_rows, wb_rows, factor_f, factor_b):
    wf_hbm, wb_hbm, wf_buf, wb_buf, sems = refs[-5:]
    place = reverse_bits(me_ref[0] & 15, 4) ^ offset
    moves = []
    for e, turn in enumerate(TURNS):
        to = place ^ turn
        wf_buf[e] = part_ref[e, :wf_rows, :].astype(F32) * factor_f
        wb_buf[e] = part_ref[e, wf_rows:, :].astype(F32) * factor_b
        for k, (buf, hbm, rows) in enumerate(((wf_buf, wf_hbm, wf_rows), (wb_buf, wb_hbm, wb_rows))):
            move = pltpu.make_async_copy(
                buf.at[e], hbm.at[pl.ds(pl.multiple_of(to * rows, rows), rows), :], sems.at[2 * e + k]
            )
            move.start()
            moves.append(move)
    for move in moves:
        move.wait()


SMEM = pl.BlockSpec(memory_space=pltpu.SMEM)
VMEM = pl.BlockSpec(memory_space=pltpu.VMEM)
HBM = pl.BlockSpec(memory_space=pltpu.HBM)
ANY = pl.BlockSpec(memory_space=pl.ANY)


def body(hidden_f, hidden_t, hidden_b, w_f, w_t, w_b, latents, latent_ids, positives):
    rows, high = hidden_f.shape
    wide = hidden_b.shape[1]
    width = w_f.shape[1]
    size = lax.axis_size("fa")
    bits = size.bit_length() - 1
    beyond = [1 << k for k in range(4, bits)]
    me = lax.axis_index("fa")
    total = size * rows
    assert bits >= 4 and size == 1 << bits and high // 4 == width == wide

    me = me.astype(jnp.int32).reshape(1)
    ends = [(at + 2) * rows + PAD for at in FEAT_AT]
    far, near, cut, head, wb_copy = pl.pallas_call(
        feature_kernel,
        in_specs=[SMEM] + [HBM] * 9,
        out_specs=[VMEM] * 5,
        out_shape=[
            jax.ShapeDtypeStruct((ends[1], width), BF),
            jax.ShapeDtypeStruct((ends[2], width), BF),
            jax.ShapeDtypeStruct((rows, width), BF),
            jax.ShapeDtypeStruct(hidden_b.shape, BF),
            jax.ShapeDtypeStruct(w_b.shape, BF),
        ],
        scratch_shapes=[
            pltpu.VMEM(hidden_f.shape, BF),
            pltpu.VMEM(hidden_t.shape, BF),
            pltpu.VMEM(w_f.shape, BF),
            pltpu.VMEM(w_t.shape, BF),
            pltpu.VMEM(latents.shape, BF),
            pltpu.VMEM((1, rows), jnp.int32),
            pltpu.VMEM((1, rows), jnp.int32),
            pltpu.SemaphoreType.DMA((9,)),
        ],
        compiler_params=pltpu.CompilerParams(vmem_limit_bytes=60 * 2**20),
        cost_estimate=pl.CostEstimate(
            flops=4 * rows * high * width, bytes_accessed=4 * high * (rows + width), transcendentals=0
        ),
    )(
        me,
        hidden_f,
        hidden_t,
        hidden_b,
        w_f,
        w_t,
        w_b,
        latents,
        latent_ids.reshape(1, rows),
        positives.reshape(1, rows),
    )
    for mask in reversed(beyond):
        head = jnp.concatenate([head, swap(head, mask, size)], axis=0)
    line = [swap(head, mask, size) for mask, _ in reversed(LINE)]
    line = [head[rows:]] * (len(beyond) > 0) + line
    far2 = swap(far, 2, size)
    over = [swap(piece, 2, size) for piece in line[-2:]]
    gated = pack(*line[:-2], after=far2)
    line = [gated] + line[-2:]
    over = [swap(gated, 2, size)] + over
    near1 = swap(near, 1, size)
    far3 = swap(far2, 1, size)
    line0, line2 = [jnp.concatenate(part, axis=0) for part in (line, over)]
    line1 = swap(line0, 1, size)
    line3 = swap(line2, 1, size)

    wf_rows, wb_rows = high // 16, wide // 16
    each = wf_rows + wb_rows
    keep, *sends = pl.pallas_call(
        functools.partial(pair_kernel, rows=rows, total=total),
        in_specs=[SMEM] + [VMEM] * 10,
        out_specs=[VMEM] * 4,
        out_shape=[jax.ShapeDtypeStruct((each + PAD, width), F32)]
        + [jax.ShapeDtypeStruct((each + PAD, width), BF)] * 3,
        scratch_shapes=[
            pltpu.VMEM((total, wide), BF),
            pltpu.VMEM((total, width), F32),
            pltpu.VMEM((total, width), BF),
            pltpu.VMEM((4 * rows, min(total, 16 * rows)), BF),
            pltpu.VMEM((width, width), F32),
            pltpu.VMEM((4 * rows, wide), F32),
            pltpu.VMEM((4 * rows, wide), BF),
            pltpu.VMEM((width, width), F32),
            pltpu.VMEM((wide // 2, width), F32),
        ],
        compiler_params=pltpu.CompilerParams(vmem_limit_bytes=15 * 2**20 + total * width * 10),
    )(me, near, far2, near1, far3, line0, line2, line1, line3, cut, wb_copy)

    got = [swap(part, mask, size) for part, (mask, _) in zip(sends, LINE)]
    result, note = pl.pallas_call(
        add_kernel,
        in_specs=[VMEM] * 4,
        out_specs=[VMEM] * 2,
        out_shape=[
            jax.ShapeDtypeStruct((each, width), F32 if beyond else BF),
            jax.ShapeDtypeStruct((1, 1), F32),
        ],
        compiler_params=pltpu.CompilerParams(vmem_limit_bytes=8 * 2**20),
    )(keep, *got)
    for mask in beyond:
        result = result + swap(result, mask, size)
        note = note + swap(note, mask, size)
    result = result.astype(BF).reshape(1, each, width)
    pieces = [swap(result, mask, size) for mask, _ in reversed(LINE)]
    near = [result, swap(result, 2, size)] + pieces + [swap(piece, 2, size) for piece in pieces]
    near = jnp.concatenate(near, axis=0)
    far = swap(near, 1, size)

    def assemble(part, offset, *begun):
        return pl.pallas_call(
            functools.partial(
                assemble_kernel,
                offset=offset,
                wf_rows=wf_rows,
                wb_rows=wb_rows,
                factor_f=math.sqrt(high),
                factor_b=math.sqrt(wide),
            ),
            in_specs=[SMEM, VMEM] + [ANY] * len(begun),
            out_specs=[ANY] * 2,
            out_shape=[
                jax.ShapeDtypeStruct((high, width), F32),
                jax.ShapeDtypeStruct((wide, width), F32),
            ],
            scratch_shapes=[
                pltpu.VMEM((8, wf_rows, width), F32),
                pltpu.VMEM((8, wb_rows, width), F32),
                pltpu.SemaphoreType.DMA((16,)),
            ],
            input_output_aliases={2 + k: k for k in range(len(begun))},
            compiler_params=pltpu.CompilerParams(vmem_limit_bytes=8 * 2**20),
        )(me, part, *begun)

    grad_wf, grad_wb = assemble(far, 8, *assemble(near, 0))
    return (grad_wf, grad_wb, note.reshape(1))


def solution(mesh):
    placed = (
        P(("grp", "fa"), None),
        P(("grp", "fa"), None),
        P(("grp", "fa"), None),
        P(),
        P(),
        P(),
        P("grp", None),
        P(("grp", "fa")),
        P(("grp", "fa")),
    )
    return jax.shard_map(
        body,
        mesh=mesh,
        in_specs=placed,
        out_specs=(P("grp", None), P("grp", None), P("grp")),
        check_vma=False,
    )
```

```python
import functools
import math

import jax
import jax.numpy as jnp
from jax import lax
from jax.experimental import pallas as pl
from jax.experimental.pallas import tpu as pltpu
from jax.sharding import PartitionSpec as P

GAMMA = 0.98
LAMBDA = 1.0
EPS = 1e-06
BF = jnp.bfloat16
F32 = jnp.float32
GROUP = (0, 2, 1, 3)
CUT_AT = (0, 0, 0, 1)
HEAD_AT = (1, 2, 1, 2)
FEAT_AT = (2, 3, 2, 3)
PAD = 16
LINE = ((12, 3), (8, 1), (4, 2))
TURNS = (2, 1, 3, 0, 6, 5, 7, 4)


def dot(left, right):
    return jnp.dot(left, right, preferred_element_type=F32)


def dot_t(left, right):
    return lax.dot_general(left, right, (((0,), (0,)), ((), ())), preferred_element_type=F32)


def halves(array):
    high = array.astype(BF)
    return high, (array - high.astype(F32)).astype(BF)


def swap(array, mask, size):
    return lax.ppermute(array, "fa", [(i, i ^ mask) for i in range(size)])


def reverse_bits(value, bits):
    out = value * 0
    for k in range(bits):
        out = out + (((value >> k) & 1) << (bits - 1 - k))
    return out


def columns_of(row, rows):
    return jnp.transpose(jnp.broadcast_to(row, (rows, rows)))


def feature_kernel(
    me_ref,
    hf_hbm,
    ht_hbm,
    hb_hbm,
    wf_hbm,
    wt_hbm,
    wb_hbm,
    lat_hbm,
    ids_hbm,
    pos_hbm,
    far_ref,
    near_ref,
    cut_ref,
    head_ref,
    wb_ref,
    hf,
    ht,
    wf,
    wt,
    lat,
    ids,
    pos,
    sems,
):
    rows = hf.shape[0]
    width = wf.shape[1]
    moves = [
        pltpu.make_async_copy(source, target, sems.at[k])
        for k, (source, target) in enumerate(
            (
                (ids_hbm, ids),
                (pos_hbm, pos),
                (lat_hbm, lat),
                (hf_hbm, hf),
                (wf_hbm, wf),
                (ht_hbm, ht),
                (wt_hbm, wt),
                (hb_hbm, head_ref),
                (wb_hbm, wb_ref),
            )
        )
    ]
    for move in moves:
        move.start()
    for move in moves[:3]:
        move.wait()
    who = columns_of(ids[...].astype(F32), rows)
    lanes = lax.broadcasted_iota(jnp.int32, (rows, rows), 1).astype(F32)
    tiles = [
        jnp.where(who == lanes + float(t * rows), 1.0, 0.0).astype(BF) for t in range(lat.shape[0] // rows)
    ]
    zrows = dot(jnp.concatenate(tiles, axis=1), lat[...])
    place = pos[...]
    line = lax.broadcasted_iota(jnp.int32, (PAD, rows), 0)
    high = jnp.broadcast_to(lax.shift_right_logical(place, 7).astype(F32), (PAD, rows))
    low = jnp.broadcast_to((place & 127).astype(F32), (PAD, rows))
    coded = jnp.where(line == 0, high, jnp.where(line == 1, low, 0.0)).astype(BF)
    coded = jnp.concatenate([coded] + [jnp.zeros((PAD, width - rows), BF)] * (width > rows), axis=1)

    def piece(slot):
        other = me_ref[0] ^ GROUP[slot]
        quarter = (other & 1) * 2 + ((other >> 1) & 1)
        return hf[:, pl.ds(pl.multiple_of(quarter * width, width), width)]

    moves[3].wait()
    cut_ref[...] = piece(0)
    far_ref[:rows, :] = piece(1)
    near_ref[:rows, :] = piece(2)
    far_ref[rows : 2 * rows, :] = piece(3)
    moves[4].wait()
    feat = (dot(hf[...], wf[...]) + zrows).astype(BF)
    moves[5].wait()
    moves[6].wait()
    feat_t = (dot(ht[...], wt[...]) + zrows).astype(BF)
    moves[7].wait()
    head = head_ref[...]
    for ref, at in ((far_ref, HEAD_AT[1]), (near_ref, HEAD_AT[2])):
        ref[at * rows : (at + 1) * rows, :] = head
        ref[(at + 1) * rows : (at + 2) * rows, :] = feat
        ref[(at + 2) * rows : (at + 3) * rows, :] = feat_t
        ref[(at + 3) * rows :, :] = coded
    moves[8].wait()


def pack_kernel(*refs):
    at = 0
    for ref in refs[:-2]:
        refs[-1][at : at + ref.shape[0], :] = ref[...]
        at = at + ref.shape[0]


def pack(*arrays, after):
    return pl.pallas_call(
        pack_kernel,
        in_specs=[VMEM] * (len(arrays) + 1),
        out_specs=VMEM,
        out_shape=jax.ShapeDtypeStruct((sum(x.shape[0] for x in arrays), arrays[0].shape[1]), BF),
        compiler_params=pltpu.CompilerParams(vmem_limit_bytes=20 * 2**20),
    )(*arrays, after)


def pair_kernel(*refs, rows, total):
    me_ref = refs[0]
    mails, lines, cut_ref, wb_ref = refs[1:5], refs[5:9], refs[9], refs[10]
    keep_ref, sends = refs[11], refs[12:15]
    hid_ref, raw_ref, back_ref, mask_ref, smat_ref, pick_ref, own_ref, wfq_ref, wbq_ref = refs[15:]
    width = wb_ref.shape[1]
    pairs = float(total * (total - 1))
    groups = total // (4 * rows)
    wb = wb_ref[...]
    end = 2 * rows + PAD
    me = me_ref[0]
    feats = [(ref, at * rows) for ref, at in zip(mails, FEAT_AT)]
    cuts = [(ref, at * rows) for ref, at in zip((cut_ref,) + mails[1:], CUT_AT)]
    length = total // 4
    for i, (mail, line) in enumerate(zip(mails, lines)):
        first, start = i * length, HEAD_AT[i] * rows
        hid_ref[first : first + rows, :] = mail[start : start + rows, :]
        if length <= 8 * rows:
            hid_ref[first + rows : first + length, :] = line[...]
        else:

            def one(k, carry, line=line, first=first + rows):
                hid_ref[pl.ds(pl.multiple_of(first + k * rows, rows), rows), :] = line[
                    pl.ds(pl.multiple_of(k * rows, rows), rows), :
                ]
                return carry

            lax.fori_loop(0, length // rows - 1, one, 0)

    def base(block):
        per = total // (16 * rows)
        way, along, within = block // (4 * per), (block // per) % 4, block % per
        other = (way >> 1) | ((way & 1) << 1) | (4 * along)
        return (me ^ (other | (reverse_bits(within, per.bit_length() - 1) << 4))) * rows

    def embed(hidden):
        raw = dot(hidden, wb)
        scale = lax.rsqrt(jnp.mean(raw * raw, axis=-1, keepdims=True) + EPS)
        return raw, scale, (raw * scale).astype(BF)

    def through(grad, raw, scale):
        along = jnp.sum(grad * raw, axis=-1, keepdims=True)
        return (scale * grad - scale * scale * scale * (1.0 / width) * along * raw).astype(BF)

    big, small = mask_ref.shape[1], 4 * rows

    def over_rows(step):
        if big == total:
            step(0)
        else:
            lax.fori_loop(0, total // big, lambda i, carry: (step(i), carry)[1], 0)

    def at(start, length):
        return pl.ds(pl.multiple_of(start, rows), length)

    wanted = []
    for ref, start in feats:
        code = ref[start + 2 * rows : start + end, :rows].astype(F32)
        wanted.append(columns_of(code[0:1] * 128.0 + code[1:2], rows))
    lanes = lax.broadcasted_iota(jnp.int32, (rows, rows), 1)
    smat_ref[...] = jnp.zeros_like(smat_ref)
    pick_ref[...] = jnp.zeros_like(pick_ref)

    def first_pass(step):
        for i in range(big // small):
            here = at(step * big + i * small, small)
            raw, _, back = embed(hid_ref[here, :])
            raw_ref[here, :] = raw
            back_ref[here, :] = back
        for t in range(big // rows):
            ids = (lanes + base(step * (big // rows) + t)).astype(F32)
            for g, want in enumerate(wanted):
                mask_ref[g * rows : (g + 1) * rows, t * rows : (t + 1) * rows] = jnp.where(
                    want == ids, 1.0, 0.0
                ).astype(BF)
        here = at(step * big, big)
        smat_ref[...] += dot_t(back_ref[here, :], back_ref[here, :])
        pick_ref[...] += dot(mask_ref[...], hid_ref[here, :])

    over_rows(first_pass)
    smat = smat_ref[...]
    s_hi, s_lo = halves(smat)
    place = reverse_bits(me & 15, 4)
    quarter, mine = place >> 2, place & 3
    half = wbq_ref.shape[0]
    columns = pl.ds(pl.multiple_of((quarter >> 1) * half, half), half)

    def rows_of(places, offset):
        return jnp.concatenate([ref[at + offset : at + offset + rows, :] for ref, at in places], axis=0)

    feat = rows_of(feats, 0)
    f32feat = feat.astype(F32)
    diff = f32feat - GAMMA * rows_of(feats, rows).astype(F32)
    d_hi, d_lo = halves(diff)
    kmat = dot_t(d_hi, feat) + dot_t(d_lo, feat)
    hidden = pick_ref[...].astype(BF)
    own_ref[...] = hidden
    raw, scale, back = embed(hidden)
    ob = back.astype(F32)
    ds = dot(d_hi, s_hi) + dot(d_lo, s_hi) + dot(d_hi, s_lo)
    db = jnp.sum(diff * ob, axis=-1, keepdims=True)
    coef = db * (1.0 / pairs) + 1.0 / total
    norm = jnp.sum(ob * ob, axis=-1, keepdims=True)
    grad_f = (ds * (1.0 / pairs) - coef * ob).astype(BF)
    wfq_ref[...] = dot_t(rows_of(cuts, 0), grad_f)
    squares = jnp.sum(diff * ds) - jnp.sum(db * db)
    squares = squares + LAMBDA * (jnp.sum(smat * smat) / groups - jnp.sum(norm * norm))
    sums = squares / (2.0 * pairs) - (jnp.sum(f32feat * ob) + LAMBDA * jnp.sum(norm)) / total
    grad_own = through(
        -coef * f32feat - (norm * (2.0 * LAMBDA / pairs) + 2.0 * LAMBDA / total) * ob, raw, scale
    )
    wbq_ref[...] = dot_t(own_ref[:, columns], grad_own)
    a_hi, a_lo = halves((kmat + (2.0 * LAMBDA / groups) * smat) * (1.0 / pairs))

    def second_pass(step):
        for i in range(big // small):
            here = at(step * big + i * small, small)
            raw = raw_ref[here, :]
            scale = lax.rsqrt(jnp.mean(raw * raw, axis=-1, keepdims=True) + EPS)
            back = back_ref[here, :]
            back_ref[here, :] = through(dot(back, a_hi) + dot(back, a_lo), raw, scale)
        here = at(step * big, big)
        wbq_ref[...] += dot_t(hid_ref[here, columns], back_ref[here, :])

    over_rows(second_pass)
    wf_rows = wfq_ref.shape[0] // 4
    wb_rows = wbq_ref.shape[0] // 8
    size = wf_rows + wb_rows

    def block(t):
        return (
            wfq_ref[pl.ds(pl.multiple_of(t * wf_rows, wf_rows), wf_rows), :],
            wbq_ref[pl.ds(pl.multiple_of(((quarter & 1) * 4 + t) * wb_rows, wb_rows), wb_rows), :],
        )

    keep_ref[:wf_rows, :], keep_ref[wf_rows:size, :] = block(mine)
    note = jnp.full((PAD, width), sums, F32)
    keep_ref[size:, :] = note
    line = lax.broadcasted_iota(jnp.int32, (PAD, width), 0)
    n_hi = note.astype(BF)
    n_mid, n_lo = halves(note - n_hi.astype(F32))
    coded = jnp.where(
        line == 0,
        n_hi.astype(F32),
        jnp.where(line == 1, n_mid.astype(F32), jnp.where(line == 2, n_lo.astype(F32), 0.0)),
    ).astype(BF)
    for ref, (_, turn) in zip(sends, LINE):
        part_f, part_b = block(mine ^ turn)
        ref[:wf_rows, :] = part_f.astype(BF)
        ref[wf_rows:size, :] = part_b.astype(BF)
        ref[size:, :] = coded


def add_kernel(keep_ref, *refs):
    sum_ref, note_ref = refs[3:]
    size, width = sum_ref.shape
    total = keep_ref[:size, :]
    note = keep_ref[size : size + 1, :1]
    for ref in refs[:3]:
        total = total + ref[:size, :].astype(F32)
        coded = ref[size:, :].astype(F32)
        note = note + (coded[0:1, :1] + coded[1:2, :1] + coded[2:3, :1])
    sum_ref[...] = total.astype(sum_ref.dtype)
    note_ref[...] = note * (1.0 / width)


def assemble_kernel(me_ref, part_ref, *refs, offset, wf_rows, wb_rows, factor_f, factor_b):
    wf_hbm, wb_hbm, wf_buf, wb_buf, sems = refs[-5:]
    place = reverse_bits(me_ref[0] & 15, 4) ^ offset
    moves = []
    for e, turn in enumerate(TURNS):
        to = place ^ turn
        wf_buf[e] = part_ref[e, :wf_rows, :].astype(F32) * factor_f
        wb_buf[e] = part_ref[e, wf_rows:, :].astype(F32) * factor_b
        for k, (buf, hbm, rows) in enumerate(((wf_buf, wf_hbm, wf_rows), (wb_buf, wb_hbm, wb_rows))):
            move = pltpu.make_async_copy(
                buf.at[e], hbm.at[pl.ds(pl.multiple_of(to * rows, rows), rows), :], sems.at[2 * e + k]
            )
            move.start()
            moves.append(move)
    for move in moves:
        move.wait()


SMEM = pl.BlockSpec(memory_space=pltpu.SMEM)
VMEM = pl.BlockSpec(memory_space=pltpu.VMEM)
HBM = pl.BlockSpec(memory_space=pltpu.HBM)
ANY = pl.BlockSpec(memory_space=pl.ANY)


def body(hidden_f, hidden_t, hidden_b, w_f, w_t, w_b, latents, latent_ids, positives):
    rows, high = hidden_f.shape
    wide = hidden_b.shape[1]
    width = w_f.shape[1]
    size = lax.axis_size("fa")
    bits = size.bit_length() - 1
    beyond = [1 << k for k in range(4, bits)]
    me = lax.axis_index("fa")
    total = size * rows
    assert bits >= 4 and size == 1 << bits and high // 4 == width == wide

    me = me.astype(jnp.int32).reshape(1)
    ends = [(at + 2) * rows + PAD for at in FEAT_AT]
    far, near, cut, head, wb_copy = pl.pallas_call(
        feature_kernel,
        in_specs=[SMEM] + [HBM] * 9,
        out_specs=[VMEM] * 5,
        out_shape=[
            jax.ShapeDtypeStruct((ends[1], width), BF),
            jax.ShapeDtypeStruct((ends[2], width), BF),
            jax.ShapeDtypeStruct((rows, width), BF),
            jax.ShapeDtypeStruct(hidden_b.shape, BF),
            jax.ShapeDtypeStruct(w_b.shape, BF),
        ],
        scratch_shapes=[
            pltpu.VMEM(hidden_f.shape, BF),
            pltpu.VMEM(hidden_t.shape, BF),
            pltpu.VMEM(w_f.shape, BF),
            pltpu.VMEM(w_t.shape, BF),
            pltpu.VMEM(latents.shape, BF),
            pltpu.VMEM((1, rows), jnp.int32),
            pltpu.VMEM((1, rows), jnp.int32),
            pltpu.SemaphoreType.DMA((9,)),
        ],
        compiler_params=pltpu.CompilerParams(vmem_limit_bytes=60 * 2**20),
        cost_estimate=pl.CostEstimate(
            flops=4 * rows * high * width, bytes_accessed=4 * high * (rows + width), transcendentals=0
        ),
    )(
        me,
        hidden_f,
        hidden_t,
        hidden_b,
        w_f,
        w_t,
        w_b,
        latents,
        latent_ids.reshape(1, rows),
        positives.reshape(1, rows),
    )
    for mask in reversed(beyond):
        head = jnp.concatenate([head, swap(head, mask, size)], axis=0)
    line = [swap(head, mask, size) for mask, _ in reversed(LINE)]
    line = [head[rows:]] * (len(beyond) > 0) + line
    far2 = swap(far, 2, size)
    over = [swap(piece, 2, size) for piece in line[-2:]]
    gated = pack(*line[:-2], after=far2)
    line = [gated] + line[-2:]
    over = [swap(gated, 2, size)] + over
    near1 = swap(near, 1, size)
    far3 = swap(far2, 1, size)
    line0, line2 = [jnp.concatenate(part, axis=0) for part in (line, over)]
    line1 = swap(line0, 1, size)
    line3 = swap(line2, 1, size)

    wf_rows, wb_rows = high // 16, wide // 16
    each = wf_rows + wb_rows
    keep, *sends = pl.pallas_call(
        functools.partial(pair_kernel, rows=rows, total=total),
        in_specs=[SMEM] + [VMEM] * 10,
        out_specs=[VMEM] * 4,
        out_shape=[jax.ShapeDtypeStruct((each + PAD, width), F32)]
        + [jax.ShapeDtypeStruct((each + PAD, width), BF)] * 3,
        scratch_shapes=[
            pltpu.VMEM((total, wide), BF),
            pltpu.VMEM((total, width), F32),
            pltpu.VMEM((total, width), BF),
            pltpu.VMEM((4 * rows, min(total, 16 * rows)), BF),
            pltpu.VMEM((width, width), F32),
            pltpu.VMEM((4 * rows, wide), F32),
            pltpu.VMEM((4 * rows, wide), BF),
            pltpu.VMEM((width, width), F32),
            pltpu.VMEM((wide // 2, width), F32),
        ],
        compiler_params=pltpu.CompilerParams(vmem_limit_bytes=15 * 2**20 + total * width * 10),
    )(me, near, far2, near1, far3, line0, line2, line1, line3, cut, wb_copy)

    got = [swap(part, mask, size) for part, (mask, _) in zip(sends, LINE)]
    result, note = pl.pallas_call(
        add_kernel,
        in_specs=[VMEM] * 4,
        out_specs=[VMEM] * 2,
        out_shape=[
            jax.ShapeDtypeStruct((each, width), F32 if beyond else BF),
            jax.ShapeDtypeStruct((1, 1), F32),
        ],
        compiler_params=pltpu.CompilerParams(vmem_limit_bytes=8 * 2**20),
    )(keep, *got)
    for mask in beyond:
        result = result + swap(result, mask, size)
        note = note + swap(note, mask, size)
    result = result.astype(BF).reshape(1, each, width)
    piece12, piece8, piece4 = [swap(result, mask, size) for mask, _ in LINE]
    pairs = [jnp.concatenate(pair, axis=0) for pair in ((piece4, piece8), (piece12, result))]
    near = jnp.concatenate(pairs + [swap(pair, 2, size) for pair in pairs], axis=0)
    far = swap(near, 1, size)

    def assemble(part, offset, *begun):
        return pl.pallas_call(
            functools.partial(
                assemble_kernel,
                offset=offset,
                wf_rows=wf_rows,
                wb_rows=wb_rows,
                factor_f=math.sqrt(high),
                factor_b=math.sqrt(wide),
            ),
            in_specs=[SMEM, VMEM] + [ANY] * len(begun),
            out_specs=[ANY] * 2,
            out_shape=[
                jax.ShapeDtypeStruct((high, width), F32),
                jax.ShapeDtypeStruct((wide, width), F32),
            ],
            scratch_shapes=[
                pltpu.VMEM((8, wf_rows, width), F32),
                pltpu.VMEM((8, wb_rows, width), F32),
                pltpu.SemaphoreType.DMA((16,)),
            ],
            input_output_aliases={2 + k: k for k in range(len(begun))},
            compiler_params=pltpu.CompilerParams(vmem_limit_bytes=8 * 2**20),
        )(me, part, *begun)

    grad_wf, grad_wb = assemble(far, 8, *assemble(near, 0))
    return (grad_wf, grad_wb, note.reshape(1))


def solution(mesh):
    placed = (
        P(("grp", "fa"), None),
        P(("grp", "fa"), None),
        P(("grp", "fa"), None),
        P(),
        P(),
        P(),
        P("grp", None),
        P(("grp", "fa")),
        P(("grp", "fa")),
    )
    return jax.shard_map(
        body,
        mesh=mesh,
        in_specs=placed,
        out_specs=(P("grp", None), P("grp", None), P("grp")),
        check_vma=False,
    )
```

```python
import functools
import math

import jax
import jax.numpy as jnp
from jax import lax
from jax.experimental import pallas as pl
from jax.experimental.pallas import tpu as pltpu
from jax.sharding import PartitionSpec as P

GAMMA = 0.98
LAMBDA = 1.0
EPS = 1e-06
BF = jnp.bfloat16
F32 = jnp.float32
GROUP = (0, 2, 1, 3)
CUT_AT = (0, 0, 0, 1)
HEAD_AT = (1, 2, 1, 2)
FEAT_AT = (2, 3, 2, 3)
PAD = 16
LINE = ((12, 3), (8, 1), (4, 2))
TURNS = (2, 1, 3, 0, 6, 5, 7, 4)


def dot(left, right):
    return jnp.dot(left, right, preferred_element_type=F32)


def dot_t(left, right):
    return lax.dot_general(left, right, (((0,), (0,)), ((), ())), preferred_element_type=F32)


def halves(array):
    high = array.astype(BF)
    return high, (array - high.astype(F32)).astype(BF)


def swap(array, mask, size):
    return lax.ppermute(array, "fa", [(i, i ^ mask) for i in range(size)])


def reverse_bits(value, bits):
    out = value * 0
    for k in range(bits):
        out = out + (((value >> k) & 1) << (bits - 1 - k))
    return out


def columns_of(row, rows):
    return jnp.transpose(jnp.broadcast_to(row, (rows, rows)))


def feature_kernel(
    me_ref,
    hf_hbm,
    ht_hbm,
    hb_hbm,
    wf_hbm,
    wt_hbm,
    wb_hbm,
    lat_hbm,
    ids_hbm,
    pos_hbm,
    far_ref,
    near_ref,
    cut_ref,
    head_ref,
    wb_ref,
    hf,
    ht,
    wf,
    wt,
    lat,
    ids,
    pos,
    sems,
):
    rows = hf.shape[0]
    width = wf.shape[1]
    moves = [
        pltpu.make_async_copy(source, target, sems.at[k])
        for k, (source, target) in enumerate(
            (
                (ids_hbm, ids),
                (pos_hbm, pos),
                (lat_hbm, lat),
                (hf_hbm, hf),
                (wf_hbm, wf),
                (ht_hbm, ht),
                (wt_hbm, wt),
                (hb_hbm, head_ref),
                (wb_hbm, wb_ref),
            )
        )
    ]
    for move in moves:
        move.start()
    for move in moves[:3]:
        move.wait()
    who = columns_of(ids[...].astype(F32), rows)
    lanes = lax.broadcasted_iota(jnp.int32, (rows, rows), 1).astype(F32)
    tiles = [
        jnp.where(who == lanes + float(t * rows), 1.0, 0.0).astype(BF) for t in range(lat.shape[0] // rows)
    ]
    zrows = dot(jnp.concatenate(tiles, axis=1), lat[...])
    place = pos[...]
    line = lax.broadcasted_iota(jnp.int32, (PAD, rows), 0)
    high = jnp.broadcast_to(lax.shift_right_logical(place, 7).astype(F32), (PAD, rows))
    low = jnp.broadcast_to((place & 127).astype(F32), (PAD, rows))
    coded = jnp.where(line == 0, high, jnp.where(line == 1, low, 0.0)).astype(BF)
    coded = jnp.concatenate([coded] + [jnp.zeros((PAD, width - rows), BF)] * (width > rows), axis=1)

    def piece(slot):
        other = me_ref[0] ^ GROUP[slot]
        quarter = (other & 1) * 2 + ((other >> 1) & 1)
        return hf[:, pl.ds(pl.multiple_of(quarter * width, width), width)]

    moves[3].wait()
    cut_ref[...] = piece(0)
    far_ref[:rows, :] = piece(1)
    near_ref[:rows, :] = piece(2)
    far_ref[rows : 2 * rows, :] = piece(3)
    moves[4].wait()
    feat = (dot(hf[...], wf[...]) + zrows).astype(BF)
    moves[5].wait()
    moves[6].wait()
    feat_t = (dot(ht[...], wt[...]) + zrows).astype(BF)
    moves[7].wait()
    head = head_ref[...]
    for ref, at in ((far_ref, HEAD_AT[1]), (near_ref, HEAD_AT[2])):
        ref[at * rows : (at + 1) * rows, :] = head
        ref[(at + 1) * rows : (at + 2) * rows, :] = feat
        ref[(at + 2) * rows : (at + 3) * rows, :] = feat_t
        ref[(at + 3) * rows :, :] = coded
    moves[8].wait()


def pack_kernel(*refs):
    at = 0
    for ref in refs[:-2]:
        refs[-1][at : at + ref.shape[0], :] = ref[...]
        at = at + ref.shape[0]


def pack(*arrays, after):
    return pl.pallas_call(
        pack_kernel,
        in_specs=[VMEM] * (len(arrays) + 1),
        out_specs=VMEM,
        out_shape=jax.ShapeDtypeStruct((sum(x.shape[0] for x in arrays), arrays[0].shape[1]), BF),
        compiler_params=pltpu.CompilerParams(vmem_limit_bytes=20 * 2**20),
    )(*arrays, after)


def pair_kernel(*refs, rows, total):
    me_ref = refs[0]
    mails, lines, cut_ref, wb_ref = refs[1:5], refs[5:9], refs[9], refs[10]
    keep_ref, sends = refs[11], refs[12:15]
    hid_ref, raw_ref, back_ref, mask_ref, smat_ref, pick_ref, own_ref, wfq_ref, wbq_ref = refs[15:]
    width = wb_ref.shape[1]
    pairs = float(total * (total - 1))
    groups = total // (4 * rows)
    wb = wb_ref[...]
    end = 2 * rows + PAD
    me = me_ref[0]
    feats = [(ref, at * rows) for ref, at in zip(mails, FEAT_AT)]
    cuts = [(ref, at * rows) for ref, at in zip((cut_ref,) + mails[1:], CUT_AT)]
    length = total // 4
    for i, (mail, line) in enumerate(zip(mails, lines)):
        first, start = i * length, HEAD_AT[i] * rows
        hid_ref[first : first + rows, :] = mail[start : start + rows, :]
        if length <= 8 * rows:
            hid_ref[first + rows : first + length, :] = line[...]
        else:

            def one(k, carry, line=line, first=first + rows):
                hid_ref[pl.ds(pl.multiple_of(first + k * rows, rows), rows), :] = line[
                    pl.ds(pl.multiple_of(k * rows, rows), rows), :
                ]
                return carry

            lax.fori_loop(0, length // rows - 1, one, 0)

    def base(block):
        per = total // (16 * rows)
        way, along, within = block // (4 * per), (block // per) % 4, block % per
        other = (way >> 1) | ((way & 1) << 1) | (4 * along)
        return (me ^ (other | (reverse_bits(within, per.bit_length() - 1) << 4))) * rows

    def embed(hidden):
        raw = dot(hidden, wb)
        scale = lax.rsqrt(jnp.mean(raw * raw, axis=-1, keepdims=True) + EPS)
        return raw, scale, (raw * scale).astype(BF)

    def through(grad, raw, scale):
        along = jnp.sum(grad * raw, axis=-1, keepdims=True)
        return (scale * grad - scale * scale * scale * (1.0 / width) * along * raw).astype(BF)

    big, small = mask_ref.shape[1], 4 * rows

    def over_rows(step):
        if big == total:
            step(0)
        else:
            lax.fori_loop(0, total // big, lambda i, carry: (step(i), carry)[1], 0)

    def at(start, length):
        return pl.ds(pl.multiple_of(start, rows), length)

    wanted = []
    for ref, start in feats:
        code = ref[start + 2 * rows : start + end, :rows].astype(F32)
        wanted.append(columns_of(code[0:1] * 128.0 + code[1:2], rows))
    lanes = lax.broadcasted_iota(jnp.int32, (rows, rows), 1)
    smat_ref[...] = jnp.zeros_like(smat_ref)
    pick_ref[...] = jnp.zeros_like(pick_ref)

    def first_pass(step):
        for i in range(big // small):
            here = at(step * big + i * small, small)
            raw, _, back = embed(hid_ref[here, :])
            raw_ref[here, :] = raw
            back_ref[here, :] = back
        for t in range(big // rows):
            ids = (lanes + base(step * (big // rows) + t)).astype(F32)
            for g, want in enumerate(wanted):
                mask_ref[g * rows : (g + 1) * rows, t * rows : (t + 1) * rows] = jnp.where(
                    want == ids, 1.0, 0.0
                ).astype(BF)
        here = at(step * big, big)
        smat_ref[...] += dot_t(back_ref[here, :], back_ref[here, :])
        pick_ref[...] += dot(mask_ref[...], hid_ref[here, :])

    over_rows(first_pass)
    smat = smat_ref[...]
    s_hi, s_lo = halves(smat)
    place = reverse_bits(me & 15, 4)
    quarter, mine = place >> 2, place & 3
    half = wbq_ref.shape[0]
    columns = pl.ds(pl.multiple_of((quarter >> 1) * half, half), half)

    def rows_of(places, offset):
        return jnp.concatenate([ref[at + offset : at + offset + rows, :] for ref, at in places], axis=0)

    feat = rows_of(feats, 0)
    f32feat = feat.astype(F32)
    diff = f32feat - GAMMA * rows_of(feats, rows).astype(F32)
    d_hi, d_lo = halves(diff)
    kmat = dot_t(d_hi, feat) + dot_t(d_lo, feat)
    hidden = pick_ref[...].astype(BF)
    own_ref[...] = hidden
    raw, scale, back = embed(hidden)
    ob = back.astype(F32)
    ds = dot(d_hi, s_hi) + dot(d_lo, s_hi) + dot(d_hi, s_lo)
    db = jnp.sum(diff * ob, axis=-1, keepdims=True)
    coef = db * (1.0 / pairs) + 1.0 / total
    norm = jnp.sum(ob * ob, axis=-1, keepdims=True)
    grad_f = (ds * (1.0 / pairs) - coef * ob).astype(BF)
    wfq_ref[...] = dot_t(rows_of(cuts, 0), grad_f)
    squares = jnp.sum(diff * ds) - jnp.sum(db * db)
    squares = squares + LAMBDA * (jnp.sum(smat * smat) / groups - jnp.sum(norm * norm))
    sums = squares / (2.0 * pairs) - (jnp.sum(f32feat * ob) + LAMBDA * jnp.sum(norm)) / total
    grad_own = through(
        -coef * f32feat - (norm * (2.0 * LAMBDA / pairs) + 2.0 * LAMBDA / total) * ob, raw, scale
    )
    wbq_ref[...] = dot_t(own_ref[:, columns], grad_own)
    a_hi, a_lo = halves((kmat + (2.0 * LAMBDA / groups) * smat) * (1.0 / pairs))

    def second_pass(step):
        for i in range(big // small):
            here = at(step * big + i * small, small)
            raw = raw_ref[here, :]
            scale = lax.rsqrt(jnp.mean(raw * raw, axis=-1, keepdims=True) + EPS)
            back = back_ref[here, :]
            back_ref[here, :] = through(dot(back, a_hi) + dot(back, a_lo), raw, scale)
        here = at(step * big, big)
        wbq_ref[...] += dot_t(hid_ref[here, columns], back_ref[here, :])

    over_rows(second_pass)
    wf_rows = wfq_ref.shape[0] // 4
    wb_rows = wbq_ref.shape[0] // 8
    size = wf_rows + wb_rows

    def block(t):
        return (
            wfq_ref[pl.ds(pl.multiple_of(t * wf_rows, wf_rows), wf_rows), :],
            wbq_ref[pl.ds(pl.multiple_of(((quarter & 1) * 4 + t) * wb_rows, wb_rows), wb_rows), :],
        )

    keep_ref[:wf_rows, :], keep_ref[wf_rows:size, :] = block(mine)
    note = jnp.full((PAD, width), sums, F32)
    keep_ref[size:, :] = note
    line = lax.broadcasted_iota(jnp.int32, (PAD, width), 0)
    n_hi = note.astype(BF)
    n_mid, n_lo = halves(note - n_hi.astype(F32))
    coded = jnp.where(
        line == 0,
        n_hi.astype(F32),
        jnp.where(line == 1, n_mid.astype(F32), jnp.where(line == 2, n_lo.astype(F32), 0.0)),
    ).astype(BF)
    for ref, (_, turn) in zip(sends, LINE):
        part_f, part_b = block(mine ^ turn)
        ref[:wf_rows, :] = part_f.astype(BF)
        ref[wf_rows:size, :] = part_b.astype(BF)
        ref[size:, :] = coded


def add_kernel(keep_ref, *refs):
    sum_ref, note_ref = refs[3:]
    size, width = sum_ref.shape
    total = keep_ref[:size, :]
    note = keep_ref[size : size + 1, :1]
    for ref in refs[:3]:
        total = total + ref[:size, :].astype(F32)
        coded = ref[size:, :].astype(F32)
        note = note + (coded[0:1, :1] + coded[1:2, :1] + coded[2:3, :1])
    sum_ref[...] = total.astype(sum_ref.dtype)
    note_ref[...] = note * (1.0 / width)


def assemble_kernel(me_ref, part_ref, *refs, offset, wf_rows, wb_rows, factor_f, factor_b):
    wf_hbm, wb_hbm, wf_buf, wb_buf, sems = refs[-5:]
    place = reverse_bits(me_ref[0] & 15, 4) ^ offset
    moves = []
    kinds = ((wf_buf, wf_hbm, 0, wf_rows, factor_f), (wb_buf, wb_hbm, wf_rows, wb_rows, factor_b))
    for k, (buf, hbm, first, rows, factor) in enumerate(kinds):
        for e, turn in enumerate(TURNS):
            to = (place ^ turn) & 7
            buf[pl.ds(pl.multiple_of(to * rows, rows), rows), :] = (
                part_ref[e, first : first + rows, :].astype(F32) * factor
            )
        start = pl.multiple_of((place >> 3) * (8 * rows), 8 * rows)
        move = pltpu.make_async_copy(buf, hbm.at[pl.ds(start, 8 * rows), :], sems.at[k])
        move.start()
        moves.append(move)
    for move in moves:
        move.wait()


SMEM = pl.BlockSpec(memory_space=pltpu.SMEM)
VMEM = pl.BlockSpec(memory_space=pltpu.VMEM)
HBM = pl.BlockSpec(memory_space=pltpu.HBM)
ANY = pl.BlockSpec(memory_space=pl.ANY)


def body(hidden_f, hidden_t, hidden_b, w_f, w_t, w_b, latents, latent_ids, positives):
    rows, high = hidden_f.shape
    wide = hidden_b.shape[1]
    width = w_f.shape[1]
    size = lax.axis_size("fa")
    bits = size.bit_length() - 1
    beyond = [1 << k for k in range(4, bits)]
    me = lax.axis_index("fa")
    total = size * rows
    assert bits >= 4 and size == 1 << bits and high // 4 == width == wide

    me = me.astype(jnp.int32).reshape(1)
    ends = [(at + 2) * rows + PAD for at in FEAT_AT]
    far, near, cut, head, wb_copy = pl.pallas_call(
        feature_kernel,
        in_specs=[SMEM] + [HBM] * 9,
        out_specs=[VMEM] * 5,
        out_shape=[
            jax.ShapeDtypeStruct((ends[1], width), BF),
            jax.ShapeDtypeStruct((ends[2], width), BF),
            jax.ShapeDtypeStruct((rows, width), BF),
            jax.ShapeDtypeStruct(hidden_b.shape, BF),
            jax.ShapeDtypeStruct(w_b.shape, BF),
        ],
        scratch_shapes=[
            pltpu.VMEM(hidden_f.shape, BF),
            pltpu.VMEM(hidden_t.shape, BF),
            pltpu.VMEM(w_f.shape, BF),
            pltpu.VMEM(w_t.shape, BF),
            pltpu.VMEM(latents.shape, BF),
            pltpu.VMEM((1, rows), jnp.int32),
            pltpu.VMEM((1, rows), jnp.int32),
            pltpu.SemaphoreType.DMA((9,)),
        ],
        compiler_params=pltpu.CompilerParams(vmem_limit_bytes=60 * 2**20),
        cost_estimate=pl.CostEstimate(
            flops=4 * rows * high * width, bytes_accessed=4 * high * (rows + width), transcendentals=0
        ),
    )(
        me,
        hidden_f,
        hidden_t,
        hidden_b,
        w_f,
        w_t,
        w_b,
        latents,
        latent_ids.reshape(1, rows),
        positives.reshape(1, rows),
    )
    for mask in reversed(beyond):
        head = jnp.concatenate([head, swap(head, mask, size)], axis=0)
    line = [swap(head, mask, size) for mask, _ in reversed(LINE)]
    line = [head[rows:]] * (len(beyond) > 0) + line
    far2 = swap(far, 2, size)
    over = [swap(piece, 2, size) for piece in line[-2:]]
    gated = pack(*line[:-2], after=far2)
    line = [gated] + line[-2:]
    over = [swap(gated, 2, size)] + over
    near1 = swap(near, 1, size)
    far3 = swap(far2, 1, size)
    line0, line2 = [jnp.concatenate(part, axis=0) for part in (line, over)]
    line1 = swap(line0, 1, size)
    line3 = swap(line2, 1, size)

    wf_rows, wb_rows = high // 16, wide // 16
    each = wf_rows + wb_rows
    keep, *sends = pl.pallas_call(
        functools.partial(pair_kernel, rows=rows, total=total),
        in_specs=[SMEM] + [VMEM] * 10,
        out_specs=[VMEM] * 4,
        out_shape=[jax.ShapeDtypeStruct((each + PAD, width), F32)]
        + [jax.ShapeDtypeStruct((each + PAD, width), BF)] * 3,
        scratch_shapes=[
            pltpu.VMEM((total, wide), BF),
            pltpu.VMEM((total, width), F32),
            pltpu.VMEM((total, width), BF),
            pltpu.VMEM((4 * rows, min(total, 16 * rows)), BF),
            pltpu.VMEM((width, width), F32),
            pltpu.VMEM((4 * rows, wide), F32),
            pltpu.VMEM((4 * rows, wide), BF),
            pltpu.VMEM((width, width), F32),
            pltpu.VMEM((wide // 2, width), F32),
        ],
        compiler_params=pltpu.CompilerParams(vmem_limit_bytes=15 * 2**20 + total * width * 10),
    )(me, near, far2, near1, far3, line0, line2, line1, line3, cut, wb_copy)

    got = [swap(part, mask, size) for part, (mask, _) in zip(sends, LINE)]
    result, note = pl.pallas_call(
        add_kernel,
        in_specs=[VMEM] * 4,
        out_specs=[VMEM] * 2,
        out_shape=[
            jax.ShapeDtypeStruct((each, width), F32 if beyond else BF),
            jax.ShapeDtypeStruct((1, 1), F32),
        ],
        compiler_params=pltpu.CompilerParams(vmem_limit_bytes=8 * 2**20),
    )(keep, *got)
    for mask in beyond:
        result = result + swap(result, mask, size)
        note = note + swap(note, mask, size)
    result = result.astype(BF).reshape(1, each, width)
    piece12, piece8, piece4 = [swap(result, mask, size) for mask, _ in LINE]
    pairs = [jnp.concatenate(pair, axis=0) for pair in ((piece4, piece8), (piece12, result))]
    near = jnp.concatenate(pairs + [swap(pair, 2, size) for pair in pairs], axis=0)
    far = swap(near, 1, size)

    def assemble(part, offset, *begun):
        return pl.pallas_call(
            functools.partial(
                assemble_kernel,
                offset=offset,
                wf_rows=wf_rows,
                wb_rows=wb_rows,
                factor_f=math.sqrt(high),
                factor_b=math.sqrt(wide),
            ),
            in_specs=[SMEM, VMEM] + [ANY] * len(begun),
            out_specs=[ANY] * 2,
            out_shape=[
                jax.ShapeDtypeStruct((high, width), F32),
                jax.ShapeDtypeStruct((wide, width), F32),
            ],
            scratch_shapes=[
                pltpu.VMEM((8 * wf_rows, width), F32),
                pltpu.VMEM((8 * wb_rows, width), F32),
                pltpu.SemaphoreType.DMA((2,)),
            ],
            input_output_aliases={2 + k: k for k in range(len(begun))},
            compiler_params=pltpu.CompilerParams(vmem_limit_bytes=8 * 2**20),
        )(me, part, *begun)

    grad_wf, grad_wb = assemble(far, 8, *assemble(near, 0))
    return (grad_wf, grad_wb, note.reshape(1))


def solution(mesh):
    placed = (
        P(("grp", "fa"), None),
        P(("grp", "fa"), None),
        P(("grp", "fa"), None),
        P(),
        P(),
        P(),
        P("grp", None),
        P(("grp", "fa")),
        P(("grp", "fa")),
    )
    return jax.shard_map(
        body,
        mesh=mesh,
        in_specs=placed,
        out_specs=(P("grp", None), P("grp", None), P("grp")),
        check_vma=False,
    )
```

```python
import functools
import math

import jax
import jax.numpy as jnp
from jax import lax
from jax.experimental import pallas as pl
from jax.experimental.pallas import tpu as pltpu
from jax.sharding import PartitionSpec as P

GAMMA = 0.98
LAMBDA = 1.0
EPS = 1e-06
BF = jnp.bfloat16
F32 = jnp.float32
GROUP = (0, 2, 1, 3)
CUT_AT = (0, 0, 0, 1)
HEAD_AT = (1, 2, 1, 2)
FEAT_AT = (2, 3, 2, 3)
PAD = 16
LINE = ((12, 3), (8, 1), (4, 2))
TURNS = (2, 1, 3, 0, 6, 5, 7, 4)


def dot(left, right):
    return jnp.dot(left, right, preferred_element_type=F32)


def dot_t(left, right):
    return lax.dot_general(left, right, (((0,), (0,)), ((), ())), preferred_element_type=F32)


def halves(array):
    high = array.astype(BF)
    return high, (array - high.astype(F32)).astype(BF)


def swap(array, mask, size):
    return lax.ppermute(array, "fa", [(i, i ^ mask) for i in range(size)])


def reverse_bits(value, bits):
    out = value * 0
    for k in range(bits):
        out = out + (((value >> k) & 1) << (bits - 1 - k))
    return out


def columns_of(row, rows):
    return jnp.transpose(jnp.broadcast_to(row, (rows, rows)))


def feature_kernel(
    me_ref,
    hf_hbm,
    ht_hbm,
    hb_hbm,
    wf_hbm,
    wt_hbm,
    wb_hbm,
    lat_hbm,
    ids_hbm,
    pos_hbm,
    far_ref,
    near_ref,
    cut_ref,
    head_ref,
    wb_ref,
    hf,
    ht,
    wf,
    wt,
    lat,
    ids,
    pos,
    sems,
):
    rows = hf.shape[0]
    width = wf.shape[1]
    moves = [
        pltpu.make_async_copy(source, target, sems.at[k])
        for k, (source, target) in enumerate(
            (
                (hf_hbm, hf),
                (wf_hbm, wf),
                (ht_hbm, ht),
                (wt_hbm, wt),
                (lat_hbm, lat),
                (ids_hbm, ids),
                (pos_hbm, pos),
                (hb_hbm, head_ref),
                (wb_hbm, wb_ref),
            )
        )
    ]
    for move in moves:
        move.start()
    def piece(slot):
        other = me_ref[0] ^ GROUP[slot]
        quarter = (other & 1) * 2 + ((other >> 1) & 1)
        return hf[:, pl.ds(pl.multiple_of(quarter * width, width), width)]

    moves[0].wait()
    cut_ref[...] = piece(0)
    far_ref[:rows, :] = piece(1)
    near_ref[:rows, :] = piece(2)
    far_ref[rows : 2 * rows, :] = piece(3)
    moves[1].wait()
    feat = dot(hf[...], wf[...])
    moves[2].wait()
    moves[3].wait()
    feat_t = dot(ht[...], wt[...])
    for move in moves[4:7]:
        move.wait()
    who = columns_of(ids[...].astype(F32), rows)
    lanes = lax.broadcasted_iota(jnp.int32, (rows, rows), 1).astype(F32)
    tiles = [
        jnp.where(who == lanes + float(t * rows), 1.0, 0.0).astype(BF) for t in range(lat.shape[0] // rows)
    ]
    zrows = dot(jnp.concatenate(tiles, axis=1), lat[...])
    place = pos[...]
    line = lax.broadcasted_iota(jnp.int32, (PAD, rows), 0)
    high = jnp.broadcast_to(lax.shift_right_logical(place, 7).astype(F32), (PAD, rows))
    low = jnp.broadcast_to((place & 127).astype(F32), (PAD, rows))
    coded = jnp.where(line == 0, high, jnp.where(line == 1, low, 0.0)).astype(BF)
    coded = jnp.concatenate([coded] + [jnp.zeros((PAD, width - rows), BF)] * (width > rows), axis=1)

    feat = (feat + zrows).astype(BF)
    feat_t = (feat_t + zrows).astype(BF)
    moves[7].wait()
    head = head_ref[...]
    for ref, at in ((far_ref, HEAD_AT[1]), (near_ref, HEAD_AT[2])):
        ref[at * rows : (at + 1) * rows, :] = head
        ref[(at + 1) * rows : (at + 2) * rows, :] = feat
        ref[(at + 2) * rows : (at + 3) * rows, :] = feat_t
        ref[(at + 3) * rows :, :] = coded
    moves[8].wait()


def pack_kernel(*refs):
    at = 0
    for ref in refs[:-2]:
        refs[-1][at : at + ref.shape[0], :] = ref[...]
        at = at + ref.shape[0]


def pack(*arrays, after):
    return pl.pallas_call(
        pack_kernel,
        in_specs=[VMEM] * (len(arrays) + 1),
        out_specs=VMEM,
        out_shape=jax.ShapeDtypeStruct((sum(x.shape[0] for x in arrays), arrays[0].shape[1]), BF),
        compiler_params=pltpu.CompilerParams(vmem_limit_bytes=20 * 2**20),
    )(*arrays, after)


def pair_kernel(*refs, rows, total):
    me_ref = refs[0]
    mails, lines, cut_ref, wb_ref = refs[1:5], refs[5:9], refs[9], refs[10]
    keep_ref, sends = refs[11], refs[12:15]
    hid_ref, raw_ref, back_ref, mask_ref, smat_ref, pick_ref, own_ref, wfq_ref, wbq_ref = refs[15:]
    width = wb_ref.shape[1]
    pairs = float(total * (total - 1))
    groups = total // (4 * rows)
    wb = wb_ref[...]
    end = 2 * rows + PAD
    me = me_ref[0]
    feats = [(ref, at * rows) for ref, at in zip(mails, FEAT_AT)]
    cuts = [(ref, at * rows) for ref, at in zip((cut_ref,) + mails[1:], CUT_AT)]
    length = total // 4
    for i, (mail, line) in enumerate(zip(mails, lines)):
        first, start = i * length, HEAD_AT[i] * rows
        hid_ref[first : first + rows, :] = mail[start : start + rows, :]
        if length <= 8 * rows:
            hid_ref[first + rows : first + length, :] = line[...]
        else:

            def one(k, carry, line=line, first=first + rows):
                hid_ref[pl.ds(pl.multiple_of(first + k * rows, rows), rows), :] = line[
                    pl.ds(pl.multiple_of(k * rows, rows), rows), :
                ]
                return carry

            lax.fori_loop(0, length // rows - 1, one, 0)

    def base(block):
        per = total // (16 * rows)
        way, along, within = block // (4 * per), (block // per) % 4, block % per
        other = (way >> 1) | ((way & 1) << 1) | (4 * along)
        return (me ^ (other | (reverse_bits(within, per.bit_length() - 1) << 4))) * rows

    def embed(hidden):
        raw = dot(hidden, wb)
        scale = lax.rsqrt(jnp.mean(raw * raw, axis=-1, keepdims=True) + EPS)
        return raw, scale, (raw * scale).astype(BF)

    def through(grad, raw, scale):
        along = jnp.sum(grad * raw, axis=-1, keepdims=True)
        return (scale * grad - scale * scale * scale * (1.0 / width) * along * raw).astype(BF)

    big, small = mask_ref.shape[1], 4 * rows

    def over_rows(step):
        if big == total:
            step(0)
        else:
            lax.fori_loop(0, total // big, lambda i, carry: (step(i), carry)[1], 0)

    def at(start, length):
        return pl.ds(pl.multiple_of(start, rows), length)

    wanted = []
    for ref, start in feats:
        code = ref[start + 2 * rows : start + end, :rows].astype(F32)
        wanted.append(columns_of(code[0:1] * 128.0 + code[1:2], rows))
    lanes = lax.broadcasted_iota(jnp.int32, (rows, rows), 1)
    smat_ref[...] = jnp.zeros_like(smat_ref)
    pick_ref[...] = jnp.zeros_like(pick_ref)

    def first_pass(step):
        for i in range(big // small):
            here = at(step * big + i * small, small)
            raw, _, back = embed(hid_ref[here, :])
            raw_ref[here, :] = raw
            back_ref[here, :] = back
        for t in range(big // rows):
            ids = (lanes + base(step * (big // rows) + t)).astype(F32)
            for g, want in enumerate(wanted):
                mask_ref[g * rows : (g + 1) * rows, t * rows : (t + 1) * rows] = jnp.where(
                    want == ids, 1.0, 0.0
                ).astype(BF)
        here = at(step * big, big)
        smat_ref[...] += dot_t(back_ref[here, :], back_ref[here, :])
        pick_ref[...] += dot(mask_ref[...], hid_ref[here, :])

    over_rows(first_pass)
    smat = smat_ref[...]
    s_hi, s_lo = halves(smat)
    place = reverse_bits(me & 15, 4)
    quarter, mine = place >> 2, place & 3
    half = wbq_ref.shape[0]
    columns = pl.ds(pl.multiple_of((quarter >> 1) * half, half), half)

    def rows_of(places, offset):
        return jnp.concatenate([ref[at + offset : at + offset + rows, :] for ref, at in places], axis=0)

    feat = rows_of(feats, 0)
    f32feat = feat.astype(F32)
    diff = f32feat - GAMMA * rows_of(feats, rows).astype(F32)
    d_hi, d_lo = halves(diff)
    kmat = dot_t(d_hi, feat) + dot_t(d_lo, feat)
    hidden = pick_ref[...].astype(BF)
    own_ref[...] = hidden
    raw, scale, back = embed(hidden)
    ob = back.astype(F32)
    ds = dot(d_hi, s_hi) + dot(d_lo, s_hi) + dot(d_hi, s_lo)
    db = jnp.sum(diff * ob, axis=-1, keepdims=True)
    coef = db * (1.0 / pairs) + 1.0 / total
    norm = jnp.sum(ob * ob, axis=-1, keepdims=True)
    grad_f = (ds * (1.0 / pairs) - coef * ob).astype(BF)
    wfq_ref[...] = dot_t(rows_of(cuts, 0), grad_f)
    squares = jnp.sum(diff * ds) - jnp.sum(db * db)
    squares = squares + LAMBDA * (jnp.sum(smat * smat) / groups - jnp.sum(norm * norm))
    sums = squares / (2.0 * pairs) - (jnp.sum(f32feat * ob) + LAMBDA * jnp.sum(norm)) / total
    grad_own = through(
        -coef * f32feat - (norm * (2.0 * LAMBDA / pairs) + 2.0 * LAMBDA / total) * ob, raw, scale
    )
    wbq_ref[...] = dot_t(own_ref[:, columns], grad_own)
    a_hi, a_lo = halves((kmat + (2.0 * LAMBDA / groups) * smat) * (1.0 / pairs))

    def second_pass(step):
        for i in range(big // small):
            here = at(step * big + i * small, small)
            raw = raw_ref[here, :]
            scale = lax.rsqrt(jnp.mean(raw * raw, axis=-1, keepdims=True) + EPS)
            back = back_ref[here, :]
            back_ref[here, :] = through(dot(back, a_hi) + dot(back, a_lo), raw, scale)
        here = at(step * big, big)
        wbq_ref[...] += dot_t(hid_ref[here, columns], back_ref[here, :])

    over_rows(second_pass)
    wf_rows = wfq_ref.shape[0] // 4
    wb_rows = wbq_ref.shape[0] // 8
    size = wf_rows + wb_rows

    def block(t):
        return (
            wfq_ref[pl.ds(pl.multiple_of(t * wf_rows, wf_rows), wf_rows), :],
            wbq_ref[pl.ds(pl.multiple_of(((quarter & 1) * 4 + t) * wb_rows, wb_rows), wb_rows), :],
        )

    keep_ref[:wf_rows, :], keep_ref[wf_rows:size, :] = block(mine)
    note = jnp.full((PAD, width), sums, F32)
    keep_ref[size:, :] = note
    line = lax.broadcasted_iota(jnp.int32, (PAD, width), 0)
    n_hi = note.astype(BF)
    n_mid, n_lo = halves(note - n_hi.astype(F32))
    coded = jnp.where(
        line == 0,
        n_hi.astype(F32),
        jnp.where(line == 1, n_mid.astype(F32), jnp.where(line == 2, n_lo.astype(F32), 0.0)),
    ).astype(BF)
    for ref, (_, turn) in zip(sends, LINE):
        part_f, part_b = block(mine ^ turn)
        ref[:wf_rows, :] = part_f.astype(BF)
        ref[wf_rows:size, :] = part_b.astype(BF)
        ref[size:, :] = coded


def add_kernel(keep_ref, *refs):
    sum_ref, note_ref = refs[3:]
    size, width = sum_ref.shape
    total = keep_ref[:size, :]
    note = keep_ref[size : size + 1, :1]
    for ref in refs[:3]:
        total = total + ref[:size, :].astype(F32)
        coded = ref[size:, :].astype(F32)
        note = note + (coded[0:1, :1] + coded[1:2, :1] + coded[2:3, :1])
    sum_ref[...] = total.astype(sum_ref.dtype)
    note_ref[...] = note * (1.0 / width)


def assemble_kernel(me_ref, part_ref, *refs, offset, wf_rows, wb_rows, factor_f, factor_b):
    wf_hbm, wb_hbm, wf_buf, wb_buf, sems = refs[-5:]
    place = reverse_bits(me_ref[0] & 15, 4) ^ offset
    moves = []
    kinds = ((wf_buf, wf_hbm, 0, wf_rows, factor_f), (wb_buf, wb_hbm, wf_rows, wb_rows, factor_b))
    for k, (buf, hbm, first, rows, factor) in enumerate(kinds):
        for e, turn in enumerate(TURNS):
            to = (place ^ turn) & 7
            buf[pl.ds(pl.multiple_of(to * rows, rows), rows), :] = (
                part_ref[e, first : first + rows, :].astype(F32) * factor
            )
        start = pl.multiple_of((place >> 3) * (8 * rows), 8 * rows)
        move = pltpu.make_async_copy(buf, hbm.at[pl.ds(start, 8 * rows), :], sems.at[k])
        move.start()
        moves.append(move)
    for move in moves:
        move.wait()


SMEM = pl.BlockSpec(memory_space=pltpu.SMEM)
VMEM = pl.BlockSpec(memory_space=pltpu.VMEM)
HBM = pl.BlockSpec(memory_space=pltpu.HBM)
ANY = pl.BlockSpec(memory_space=pl.ANY)


def body(hidden_f, hidden_t, hidden_b, w_f, w_t, w_b, latents, latent_ids, positives):
    rows, high = hidden_f.shape
    wide = hidden_b.shape[1]
    width = w_f.shape[1]
    size = lax.axis_size("fa")
    bits = size.bit_length() - 1
    beyond = [1 << k for k in range(4, bits)]
    me = lax.axis_index("fa")
    total = size * rows
    assert bits >= 4 and size == 1 << bits and high // 4 == width == wide

    me = me.astype(jnp.int32).reshape(1)
    ends = [(at + 2) * rows + PAD for at in FEAT_AT]
    far, near, cut, head, wb_copy = pl.pallas_call(
        feature_kernel,
        in_specs=[SMEM] + [HBM] * 9,
        out_specs=[VMEM] * 5,
        out_shape=[
            jax.ShapeDtypeStruct((ends[1], width), BF),
            jax.ShapeDtypeStruct((ends[2], width), BF),
            jax.ShapeDtypeStruct((rows, width), BF),
            jax.ShapeDtypeStruct(hidden_b.shape, BF),
            jax.ShapeDtypeStruct(w_b.shape, BF),
        ],
        scratch_shapes=[
            pltpu.VMEM(hidden_f.shape, BF),
            pltpu.VMEM(hidden_t.shape, BF),
            pltpu.VMEM(w_f.shape, BF),
            pltpu.VMEM(w_t.shape, BF),
            pltpu.VMEM(latents.shape, BF),
            pltpu.VMEM((1, rows), jnp.int32),
            pltpu.VMEM((1, rows), jnp.int32),
            pltpu.SemaphoreType.DMA((9,)),
        ],
        compiler_params=pltpu.CompilerParams(vmem_limit_bytes=60 * 2**20),
        cost_estimate=pl.CostEstimate(
            flops=4 * rows * high * width, bytes_accessed=4 * high * (rows + width), transcendentals=0
        ),
    )(
        me,
        hidden_f,
        hidden_t,
        hidden_b,
        w_f,
        w_t,
        w_b,
        latents,
        latent_ids.reshape(1, rows),
        positives.reshape(1, rows),
    )
    for mask in reversed(beyond):
        head = jnp.concatenate([head, swap(head, mask, size)], axis=0)
    line = [swap(head, mask, size) for mask, _ in reversed(LINE)]
    line = [head[rows:]] * (len(beyond) > 0) + line
    far2 = swap(far, 2, size)
    over = [swap(piece, 2, size) for piece in line[-2:]]
    gated = pack(*line[:-2], after=far2)
    line = [gated] + line[-2:]
    over = [swap(gated, 2, size)] + over
    near1 = swap(near, 1, size)
    far3 = swap(far2, 1, size)
    line0, line2 = [jnp.concatenate(part, axis=0) for part in (line, over)]
    line1 = swap(line0, 1, size)
    line3 = swap(line2, 1, size)

    wf_rows, wb_rows = high // 16, wide // 16
    each = wf_rows + wb_rows
    keep, *sends = pl.pallas_call(
        functools.partial(pair_kernel, rows=rows, total=total),
        in_specs=[SMEM] + [VMEM] * 10,
        out_specs=[VMEM] * 4,
        out_shape=[jax.ShapeDtypeStruct((each + PAD, width), F32)]
        + [jax.ShapeDtypeStruct((each + PAD, width), BF)] * 3,
        scratch_shapes=[
            pltpu.VMEM((total, wide), BF),
            pltpu.VMEM((total, width), F32),
            pltpu.VMEM((total, width), BF),
            pltpu.VMEM((4 * rows, min(total, 16 * rows)), BF),
            pltpu.VMEM((width, width), F32),
            pltpu.VMEM((4 * rows, wide), F32),
            pltpu.VMEM((4 * rows, wide), BF),
            pltpu.VMEM((width, width), F32),
            pltpu.VMEM((wide // 2, width), F32),
        ],
        compiler_params=pltpu.CompilerParams(vmem_limit_bytes=15 * 2**20 + total * width * 10),
    )(me, near, far2, near1, far3, line0, line2, line1, line3, cut, wb_copy)

    got = [swap(part, mask, size) for part, (mask, _) in zip(sends, LINE)]
    result, note = pl.pallas_call(
        add_kernel,
        in_specs=[VMEM] * 4,
        out_specs=[VMEM] * 2,
        out_shape=[
            jax.ShapeDtypeStruct((each, width), F32 if beyond else BF),
            jax.ShapeDtypeStruct((1, 1), F32),
        ],
        compiler_params=pltpu.CompilerParams(vmem_limit_bytes=8 * 2**20),
    )(keep, *got)
    for mask in beyond:
        result = result + swap(result, mask, size)
        note = note + swap(note, mask, size)
    result = result.astype(BF).reshape(1, each, width)
    piece12, piece8, piece4 = [swap(result, mask, size) for mask, _ in LINE]
    pairs = [jnp.concatenate(pair, axis=0) for pair in ((piece4, piece8), (piece12, result))]
    near = jnp.concatenate(pairs + [swap(pair, 2, size) for pair in pairs], axis=0)
    far = swap(near, 1, size)

    def assemble(part, offset, *begun):
        return pl.pallas_call(
            functools.partial(
                assemble_kernel,
                offset=offset,
                wf_rows=wf_rows,
                wb_rows=wb_rows,
                factor_f=math.sqrt(high),
                factor_b=math.sqrt(wide),
            ),
            in_specs=[SMEM, VMEM] + [ANY] * len(begun),
            out_specs=[ANY] * 2,
            out_shape=[
                jax.ShapeDtypeStruct((high, width), F32),
                jax.ShapeDtypeStruct((wide, width), F32),
            ],
            scratch_shapes=[
                pltpu.VMEM((8 * wf_rows, width), F32),
                pltpu.VMEM((8 * wb_rows, width), F32),
                pltpu.SemaphoreType.DMA((2,)),
            ],
            input_output_aliases={2 + k: k for k in range(len(begun))},
            compiler_params=pltpu.CompilerParams(vmem_limit_bytes=8 * 2**20),
        )(me, part, *begun)

    grad_wf, grad_wb = assemble(far, 8, *assemble(near, 0))
    return (grad_wf, grad_wb, note.reshape(1))


def solution(mesh):
    placed = (
        P(("grp", "fa"), None),
        P(("grp", "fa"), None),
        P(("grp", "fa"), None),
        P(),
        P(),
        P(),
        P("grp", None),
        P(("grp", "fa")),
        P(("grp", "fa")),
    )
    return jax.shard_map(
        body,
        mesh=mesh,
        in_specs=placed,
        out_specs=(P("grp", None), P("grp", None), P("grp")),
        check_vma=False,
    )
```
